32 devices in a mesh: blk: 16 (over z, y, core), dp: 2 (over x).
Axes of the slice: x: 2, y: 2, z: 4, core: 2. Of those that a mesh axis runs over, the one named last changes fastest.
Arguments:
- tokens: bfloat16 [16, 768, 576], P('blk', 'dp'), may hold values from -6 to 6
- cotangent: bfloat16 [16, 768, 576], P('blk', 'dp'), may hold values from -0.59765625 to 0.59765625
- w_gate: bfloat16 [16, 576, 1536], P('blk'), may hold values from -0.25 to 0.25
- w_up: bfloat16 [16, 576, 1536], P('blk'), may hold values from -0.25 to 0.25
- w_down: bfloat16 [16, 1536, 576], P('blk'), may hold values from -0.15625 to 0.15625
Outputs:
- d_tokens: bfloat16 [16, 768, 576], P('blk', 'dp')
- grad_gate: bfloat16 [16, 576, 1536], P('blk')
- grad_up: bfloat16 [16, 576, 1536], P('blk')
- grad_down: bfloat16 [16, 1536, 576], P('blk')
The draws below stay inside these ranges and needn't reach their ends.
All inputs are finite; a program needn't handle non-finite values.
Results may differ from the reference program's by a relative error of at most 0.027.
Values may be sent and summed in bfloat16 or wider, within the bound.
No kernel may reach another device: no remote copies, remote signals or barrier semaphores. Data moves between devices by JAX's collectives and lax.ppermute only.
A program may use at most 64 MiB of HBM per device.

```python
import jax
import jax.numpy as jnp
from jax import lax

D = 576
HB = 1536
TOK = 384
ROWS = 768
N_BLK = 16
N_DP = 2


def block_scale(stream_key, dims, pieces, least, top_value):
    def one(axis_at, blocks):
        draws = jax.random.uniform(jax.random.fold_in(jax.random.fold_in(stream_key, 6), axis_at), (blocks,), jnp.float32, least / len(pieces), top_value / len(pieces))
        return jnp.repeat(jnp.exp(draws), dims[axis_at] // blocks).reshape((-1,) + (1,) * (len(dims) - axis_at - 1))

    level = one(*pieces[0])
    for cut in pieces[1:]:
        level = level * one(*cut)
    return level


def bell_draw(stream_key, extent, spread, limit, shards=(), kind=jnp.bfloat16):
    loudness = block_scale(stream_key, extent, shards, -0.22, 0.18) if shards else 1.0
    array = jax.random.normal(stream_key, extent, jnp.float32) * spread * loudness
    return jnp.minimum(jnp.maximum(array, -limit), limit).astype(kind)


def setup_inputs(seed: int = 0) -> dict:
    seeds = jax.random.split(jax.random.key(seed), 6)
    return {
        "tokens": bell_draw(seeds[0], (N_BLK, ROWS, D), 1.0, 6.0, ((0, 16), (1, 2))),
        "cotangent": bell_draw(seeds[1], (N_BLK, ROWS, D), 0.1, 0.59765625, ((0, 16), (1, 2))),
        "w_gate": bell_draw(seeds[2], (N_BLK, D, HB), D ** -0.5, 0.25, ((0, 16),)),
        "w_up": bell_draw(seeds[3], (N_BLK, D, HB), D ** -0.5, 0.25, ((0, 16),)),
        "w_down": bell_draw(seeds[4], (N_BLK, HB, D), HB ** -0.5, 0.15625, ((0, 16),)),
    }


def sublayer_fwd(vector, w_first, w_second, w_lower):
    vf = vector.astype(jnp.float32)
    inverse = lax.rsqrt(lax.optimization_barrier(jnp.mean(vf * vf, axis=-1, keepdims=True)) + 1e-05)
    normed = vf * inverse
    zed = normed.astype(jnp.bfloat16)
    pre_g = jnp.dot(zed, w_first, preferred_element_type=jnp.float32)
    pre_u = jnp.dot(zed, w_second, preferred_element_type=jnp.float32)
    active = (jax.nn.silu(pre_g) * pre_u).astype(jnp.bfloat16)
    output = (vf + jnp.dot(active, w_lower, preferred_element_type=jnp.float32)).astype(jnp.bfloat16)
    return (output, (inverse, normed, zed, pre_g, pre_u, active))

def sublayer_bwd(incoming, saved, w_first, w_second, w_lower):
    inverse, normed, zed, pre_g, pre_u, active = saved
    d_lower = jnp.dot(active.T, incoming, preferred_element_type=jnp.float32)
    d_active = jnp.dot(incoming, w_lower.T, preferred_element_type=jnp.float32)
    sigma = jax.nn.sigmoid(pre_g)
    d_gate = (d_active * pre_u * sigma * (1.0 + pre_g * (1.0 - sigma))).astype(jnp.bfloat16)
    d_upper = (d_active * pre_g * sigma).astype(jnp.bfloat16)
    g_first = jnp.dot(zed.T, d_gate, preferred_element_type=jnp.float32)
    g_second = jnp.dot(zed.T, d_upper, preferred_element_type=jnp.float32)
    d_zed = jnp.dot(d_gate, w_first.T, preferred_element_type=jnp.float32) + jnp.dot(d_upper, w_second.T, preferred_element_type=jnp.float32)
    inner = lax.optimization_barrier(jnp.mean(d_zed * normed, axis=-1, keepdims=True))
    d_vector = (incoming.astype(jnp.float32) + inverse * (d_zed - normed * inner)).astype(jnp.bfloat16)
    return (d_vector, (g_first.astype(jnp.bfloat16), g_second.astype(jnp.bfloat16), d_lower.astype(jnp.bfloat16)))

def worker(inputs, grads_in, own, prev):
    middle, saved_a = sublayer_fwd(inputs, own[0], own[1], own[2])
    final, saved_b = sublayer_fwd(middle, prev[0], prev[1], prev[2])
    d_middle, terms_b = sublayer_bwd(grads_in, saved_b, prev[0], prev[1], prev[2])
    d_inputs, terms_a = sublayer_bwd(d_middle, saved_a, own[0], own[1], own[2])
    return (d_inputs, terms_a, terms_b)

def position(items):
    xs, gs, own, prev = items
    xs = xs.reshape(N_DP, TOK, D)
    gs = gs.reshape(N_DP, TOK, D)
    d_inputs, terms_a, terms_b = jax.vmap(worker, in_axes=(0, 0, None, None))(xs, gs, own, prev)
    return (d_inputs.reshape(N_DP * TOK, D), terms_a, terms_b)

def combine(terms_a, terms_b):
    result = []
    for first, second in zip(terms_a, terms_b):
        partial_sum = (first.astype(jnp.float32) + second.astype(jnp.float32)).astype(jnp.bfloat16)
        result.append(lax.optimization_barrier(jnp.sum(partial_sum.astype(jnp.float32), axis=0)).astype(jnp.bfloat16))
    return tuple(result)

def reference(tokens, cotangent, w_gate, w_up, w_down):
    own = (w_gate, w_up, w_down)
    prev = (jnp.roll(w_gate, 1, axis=0), jnp.roll(w_up, 1, axis=0), jnp.roll(w_down, 1, axis=0))
    d_tokens, terms_a, terms_b = lax.map(position, (tokens, cotangent, own, prev))

    def block_grads(index):
        later = ((index + 1) % N_BLK).astype(jnp.int32)
        mine = tuple((lax.dynamic_index_in_dim(t, index, 0, keepdims=False) for t in terms_a))
        other = tuple((lax.dynamic_index_in_dim(t, later, 0, keepdims=False) for t in terms_b))
        return combine(mine, other)
    grads = lax.map(block_grads, jnp.arange(N_BLK, dtype=jnp.int32))
    return (d_tokens, grads[0], grads[1], grads[2])
```

```python
import jax
import jax.numpy as jnp
from jax import lax
from jax.sharding import PartitionSpec as P

F32 = jnp.float32
BF16 = jnp.bfloat16


def shift(x, by, flip=False):
    blk, dp = lax.axis_size("blk"), lax.axis_size("dp")
    pairs = []
    for i in range(blk):
        for r in range(dp):
            to = (dp - 1 - r) if flip else r
            pairs.append((i * dp + r, ((i + by) % blk) * dp + to))
    return lax.ppermute(x, ("blk", "dp"), pairs)


def dot(a, b, dims=((1,), (0,))):
    return lax.dot_general(a, b, (dims, ((), ())), preferred_element_type=F32)


def normalize(v):
    vf = v.astype(F32)
    inverse = lax.rsqrt(jnp.mean(vf * vf, axis=-1, keepdims=True) + 1e-05)
    return inverse, vf * inverse


def gates(zed, gate, up):
    pre_g = dot(zed, gate)
    pre_u = dot(zed, up)
    s = jax.nn.sigmoid(pre_g)
    q = pre_g * s
    p = pre_u * s * (1.0 + pre_g * (1.0 - s))
    return (q * pre_u).astype(BF16), p, q


def forward(v, gate, up, down):
    inverse, normed = normalize(v)
    zed = normed.astype(BF16)
    active, p, q = gates(zed, gate, up)
    out = (v.astype(F32) + dot(active, down)).astype(BF16)
    return out, (inverse, normed, zed, active, p, q)


def backward_hidden(c, saved, down):
    da = dot(c, down, ((1,), (1,)))
    return (da * saved[4]).astype(BF16), (da * saved[5]).astype(BF16)


def backward_input(c, saved, dgate, dup, gate, up):
    inverse, normed = saved[0], saved[1]
    dz = dot(dgate, gate, ((1,), (1,))) + dot(dup, up, ((1,), (1,)))
    inner = jnp.mean(dz * normed, axis=-1, keepdims=True)
    return (c.astype(F32) + inverse * (dz - normed * inner)).astype(BF16)


def second(v, c, gate, up, down):
    inverse, normed = normalize(v)
    zed = normed.astype(BF16)
    active, p, q = gates(zed, gate, up)
    saved = (inverse, normed, zed, active, p, q)
    dgate, dup = backward_hidden(c, saved, down)
    dv = backward_input(c, saved, dgate, dup, gate, up)
    return dv, (zed, active, dgate, dup, c)


def grads(terms):
    zed, active, dgate, dup, c = (jnp.concatenate(t, axis=0) for t in zip(*terms))
    tn = ((0,), (0,))
    return dot(zed, dgate, tn).astype(BF16), dot(zed, dup, tn).astype(BF16), dot(active, c, tn).astype(BF16)


def local_pair(tokens, cotangent, w_gate, w_up, w_down):
    x, g = tokens[0], cotangent[0]
    w = (w_gate[0], w_up[0], w_down[0])
    x_o = shift(x, 0, True)
    g_b = shift(g, -1)
    g_bo = shift(g, -1, True)
    h, saved = forward(x, *w)
    h_b = shift(h, -1)
    h_o, saved_o = forward(x_o, *w)
    h_bo = shift(h_o, -1)
    d_b, terms_b = second(h_b, g_b, *w)
    d = shift(d_b, 1)
    d_bo, terms_bo = second(h_bo, g_bo, *w)
    d_o = shift(d_bo, 1)
    dgate, dup = backward_hidden(d, saved, w[2])
    dx = backward_input(d, saved, dgate, dup, w[0], w[1])
    terms_a = (saved[2], saved[3], dgate, dup, d)
    dgate_o, dup_o = backward_hidden(d_o, saved_o, w[2])
    terms_ao = (saved_o[2], saved_o[3], dgate_o, dup_o, d_o)
    gg, gu, gd = grads((terms_b, terms_bo, terms_a, terms_ao))
    return dx[None], gg[None], gu[None], gd[None]


def local_many(tokens, cotangent, w_gate, w_up, w_down):
    x, g = tokens[0], cotangent[0]
    w = (w_gate[0], w_up[0], w_down[0])
    g_b = shift(g, -1)
    h, saved = forward(x, *w)
    h_b = shift(h, -1)
    d_b, terms_b = second(h_b, g_b, *w)
    d = shift(d_b, 1)
    dgate, dup = backward_hidden(d, saved, w[2])
    dx = backward_input(d, saved, dgate, dup, w[0], w[1])
    terms_a = (saved[2], saved[3], dgate, dup, d)
    gg, gu, gd = lax.psum(grads((terms_b, terms_a)), "dp")
    return dx[None], gg[None], gu[None], gd[None]


def solution(mesh):
    rows = P("blk", "dp", None)
    blocks = P("blk", None, None)
    body = local_pair if mesh.shape["dp"] == 2 else local_many
    return jax.shard_map(
        body,
        mesh=mesh,
        in_specs=(rows, rows, blocks, blocks, blocks),
        out_specs=(rows, blocks, blocks, blocks),
        check_vma=False,
    )
```

```python
import functools

import jax
import jax.numpy as jnp
from jax import lax
from jax.experimental import pallas as pl
from jax.experimental.pallas import tpu as pltpu
from jax.sharding import PartitionSpec as P

F32 = jnp.float32
BF16 = jnp.bfloat16
EPS = 1e-05


def shift(x, by, flip=False):
    blk, dp = lax.axis_size("blk"), lax.axis_size("dp")
    pairs = []
    for i in range(blk):
        for r in range(dp):
            to = (dp - 1 - r) if flip else r
            pairs.append((i * dp + r, ((i + by) % blk) * dp + to))
    return lax.ppermute(x, ("blk", "dp"), pairs)


def dot(a, b, dims=((1,), (0,))):
    return lax.dot_general(a, b, (dims, ((), ())), preferred_element_type=F32)


def after(x, y):
    return lax.optimization_barrier((x, y))[0]


def normalize(v):
    inverse = lax.rsqrt(jnp.mean(v * v, axis=0, keepdims=True) + EPS)
    return inverse, v * inverse


def chunks(size):
    step = 512 if size % 512 == 0 else (256 if size % 256 == 0 else size)
    return [slice(k, k + step) for k in range(0, size, step)]


def gate_values(pre_g, pre_u):
    s = 0.5 * jnp.tanh(0.5 * pre_g) + 0.5
    q = pre_g * s
    p = pre_u * (s + q * (1.0 - s))
    return q * pre_u, p, q


def input_cotangent(c, dz, inverse, normed):
    inner = jnp.mean(dz * normed, axis=0, keepdims=True)
    return (c + inverse * (dz - normed * inner)).astype(BF16)


def forward_kernel(x_ref, gate_ref, up_ref, down_ref, h_ref, z_ref, act_ref, p_ref, q_ref):
    x = x_ref[...].astype(F32)
    _, normed = normalize(x)
    zed = normed.astype(BF16)
    z_ref[...] = zed
    zt = zed.T
    total = x
    for hc in chunks(gate_ref.shape[1]):
        pre_g = dot(zt, gate_ref[:, hc])
        pre_u = dot(zt, up_ref[:, hc])
        active, p, q = gate_values(pre_g, pre_u)
        active = active.astype(BF16)
        act_ref[:, hc] = active
        p_ref[:, hc] = p.astype(BF16)
        q_ref[:, hc] = q.astype(BF16)
        total += dot(down_ref[:, hc], active, ((1,), (1,)))
    h_ref[...] = total.astype(BF16)


def second_kernel(h_ref, c_ref, gate_ref, up_ref, down_ref, d_ref, z_ref, act_ref, dg_ref, du_ref):
    inverse, normed = normalize(h_ref[...].astype(F32))
    zed = normed.astype(BF16)
    z_ref[...] = zed
    zt = zed.T
    ct = c_ref[...].T
    dz = jnp.zeros(c_ref.shape, F32)
    for hc in chunks(gate_ref.shape[1]):
        pre_g = dot(zt, gate_ref[:, hc])
        pre_u = dot(zt, up_ref[:, hc])
        da = dot(ct, down_ref[:, hc])
        active, p, q = gate_values(pre_g, pre_u)
        act_ref[:, hc] = active.astype(BF16)
        dgate = (da * p).astype(BF16)
        dup = (da * q).astype(BF16)
        dg_ref[:, hc] = dgate
        du_ref[:, hc] = dup
        dz += dot(gate_ref[:, hc], dgate, ((1,), (1,)))
        dz += dot(up_ref[:, hc], dup, ((1,), (1,)))
    d_ref[...] = input_cotangent(c_ref[...].astype(F32), dz, inverse, normed)


def first_back_kernel(x_ref, c_ref, p_ref, q_ref, gate_ref, up_ref, down_ref, d_ref, dg_ref, du_ref):
    inverse, normed = normalize(x_ref[...].astype(F32))
    ct = c_ref[...].T
    dz = jnp.zeros(c_ref.shape, F32)
    for hc in chunks(gate_ref.shape[1]):
        da = dot(ct, down_ref[:, hc])
        dgate = (da * p_ref[:, hc].astype(F32)).astype(BF16)
        dup = (da * q_ref[:, hc].astype(F32)).astype(BF16)
        dg_ref[:, hc] = dgate
        du_ref[:, hc] = dup
        dz += dot(gate_ref[:, hc], dgate, ((1,), (1,)))
        dz += dot(up_ref[:, hc], dup, ((1,), (1,)))
    d_ref[...] = input_cotangent(c_ref[...].astype(F32), dz, inverse, normed)


def grads_kernel(
    p_ref, q_ref, down_ref,
    z0, z1, z2, z3, c0, c1, c2, c3, act0, act1, act2, act3, dg0, dg1, dg2, du0, du1, du2,
    gg_ref, gu_ref, gd_ref,
):
    da = dot(c3[...].T, down_ref[...])
    dg3 = (da * p_ref[...].astype(F32)).astype(BF16)
    du3 = (da * q_ref[...].astype(F32)).astype(BF16)
    z = jnp.concatenate([z0[...], z1[...], z2[...], z3[...]], axis=1)
    dg = jnp.concatenate([dg0[...], dg1[...], dg2[...], dg3], axis=0)
    du = jnp.concatenate([du0[...], du1[...], du2[...], du3], axis=0)
    c = jnp.concatenate([c0[...], c1[...], c2[...], c3[...]], axis=1)
    act = jnp.concatenate([act0[...], act1[...], act2[...], act3[...]], axis=0)
    gd_ref[...] = dot(c, act).astype(BF16)
    gg_ref[...] = dot(z, dg).astype(BF16)
    gu_ref[...] = dot(z, du).astype(BF16)


PARAMS = pltpu.CompilerParams(vmem_limit_bytes=20 * 1024 * 1024)


def in_vmem(x):
    return pltpu.with_memory_space_constraint(x, pltpu.VMEM)


def whole(kernel, args, out_shapes, name):
    spec = pl.BlockSpec(memory_space=pltpu.VMEM)
    return pl.pallas_call(
        kernel,
        in_specs=[spec] * len(args),
        out_specs=[spec] * len(out_shapes),
        out_shape=[pltpu.VMEM(s, BF16) for s in out_shapes],
        compiler_params=PARAMS,
        name=name,
    )(*(in_vmem(a) for a in args))


def first(x, w, name):
    d, t = x.shape
    h = w[0].shape[1]
    return whole(forward_kernel, (x, *w), [(d, t), (d, t), (t, h), (t, h), (t, h)], name)


def second(v, c, w, name):
    d, t = v.shape
    h = w[0].shape[1]
    return whole(second_kernel, (v, c, *w), [(d, t), (d, t), (t, h), (t, h), (t, h)], name)


def first_back(x, c, p, q, w, name):
    d, t = x.shape
    h = w[0].shape[1]
    return whole(first_back_kernel, (x, c, p, q, *w), [(d, t), (t, h), (t, h)], name)


def grads(p, q, down, zs, cs, acts, dgs, dus):
    d, t = zs[0].shape
    h = down.shape[1]
    step = 512
    full = pl.BlockSpec(memory_space=pltpu.VMEM)
    tile = pl.BlockSpec((t, step), lambda k: (0, k))
    wide = pl.BlockSpec((d, step), lambda k: (0, k))
    return pl.pallas_call(
        grads_kernel,
        grid=(h // step,),
        in_specs=[tile, tile, wide] + [full] * 8 + [tile] * 10,
        out_specs=[wide] * 3,
        out_shape=[jax.ShapeDtypeStruct((d, h), BF16)] * 3,
        compiler_params=PARAMS,
        name="grads",
    )(p, q, down, *(in_vmem(a) for a in (*zs, *cs)), *acts, *dgs, *dus)


def local_pair(tokens, cotangent, w_gate, w_up, w_down):
    x, g = tokens[0].T, cotangent[0].T
    w = (w_gate[0], w_up[0], w_down[0].T)
    x_o = shift(x, 0, True)
    g_b = shift(g, -1)
    h, z2, act2, p2, q2 = first(x, w, "first_own")
    h_b = shift(h, -1)
    g_bo = shift(after(g_b, x_o), 0, True)
    d_b, z0, act0, dg0, du0 = second(h_b, g_b, w, "second_own")
    d = shift(d_b, 1)
    h_o, z3, act3, p3, q3 = first(x_o, w, "first_other")
    h_bo = shift(h_o, -1)
    dx, dg2, du2 = first_back(x, d, p2, q2, w, "first_back_own")
    d_bo, z1, act1, dg1, du1 = second(h_bo, g_bo, w, "second_other")
    d_o = shift(d_bo, 1)
    gg, gu, gd = grads(
        p3, q3, w[2], (z0, z1, z2, z3), (g_b, g_bo, d, d_o), (act0, act1, act2, act3), (dg0, dg1, dg2), (du0, du1, du2)
    )
    return dx.T[None], gg[None], gu[None], gd.T[None]


def many_gates(v, gate, up):
    vf = v.astype(F32)
    inverse = lax.rsqrt(jnp.mean(vf * vf, axis=-1, keepdims=True) + EPS)
    normed = vf * inverse
    zed = normed.astype(BF16)
    active, p, q = gate_values(dot(zed, gate), dot(zed, up))
    return inverse, normed, zed, active.astype(BF16), p, q


def many_back(c, saved, gate, up, down):
    inverse, normed, _, _, p, q = saved
    da = dot(c, down, ((1,), (1,)))
    dgate, dup = (da * p).astype(BF16), (da * q).astype(BF16)
    dz = dot(dgate, gate, ((1,), (1,))) + dot(dup, up, ((1,), (1,)))
    inner = jnp.mean(dz * normed, axis=-1, keepdims=True)
    return (c.astype(F32) + inverse * (dz - normed * inner)).astype(BF16), dgate, dup


def local_many(tokens, cotangent, w_gate, w_up, w_down):
    x, g = tokens[0], cotangent[0]
    gate, up, down = w_gate[0], w_up[0], w_down[0]
    g_b = shift(g, -1)
    saved = many_gates(x, gate, up)
    h = (x.astype(F32) + dot(saved[3], down)).astype(BF16)
    saved_b = many_gates(shift(h, -1), gate, up)
    d_b, dg_b, du_b = many_back(g_b, saved_b, gate, up, down)
    d = shift(d_b, 1)
    dx, dg, du = many_back(d, saved, gate, up, down)
    tn = ((0,), (0,))
    zed = jnp.concatenate([saved_b[2], saved[2]])
    parts = (
        dot(zed, jnp.concatenate([dg_b, dg]), tn),
        dot(zed, jnp.concatenate([du_b, du]), tn),
        dot(jnp.concatenate([saved_b[3], saved[3]]), jnp.concatenate([g_b, d]), tn),
    )
    gg, gu, gd = lax.psum(tuple(a.astype(BF16) for a in parts), "dp")
    return dx[None], gg[None], gu[None], gd[None]


def solution(mesh):
    rows = P("blk", "dp", None)
    blocks = P("blk", None, None)
    body = local_pair if mesh.shape["dp"] == 2 else local_many
    return jax.shard_map(
        body,
        mesh=mesh,
        in_specs=(rows, rows, blocks, blocks, blocks),
        out_specs=(rows, blocks, blocks, blocks),
        check_vma=False,
    )
```

```python
import functools

import jax
import jax.numpy as jnp
from jax import lax
from jax.experimental import pallas as pl
from jax.experimental.pallas import tpu as pltpu
from jax.sharding import PartitionSpec as P

F32 = jnp.float32
BF16 = jnp.bfloat16
EPS = 1e-05


def shift(x, by, flip=False):
    blk, dp = lax.axis_size("blk"), lax.axis_size("dp")
    pairs = []
    for i in range(blk):
        for r in range(dp):
            to = (dp - 1 - r) if flip else r
            pairs.append((i * dp + r, ((i + by) % blk) * dp + to))
    return lax.ppermute(x, ("blk", "dp"), pairs)


def dot(a, b, dims=((1,), (0,))):
    return lax.dot_general(a, b, (dims, ((), ())), preferred_element_type=F32)


def after(x, y):
    return lax.optimization_barrier((x, y))[0]


def normalize(v):
    inverse = lax.rsqrt(jnp.mean(v * v, axis=0, keepdims=True) + EPS)
    return inverse, v * inverse


def chunks(size):
    step = 512 if size % 512 == 0 else (256 if size % 256 == 0 else size)
    return [slice(k, k + step) for k in range(0, size, step)]


def gate_values(pre_g, pre_u):
    s = 0.5 * jnp.tanh(0.5 * pre_g) + 0.5
    q = pre_g * s
    p = pre_u * (s + q * (1.0 - s))
    return q * pre_u, p, q


def input_cotangent(c, dz, inverse, normed):
    inner = jnp.mean(dz * normed, axis=0, keepdims=True)
    return (c + inverse * (dz - normed * inner)).astype(BF16)


def forward_chunk(hc, zt, total, gate, up, down, act_ref, p_ref, q_ref):
    pre_g = dot(zt, gate[:, hc])
    pre_u = dot(zt, up[:, hc])
    active, p, q = gate_values(pre_g, pre_u)
    active = active.astype(BF16)
    act_ref[:, hc] = active
    p_ref[:, hc] = p.astype(BF16)
    q_ref[:, hc] = q.astype(BF16)
    return total + dot(down[:, hc], active, ((1,), (1,)))


def forward_kernel(x_ref, gate_ref, up_ref, down_ref, h_ref, z_ref, act_ref, p_ref, q_ref):
    x = x_ref[...].astype(F32)
    _, normed = normalize(x)
    zed = normed.astype(BF16)
    z_ref[...] = zed
    zt = zed.T
    total = x
    for hc in chunks(gate_ref.shape[1]):
        total = forward_chunk(hc, zt, total, gate_ref, up_ref, down_ref, act_ref, p_ref, q_ref)
    h_ref[...] = total.astype(BF16)


def loading_forward_kernel(
    x_hbm, gate_hbm, up_hbm, down_hbm, h_ref, z_ref, act_ref, p_ref, q_ref, x_ref, gate_ref, up_ref, down_ref, sem
):
    x_copy = pltpu.make_async_copy(x_hbm, x_ref, sem.at[0])
    x_copy.start()
    parts = chunks(gate_ref.shape[1])
    copies = []
    for k, hc in enumerate(parts):
        copies.append([])
        for m, (src, dst) in enumerate(((gate_hbm, gate_ref), (up_hbm, up_ref), (down_hbm, down_ref))):
            copy = pltpu.make_async_copy(src.at[:, hc], dst.at[:, hc], sem.at[1 + 3 * k + m])
            copy.start()
            copies[-1].append(copy)
    x_copy.wait()
    x = x_ref[...].astype(F32)
    _, normed = normalize(x)
    zed = normed.astype(BF16)
    z_ref[...] = zed
    zt = zed.T
    total = x
    for k, hc in enumerate(parts):
        for copy in copies[k]:
            copy.wait()
        total = forward_chunk(hc, zt, total, gate_ref, up_ref, down_ref, act_ref, p_ref, q_ref)
    h_ref[...] = total.astype(BF16)


def second_kernel(h_ref, c_ref, gate_ref, up_ref, down_ref, d_ref, z_ref, act_ref, dg_ref, du_ref):
    inverse, normed = normalize(h_ref[...].astype(F32))
    zed = normed.astype(BF16)
    z_ref[...] = zed
    zt = zed.T
    ct = c_ref[...].T
    dz = jnp.zeros(c_ref.shape, F32)
    for hc in chunks(gate_ref.shape[1]):
        pre_g = dot(zt, gate_ref[:, hc])
        pre_u = dot(zt, up_ref[:, hc])
        da = dot(ct, down_ref[:, hc])
        active, p, q = gate_values(pre_g, pre_u)
        act_ref[:, hc] = active.astype(BF16)
        dgate = (da * p).astype(BF16)
        dup = (da * q).astype(BF16)
        dg_ref[:, hc] = dgate
        du_ref[:, hc] = dup
        dz += dot(gate_ref[:, hc], dgate, ((1,), (1,)))
        dz += dot(up_ref[:, hc], dup, ((1,), (1,)))
    d_ref[...] = input_cotangent(c_ref[...].astype(F32), dz, inverse, normed)


def first_back_kernel(x_ref, c_ref, p_ref, q_ref, gate_ref, up_ref, down_ref, d_ref, dg_ref, du_ref):
    inverse, normed = normalize(x_ref[...].astype(F32))
    ct = c_ref[...].T
    dz = jnp.zeros(c_ref.shape, F32)
    for hc in chunks(gate_ref.shape[1]):
        da = dot(ct, down_ref[:, hc])
        dgate = (da * p_ref[:, hc].astype(F32)).astype(BF16)
        dup = (da * q_ref[:, hc].astype(F32)).astype(BF16)
        dg_ref[:, hc] = dgate
        du_ref[:, hc] = dup
        dz += dot(gate_ref[:, hc], dgate, ((1,), (1,)))
        dz += dot(up_ref[:, hc], dup, ((1,), (1,)))
    d_ref[...] = input_cotangent(c_ref[...].astype(F32), dz, inverse, normed)


def join(refs, hc, axis):
    return jnp.concatenate([r[:, hc] for r in refs], axis=axis)


def partial_kernel(*refs):
    zs, cs, acts, dgs, dus = (refs[3 * k : 3 * k + 3] for k in range(5))
    gg_ref, gu_ref, gd_ref = refs[15:]
    z = join(zs, slice(None), 1)
    c = join(cs, slice(None), 1)
    for hc in chunks(gg_ref.shape[1]):
        gd_ref[:, hc] = dot(c, join(acts, hc, 0)).astype(BF16)
        gg_ref[:, hc] = dot(z, join(dgs, hc, 0)).astype(BF16)
        gu_ref[:, hc] = dot(z, join(dus, hc, 0)).astype(BF16)


def final_kernel(
    c_ref, z_ref, act_ref, p_ref, q_ref, down_ref, pg_ref, pu_ref, pd_ref, dx_ref,
    gg_hbm, gu_hbm, gd_hbm, dx_hbm, gg_ref, gu_ref, gd_ref, sem,
):
    copies = [pltpu.make_async_copy(dx_ref, dx_hbm, sem.at[0])]
    copies[0].start()
    ct = c_ref[...].T
    c, z = c_ref[...], z_ref[...]
    for k, hc in enumerate(chunks(gg_ref.shape[1])):
        da = dot(ct, down_ref[:, hc])
        gd_ref[:, hc] = (pd_ref[:, hc].astype(F32) + dot(c, act_ref[:, hc])).astype(BF16)
        dgate = (da * p_ref[:, hc].astype(F32)).astype(BF16)
        gg_ref[:, hc] = (pg_ref[:, hc].astype(F32) + dot(z, dgate)).astype(BF16)
        dup = (da * q_ref[:, hc].astype(F32)).astype(BF16)
        gu_ref[:, hc] = (pu_ref[:, hc].astype(F32) + dot(z, dup)).astype(BF16)
        for m, (src, dst) in enumerate(((gg_ref, gg_hbm), (gu_ref, gu_hbm), (gd_ref, gd_hbm))):
            copies.append(pltpu.make_async_copy(src.at[:, hc], dst.at[:, hc], sem.at[1 + 3 * k + m]))
            copies[-1].start()
    for copy in copies:
        copy.wait()


PARAMS = pltpu.CompilerParams(vmem_limit_bytes=20 * 1024 * 1024)


def in_vmem(x):
    return pltpu.with_memory_space_constraint(x, pltpu.VMEM)


def whole(kernel, args, out_shapes, name):
    spec = pl.BlockSpec(memory_space=pltpu.VMEM)
    return pl.pallas_call(
        kernel,
        in_specs=[spec] * len(args),
        out_specs=[spec] * len(out_shapes),
        out_shape=[pltpu.VMEM(s, BF16) for s in out_shapes],
        compiler_params=PARAMS,
        name=name,
    )(*(in_vmem(a) for a in args))


def first(x, w, name):
    d, t = x.shape
    h = w[0].shape[1]
    return whole(forward_kernel, (x, *w), [(d, t), (d, t), (t, h), (t, h), (t, h)], name)


def loading_first(x, w, name):
    d, t = x.shape
    h = w[0].shape[1]
    shapes = [(d, t), (d, t), (t, h), (t, h), (t, h), (d, t), (d, h), (d, h), (d, h)]
    return pl.pallas_call(
        loading_forward_kernel,
        in_specs=[pl.BlockSpec(memory_space=pltpu.HBM)] * 4,
        out_specs=[pl.BlockSpec(memory_space=pltpu.VMEM)] * len(shapes),
        out_shape=[pltpu.VMEM(s, BF16) for s in shapes],
        scratch_shapes=[pltpu.SemaphoreType.DMA((1 + 3 * len(chunks(h)),))],
        compiler_params=PARAMS,
        name=name,
    )(*(pltpu.with_memory_space_constraint(a, pltpu.HBM) for a in (x, *w)))


def second(v, c, w, name):
    d, t = v.shape
    h = w[0].shape[1]
    return whole(second_kernel, (v, c, *w), [(d, t), (d, t), (t, h), (t, h), (t, h)], name)


def first_back(x, c, p, q, w, name):
    d, t = x.shape
    h = w[0].shape[1]
    return whole(first_back_kernel, (x, c, p, q, *w), [(d, t), (t, h), (t, h)], name)


def partial(zs, cs, acts, dgs, dus):
    d, h = zs[0].shape[0], acts[0].shape[1]
    return whole(partial_kernel, (*zs, *cs, *acts, *dgs, *dus), [(d, h)] * 3, "partial")


def final(c, z, act, p, q, down, parts, dx):
    d, t = c.shape
    h = down.shape[1]
    args = (c, z, act, p, q, down, *parts, dx)
    return pl.pallas_call(
        final_kernel,
        in_specs=[pl.BlockSpec(memory_space=pltpu.VMEM)] * len(args),
        out_specs=[pl.BlockSpec(memory_space=pltpu.HBM)] * 4,
        out_shape=[pltpu.HBM(s, BF16) for s in ((d, h), (d, h), (d, h), (d, t))],
        scratch_shapes=[pltpu.VMEM((d, h), BF16)] * 3 + [pltpu.SemaphoreType.DMA((1 + 3 * len(chunks(h)),))],
        compiler_params=PARAMS,
        name="final",
    )(*(in_vmem(a) for a in args))


def local_pair(tokens, cotangent, w_gate, w_up, w_down):
    x, g = tokens[0].T, cotangent[0].T
    x_o = shift(x, 0, True)
    g_b = shift(g, -1)
    h, z2, act2, p2, q2, x, *w = loading_first(x, (w_gate[0], w_up[0], w_down[0].T), "first_own")
    h_b = shift(h, -1)
    g_bo = shift(after(g_b, h), 0, True)
    x_o = after(x_o, g_b)
    h_o, z3, act3, p3, q3 = first(x_o, w, "first_other")
    h_bo = shift(h_o, -1)
    d_b, z0, act0, dg0, du0 = second(after(h_b, h_o), g_b, w, "second_own")
    d = shift(d_b, 1)
    d_bo, z1, act1, dg1, du1 = second(after(h_bo, d_b), g_bo, w, "second_other")
    d_o = shift(d_bo, 1)
    dx, dg2, du2 = first_back(x, after(d, d_bo), p2, q2, w, "first_back_own")
    parts = partial((z0, z1, z2), (g_b, g_bo, d), (act0, act1, act2), (dg0, dg1, dg2), (du0, du1, du2))
    gg, gu, gd, dx = final(d_o, z3, act3, p3, q3, w[2], parts, dx)
    return dx.T[None], gg[None], gu[None], gd.T[None]


def many_gates(v, gate, up):
    vf = v.astype(F32)
    inverse = lax.rsqrt(jnp.mean(vf * vf, axis=-1, keepdims=True) + EPS)
    normed = vf * inverse
    zed = normed.astype(BF16)
    active, p, q = gate_values(dot(zed, gate), dot(zed, up))
    return inverse, normed, zed, active.astype(BF16), p, q


def many_back(c, saved, gate, up, down):
    inverse, normed, _, _, p, q = saved
    da = dot(c, down, ((1,), (1,)))
    dgate, dup = (da * p).astype(BF16), (da * q).astype(BF16)
    dz = dot(dgate, gate, ((1,), (1,))) + dot(dup, up, ((1,), (1,)))
    inner = jnp.mean(dz * normed, axis=-1, keepdims=True)
    return (c.astype(F32) + inverse * (dz - normed * inner)).astype(BF16), dgate, dup


def local_many(tokens, cotangent, w_gate, w_up, w_down):
    x, g = tokens[0], cotangent[0]
    gate, up, down = w_gate[0], w_up[0], w_down[0]
    g_b = shift(g, -1)
    saved = many_gates(x, gate, up)
    h = (x.astype(F32) + dot(saved[3], down)).astype(BF16)
    saved_b = many_gates(shift(h, -1), gate, up)
    d_b, dg_b, du_b = many_back(g_b, saved_b, gate, up, down)
    d = shift(d_b, 1)
    dx, dg, du = many_back(d, saved, gate, up, down)
    tn = ((0,), (0,))
    zed = jnp.concatenate([saved_b[2], saved[2]])
    parts = (
        dot(zed, jnp.concatenate([dg_b, dg]), tn),
        dot(zed, jnp.concatenate([du_b, du]), tn),
        dot(jnp.concatenate([saved_b[3], saved[3]]), jnp.concatenate([g_b, d]), tn),
    )
    gg, gu, gd = lax.psum(tuple(a.astype(BF16) for a in parts), "dp")
    return dx[None], gg[None], gu[None], gd[None]


def solution(mesh):
    rows = P("blk", "dp", None)
    blocks = P("blk", None, None)
    body = local_pair if mesh.shape["dp"] == 2 else local_many
    return jax.shard_map(
        body,
        mesh=mesh,
        in_specs=(rows, rows, blocks, blocks, blocks),
        out_specs=(rows, blocks, blocks, blocks),
        check_vma=False,
    )
```

```python
import functools

import jax
import jax.numpy as jnp
from jax import lax
from jax.experimental import pallas as pl
from jax.experimental.pallas import tpu as pltpu
from jax.sharding import PartitionSpec as P

F32 = jnp.float32
BF16 = jnp.bfloat16
EPS = 1e-05


def shift(x, by, flip=False):
    blk, dp = lax.axis_size("blk"), lax.axis_size("dp")
    pairs = []
    for i in range(blk):
        for r in range(dp):
            to = (dp - 1 - r) if flip else r
            pairs.append((i * dp + r, ((i + by) % blk) * dp + to))
    return lax.ppermute(x, ("blk", "dp"), pairs)


def dot(a, b, dims=((1,), (0,))):
    return lax.dot_general(a, b, (dims, ((), ())), preferred_element_type=F32)


NT = ((1,), (1,))


def after(x, y):
    return lax.optimization_barrier((x, y))[0]


def normalize(v):
    inverse = lax.rsqrt(jnp.mean(v * v, axis=0, keepdims=True) + EPS)
    return inverse, v * inverse


def chunks(size, step=256):
    step = step if size % step == 0 else size
    return [slice(k, k + step) for k in range(0, size, step)]


def staggered(parts, ahead, use):
    ready = ahead(parts[0])
    for k, part in enumerate(parts):
        following = ahead(parts[k + 1]) if k + 1 < len(parts) else None
        use(part, ready)
        ready = following


def gate_values(pre_g, pre_u):
    s = 0.5 * jnp.tanh(0.5 * pre_g) + 0.5
    q = pre_g * s
    p = pre_u * (s + q * (1.0 - s))
    return q * pre_u, p, q


def input_cotangent(c, dz, inverse, normed):
    inner = jnp.mean(dz * normed, axis=0, keepdims=True)
    return (c + inverse * (dz - normed * inner)).astype(BF16)


def forward_body(x_ref, gate_ref, up_ref, down_ref, h_ref, z_ref, act_ref, p_ref, q_ref, arrived):
    x = x_ref[...].astype(F32)
    _, normed = normalize(x)
    zed = normed.astype(BF16)
    z_ref[...] = zed
    zt = zed.T
    total = [x]

    def ahead(hc):
        arrived(hc)
        return dot(zt, gate_ref[:, hc]), dot(zt, up_ref[:, hc])

    def use(hc, ready):
        active, p, q = gate_values(*ready)
        active = active.astype(BF16)
        act_ref[:, hc] = active
        p_ref[:, hc] = p.astype(BF16)
        q_ref[:, hc] = q.astype(BF16)
        total[0] += dot(down_ref[:, hc], active, NT)

    staggered(chunks(gate_ref.shape[1]), ahead, use)
    h_ref[...] = total[0].astype(BF16)


def forward_kernel(*refs):
    forward_body(*refs, arrived=lambda hc: None)


def loading_forward_kernel(
    x_hbm, gate_hbm, up_hbm, down_hbm, h_ref, z_ref, act_ref, p_ref, q_ref, x_ref, gate_ref, up_ref, down_ref, sem
):
    x_copy = pltpu.make_async_copy(x_hbm, x_ref, sem.at[0])
    x_copy.start()
    copies = {}
    for k, hc in enumerate(chunks(gate_ref.shape[1])):
        copies[hc.start] = []
        for m, (src, dst) in enumerate(((gate_hbm, gate_ref), (up_hbm, up_ref), (down_hbm, down_ref))):
            copy = pltpu.make_async_copy(src.at[:, hc], dst.at[:, hc], sem.at[1 + 3 * k + m])
            copy.start()
            copies[hc.start].append(copy)
    x_copy.wait()

    def arrived(hc):
        for copy in copies[hc.start]:
            copy.wait()

    forward_body(x_ref, gate_ref, up_ref, down_ref, h_ref, z_ref, act_ref, p_ref, q_ref, arrived)


def second_kernel(h_ref, c_ref, gate_ref, up_ref, down_ref, d_ref, z_ref, act_ref, dg_ref, du_ref):
    inverse, normed = normalize(h_ref[...].astype(F32))
    zed = normed.astype(BF16)
    z_ref[...] = zed
    zt = zed.T
    ct = c_ref[...].T
    dz = [jnp.zeros(c_ref.shape, F32)]

    def ahead(hc):
        return dot(zt, gate_ref[:, hc]), dot(zt, up_ref[:, hc]), dot(ct, down_ref[:, hc])

    def use(hc, ready):
        active, p, q = gate_values(*ready[:2])
        dgate = (ready[2] * p).astype(BF16)
        dup = (ready[2] * q).astype(BF16)
        act_ref[:, hc] = active.astype(BF16)
        dg_ref[:, hc] = dgate
        du_ref[:, hc] = dup
        dz[0] += dot(gate_ref[:, hc], dgate, NT) + dot(up_ref[:, hc], dup, NT)

    staggered(chunks(gate_ref.shape[1]), ahead, use)
    d_ref[...] = input_cotangent(c_ref[...].astype(F32), dz[0], inverse, normed)


def first_back_kernel(x_ref, c_ref, p_ref, q_ref, gate_ref, up_ref, down_ref, d_ref, dg_ref, du_ref):
    inverse, normed = normalize(x_ref[...].astype(F32))
    ct = c_ref[...].T
    dz = [jnp.zeros(c_ref.shape, F32)]

    def ahead(hc):
        return dot(ct, down_ref[:, hc])

    def use(hc, da):
        dgate = (da * p_ref[:, hc].astype(F32)).astype(BF16)
        dup = (da * q_ref[:, hc].astype(F32)).astype(BF16)
        dg_ref[:, hc] = dgate
        du_ref[:, hc] = dup
        dz[0] += dot(gate_ref[:, hc], dgate, NT) + dot(up_ref[:, hc], dup, NT)

    staggered(chunks(gate_ref.shape[1]), ahead, use)
    d_ref[...] = input_cotangent(c_ref[...].astype(F32), dz[0], inverse, normed)


def split(tokens):
    return (3 * tokens // 256) * 256 - 2 * tokens


def partial_kernel(*refs):
    zs, cs, acts, dgs, dus = (refs[3 * k : 3 * k + 3] for k in range(5))
    gg_ref, gu_ref, gd_ref = refs[15:]
    cut = split(acts[0].shape[0])
    z = jnp.concatenate([zs[0][...], zs[1][...], zs[2][:, :cut]], axis=1)
    c = jnp.concatenate([cs[0][...], cs[1][...], cs[2][:, :cut]], axis=1)

    def join(three, hc):
        return jnp.concatenate([three[0][:, hc], three[1][:, hc], three[2][:cut, hc]], axis=0)

    for hc in chunks(gg_ref.shape[1]):
        gd_ref[:, hc] = dot(c, join(acts, hc)).astype(BF16)
        gg_ref[:, hc] = dot(z, join(dgs, hc)).astype(BF16)
        gu_ref[:, hc] = dot(z, join(dus, hc)).astype(BF16)


def final_kernel(
    c_ref, z_ref, act_ref, p_ref, q_ref, down_ref, pg_ref, pu_ref, pd_ref, dx_ref, c2_ref, z2_ref, act2_ref, dg2_ref, du2_ref,
    gg_hbm, gu_hbm, gd_hbm, dx_hbm, gg_ref, gu_ref, gd_ref, sem,
):
    copies = [pltpu.make_async_copy(dx_ref, dx_hbm, sem.at[0])]
    copies[0].start()
    cut = split(act_ref.shape[0])
    ct = c_ref[...].T
    c = jnp.concatenate([c2_ref[:, cut:], c_ref[...]], axis=1)
    z = jnp.concatenate([z2_ref[:, cut:], z_ref[...]], axis=1)
    parts = chunks(gg_ref.shape[1])

    def add(hc, m, left, rows, part_ref, ref, hbm):
        ref[:, hc] = (part_ref[:, hc].astype(F32) + dot(left, jnp.concatenate(rows, axis=0))).astype(BF16)
        copy = pltpu.make_async_copy(ref.at[:, hc], hbm.at[:, hc], sem.at[1 + 3 * (hc.start // parts[0].stop) + m])
        copy.start()
        copies.append(copy)

    def ahead(hc):
        return dot(ct, down_ref[:, hc])

    def use(hc, da):
        dgate = (da * p_ref[:, hc].astype(F32)).astype(BF16)
        dup = (da * q_ref[:, hc].astype(F32)).astype(BF16)
        add(hc, 2, c, [act2_ref[cut:, hc], act_ref[:, hc]], pd_ref, gd_ref, gd_hbm)
        add(hc, 0, z, [dg2_ref[cut:, hc], dgate], pg_ref, gg_ref, gg_hbm)
        add(hc, 1, z, [du2_ref[cut:, hc], dup], pu_ref, gu_ref, gu_hbm)

    staggered(parts, ahead, use)
    for copy in copies:
        copy.wait()


PARAMS = pltpu.CompilerParams(vmem_limit_bytes=20 * 1024 * 1024)
COST = pl.CostEstimate(flops=10**10, bytes_accessed=3 * 10**7, transcendentals=0)


def in_vmem(x):
    return pltpu.with_memory_space_constraint(x, pltpu.VMEM)


def whole(kernel, args, out_shapes, name):
    spec = pl.BlockSpec(memory_space=pltpu.VMEM)
    return pl.pallas_call(
        kernel,
        in_specs=[spec] * len(args),
        out_specs=[spec] * len(out_shapes),
        out_shape=[pltpu.VMEM(s, BF16) for s in out_shapes],
        compiler_params=PARAMS,
        cost_estimate=COST,
        name=name,
    )(*(in_vmem(a) for a in args))


def first(x, w, name):
    d, t = x.shape
    h = w[0].shape[1]
    return whole(forward_kernel, (x, *w), [(d, t), (d, t), (t, h), (t, h), (t, h)], name)


def loading_first(x, w, name):
    d, t = x.shape
    h = w[0].shape[1]
    shapes = [(d, t), (d, t), (t, h), (t, h), (t, h), (d, t), (d, h), (d, h), (d, h)]
    return pl.pallas_call(
        loading_forward_kernel,
        in_specs=[pl.BlockSpec(memory_space=pltpu.HBM)] * 4,
        out_specs=[pl.BlockSpec(memory_space=pltpu.VMEM)] * len(shapes),
        out_shape=[pltpu.VMEM(s, BF16) for s in shapes],
        scratch_shapes=[pltpu.SemaphoreType.DMA((1 + 3 * len(chunks(h)),))],
        compiler_params=PARAMS,
        cost_estimate=COST,
        name=name,
    )(*(pltpu.with_memory_space_constraint(a, pltpu.HBM) for a in (x, *w)))


def second(v, c, w, name):
    d, t = v.shape
    h = w[0].shape[1]
    return whole(second_kernel, (v, c, *w), [(d, t), (d, t), (t, h), (t, h), (t, h)], name)


def first_back(x, c, p, q, w, name):
    d, t = x.shape
    h = w[0].shape[1]
    return whole(first_back_kernel, (x, c, p, q, *w), [(d, t), (t, h), (t, h)], name)


def partial(zs, cs, acts, dgs, dus):
    d, h = zs[0].shape[0], acts[0].shape[1]
    return whole(partial_kernel, (*zs, *cs, *acts, *dgs, *dus), [(d, h)] * 3, "partial")


def final(c, z, act, p, q, down, parts, dx, held):
    d, t = c.shape
    h = down.shape[1]
    args = (c, z, act, p, q, down, *parts, dx, *held)
    return pl.pallas_call(
        final_kernel,
        in_specs=[pl.BlockSpec(memory_space=pltpu.VMEM)] * len(args),
        out_specs=[pl.BlockSpec(memory_space=pltpu.HBM)] * 4,
        out_shape=[pltpu.HBM(s, BF16) for s in ((d, h), (d, h), (d, h), (d, t))],
        scratch_shapes=[pltpu.VMEM((d, h), BF16)] * 3 + [pltpu.SemaphoreType.DMA((1 + 3 * len(chunks(h)),))],
        compiler_params=PARAMS,
        cost_estimate=COST,
        name="final",
    )(*(in_vmem(a) for a in args))


def local_pair(tokens, cotangent, w_gate, w_up, w_down):
    x, g = tokens[0].T, cotangent[0].T
    x_o = shift(x, 0, True)
    g_b = shift(g, -1)
    h, z2, act2, p2, q2, x, *w = loading_first(x, (w_gate[0], w_up[0], w_down[0].T), "first_own")
    h_b = shift(h, -1)
    g_bo = shift(after(g_b, h), 0, True)
    x_o = after(x_o, g_b)
    h_o, z3, act3, p3, q3 = first(x_o, w, "first_other")
    h_bo = shift(h_o, -1)
    d_b, z0, act0, dg0, du0 = second(after(h_b, h_o), g_b, w, "second_own")
    d = shift(d_b, 1)
    d_bo, z1, act1, dg1, du1 = second(after(h_bo, d_b), g_bo, w, "second_other")
    d_o = shift(d_bo, 1)
    dx, dg2, du2 = first_back(x, after(d, d_bo), p2, q2, w, "first_back_own")
    parts = partial((z0, z1, z2), (g_b, g_bo, d), (act0, act1, act2), (dg0, dg1, dg2), (du0, du1, du2))
    gg, gu, gd, dx = final(d_o, z3, act3, p3, q3, w[2], parts, dx, (d, z2, act2, dg2, du2))
    return dx.T[None], gg[None], gu[None], gd.T[None]


def many_gates(v, gate, up):
    vf = v.astype(F32)
    inverse = lax.rsqrt(jnp.mean(vf * vf, axis=-1, keepdims=True) + EPS)
    normed = vf * inverse
    zed = normed.astype(BF16)
    active, p, q = gate_values(dot(zed, gate), dot(zed, up))
    return inverse, normed, zed, active.astype(BF16), p, q


def many_back(c, saved, gate, up, down):
    inverse, normed, _, _, p, q = saved
    da = dot(c, down, ((1,), (1,)))
    dgate, dup = (da * p).astype(BF16), (da * q).astype(BF16)
    dz = dot(dgate, gate, ((1,), (1,))) + dot(dup, up, ((1,), (1,)))
    inner = jnp.mean(dz * normed, axis=-1, keepdims=True)
    return (c.astype(F32) + inverse * (dz - normed * inner)).astype(BF16), dgate, dup


def local_many(tokens, cotangent, w_gate, w_up, w_down):
    x, g = tokens[0], cotangent[0]
    gate, up, down = w_gate[0], w_up[0], w_down[0]
    g_b = shift(g, -1)
    saved = many_gates(x, gate, up)
    h = (x.astype(F32) + dot(saved[3], down)).astype(BF16)
    saved_b = many_gates(shift(h, -1), gate, up)
    d_b, dg_b, du_b = many_back(g_b, saved_b, gate, up, down)
    d = shift(d_b, 1)
    dx, dg, du = many_back(d, saved, gate, up, down)
    tn = ((0,), (0,))
    zed = jnp.concatenate([saved_b[2], saved[2]])
    parts = (
        dot(zed, jnp.concatenate([dg_b, dg]), tn),
        dot(zed, jnp.concatenate([du_b, du]), tn),
        dot(jnp.concatenate([saved_b[3], saved[3]]), jnp.concatenate([g_b, d]), tn),
    )
    gg, gu, gd = lax.psum(tuple(a.astype(BF16) for a in parts), "dp")
    return dx[None], gg[None], gu[None], gd[None]


def solution(mesh):
    rows = P("blk", "dp", None)
    blocks = P("blk", None, None)
    body = local_pair if mesh.shape["dp"] == 2 else local_many
    return jax.shard_map(
        body,
        mesh=mesh,
        in_specs=(rows, rows, blocks, blocks, blocks),
        out_specs=(rows, blocks, blocks, blocks),
        check_vma=False,
    )
```

```python
import functools

import jax
import jax.numpy as jnp
from jax import lax
from jax.experimental import pallas as pl
from jax.experimental.pallas import tpu as pltpu
from jax.sharding import PartitionSpec as P

F32 = jnp.float32
BF16 = jnp.bfloat16
EPS = 1e-05


def shift(x, by, flip=False):
    blk, dp = lax.axis_size("blk"), lax.axis_size("dp")
    pairs = []
    for i in range(blk):
        for r in range(dp):
            to = (dp - 1 - r) if flip else r
            pairs.append((i * dp + r, ((i + by) % blk) * dp + to))
    return lax.ppermute(x, ("blk", "dp"), pairs)


def dot(a, b, dims=((1,), (0,))):
    return lax.dot_general(a, b, (dims, ((), ())), preferred_element_type=F32)


NT = ((1,), (1,))


def after(x, y):
    return lax.optimization_barrier((x, y))[0]


def normalize(v):
    inverse = lax.rsqrt(jnp.mean(v * v, axis=0, keepdims=True) + EPS)
    return inverse, v * inverse


def chunks(size, step=256):
    step = step if size % step == 0 else size
    return [slice(k, k + step) for k in range(0, size, step)]


def staggered(parts, ahead, use):
    ready = ahead(parts[0])
    for k, part in enumerate(parts):
        following = ahead(parts[k + 1]) if k + 1 < len(parts) else None
        use(part, ready)
        ready = following


def gate_values(pre_g, pre_u):
    s = 0.5 * jnp.tanh(0.5 * pre_g) + 0.5
    q = pre_g * s
    p = pre_u * (s + q * (1.0 - s))
    return q * pre_u, p, q


def input_cotangent(c, dz, inverse, normed):
    inner = jnp.mean(dz * normed, axis=0, keepdims=True)
    return (c + inverse * (dz - normed * inner)).astype(BF16)


def forward_body(x_ref, gate_ref, up_ref, down_ref, h_ref, z_ref, act_ref, p_ref, q_ref, arrived):
    x = x_ref[...].astype(F32)
    _, normed = normalize(x)
    zed = normed.astype(BF16)
    z_ref[...] = zed
    zt = zed.T

    def ahead(hc):
        arrived(hc)
        return dot(zt, gate_ref[:, hc]), dot(zt, up_ref[:, hc])

    def use(hc, ready):
        active, p, q = gate_values(*ready)
        act_ref[:, hc] = active.astype(BF16)
        p_ref[:, hc] = p.astype(BF16)
        q_ref[:, hc] = q.astype(BF16)

    staggered(chunks(gate_ref.shape[1]), ahead, use)
    h_ref[...] = (x + dot(down_ref[...], act_ref[...], NT)).astype(BF16)


def forward_kernel(*refs):
    forward_body(*refs, arrived=lambda hc: None)


def loading_forward_kernel(
    x_hbm, gate_hbm, up_hbm, down_hbm, h_ref, z_ref, act_ref, p_ref, q_ref, x_ref, gate_ref, up_ref, down_ref, sem
):
    x_copy = pltpu.make_async_copy(x_hbm, x_ref, sem.at[0])
    x_copy.start()
    copies = {}
    for k, hc in enumerate(chunks(gate_ref.shape[1])):
        copies[hc.start] = []
        for m, (src, dst) in enumerate(((gate_hbm, gate_ref), (up_hbm, up_ref), (down_hbm, down_ref))):
            copy = pltpu.make_async_copy(src.at[:, hc], dst.at[:, hc], sem.at[1 + 3 * k + m])
            copy.start()
            copies[hc.start].append(copy)
    x_copy.wait()

    def arrived(hc):
        for copy in copies[hc.start]:
            copy.wait()

    forward_body(x_ref, gate_ref, up_ref, down_ref, h_ref, z_ref, act_ref, p_ref, q_ref, arrived)


def second_kernel(h_ref, c_ref, gate_ref, up_ref, down_ref, d_ref, z_ref, act_ref, dg_ref, du_ref):
    inverse, normed = normalize(h_ref[...].astype(F32))
    zed = normed.astype(BF16)
    z_ref[...] = zed
    zt = zed.T
    ct = c_ref[...].T

    def ahead(hc):
        return dot(zt, gate_ref[:, hc]), dot(zt, up_ref[:, hc]), dot(ct, down_ref[:, hc])

    def use(hc, ready):
        active, p, q = gate_values(*ready[:2])
        act_ref[:, hc] = active.astype(BF16)
        dg_ref[:, hc] = (ready[2] * p).astype(BF16)
        du_ref[:, hc] = (ready[2] * q).astype(BF16)

    staggered(chunks(gate_ref.shape[1]), ahead, use)
    dz = dot(gate_ref[...], dg_ref[...], NT) + dot(up_ref[...], du_ref[...], NT)
    d_ref[...] = input_cotangent(c_ref[...].astype(F32), dz, inverse, normed)


def first_back_kernel(x_ref, c_ref, p_ref, q_ref, gate_ref, up_ref, down_ref, d_ref, dg_ref, du_ref):
    inverse, normed = normalize(x_ref[...].astype(F32))
    ct = c_ref[...].T

    def ahead(hc):
        return dot(ct, down_ref[:, hc])

    def use(hc, da):
        dg_ref[:, hc] = (da * p_ref[:, hc].astype(F32)).astype(BF16)
        du_ref[:, hc] = (da * q_ref[:, hc].astype(F32)).astype(BF16)

    staggered(chunks(gate_ref.shape[1]), ahead, use)
    dz = dot(gate_ref[...], dg_ref[...], NT) + dot(up_ref[...], du_ref[...], NT)
    d_ref[...] = input_cotangent(c_ref[...].astype(F32), dz, inverse, normed)


def split(tokens):
    return (3 * tokens // 256) * 256 - 2 * tokens


def partial_kernel(*refs):
    zs, cs, acts, dgs, dus = (refs[3 * k : 3 * k + 3] for k in range(5))
    gg_ref, gu_ref, gd_ref = refs[15:]
    cut = split(acts[0].shape[0])
    z = jnp.concatenate([zs[0][...], zs[1][...], zs[2][:, :cut]], axis=1)
    c = jnp.concatenate([cs[0][...], cs[1][...], cs[2][:, :cut]], axis=1)

    def join(three, hc):
        return jnp.concatenate([three[0][:, hc], three[1][:, hc], three[2][:cut, hc]], axis=0)

    for hc in chunks(gg_ref.shape[1]):
        gd_ref[:, hc] = dot(c, join(acts, hc)).astype(BF16)
        gg_ref[:, hc] = dot(z, join(dgs, hc)).astype(BF16)
        gu_ref[:, hc] = dot(z, join(dus, hc)).astype(BF16)


def final_kernel(
    c_ref, z_ref, act_ref, p_ref, q_ref, down_ref, pg_ref, pu_ref, pd_ref, dx_ref, c2_ref, z2_ref, act2_ref, dg2_ref, du2_ref,
    gg_hbm, gu_hbm, gd_hbm, dx_hbm, gg_ref, gu_ref, gd_ref, sem,
):
    copies = [pltpu.make_async_copy(dx_ref, dx_hbm, sem.at[0])]
    copies[0].start()
    cut = split(act_ref.shape[0])
    ct = c_ref[...].T
    c = jnp.concatenate([c2_ref[:, cut:], c_ref[...]], axis=1)
    z = jnp.concatenate([z2_ref[:, cut:], z_ref[...]], axis=1)
    parts = chunks(gg_ref.shape[1])

    def add(hc, m, left, rows, part_ref, ref, hbm):
        ref[:, hc] = (part_ref[:, hc].astype(F32) + dot(left, jnp.concatenate(rows, axis=0))).astype(BF16)
        copy = pltpu.make_async_copy(ref.at[:, hc], hbm.at[:, hc], sem.at[1 + 3 * (hc.start // parts[0].stop) + m])
        copy.start()
        copies.append(copy)

    def ahead(hc):
        return dot(ct, down_ref[:, hc])

    def use(hc, da):
        dgate = (da * p_ref[:, hc].astype(F32)).astype(BF16)
        dup = (da * q_ref[:, hc].astype(F32)).astype(BF16)
        add(hc, 2, c, [act2_ref[cut:, hc], act_ref[:, hc]], pd_ref, gd_ref, gd_hbm)
        add(hc, 0, z, [dg2_ref[cut:, hc], dgate], pg_ref, gg_ref, gg_hbm)
        add(hc, 1, z, [du2_ref[cut:, hc], dup], pu_ref, gu_ref, gu_hbm)

    staggered(parts, ahead, use)
    for copy in copies:
        copy.wait()


PARAMS = pltpu.CompilerParams(vmem_limit_bytes=20 * 1024 * 1024)
COST = pl.CostEstimate(flops=10**10, bytes_accessed=3 * 10**7, transcendentals=0)


def in_vmem(x):
    return pltpu.with_memory_space_constraint(x, pltpu.VMEM)


def whole(kernel, args, out_shapes, name):
    spec = pl.BlockSpec(memory_space=pltpu.VMEM)
    return pl.pallas_call(
        kernel,
        in_specs=[spec] * len(args),
        out_specs=[spec] * len(out_shapes),
        out_shape=[pltpu.VMEM(s, BF16) for s in out_shapes],
        compiler_params=PARAMS,
        cost_estimate=COST,
        name=name,
    )(*(in_vmem(a) for a in args))


def first(x, w, name):
    d, t = x.shape
    h = w[0].shape[1]
    return whole(forward_kernel, (x, *w), [(d, t), (d, t), (t, h), (t, h), (t, h)], name)


def loading_first(x, w, name):
    d, t = x.shape
    h = w[0].shape[1]
    shapes = [(d, t), (d, t), (t, h), (t, h), (t, h), (d, t), (d, h), (d, h), (d, h)]
    return pl.pallas_call(
        loading_forward_kernel,
        in_specs=[pl.BlockSpec(memory_space=pltpu.HBM)] * 4,
        out_specs=[pl.BlockSpec(memory_space=pltpu.VMEM)] * len(shapes),
        out_shape=[pltpu.VMEM(s, BF16) for s in shapes],
        scratch_shapes=[pltpu.SemaphoreType.DMA((1 + 3 * len(chunks(h)),))],
        compiler_params=PARAMS,
        cost_estimate=COST,
        name=name,
    )(*(pltpu.with_memory_space_constraint(a, pltpu.HBM) for a in (x, *w)))


def second(v, c, w, name):
    d, t = v.shape
    h = w[0].shape[1]
    return whole(second_kernel, (v, c, *w), [(d, t), (d, t), (t, h), (t, h), (t, h)], name)


def first_back(x, c, p, q, w, name):
    d, t = x.shape
    h = w[0].shape[1]
    return whole(first_back_kernel, (x, c, p, q, *w), [(d, t), (t, h), (t, h)], name)


def partial(zs, cs, acts, dgs, dus):
    d, h = zs[0].shape[0], acts[0].shape[1]
    return whole(partial_kernel, (*zs, *cs, *acts, *dgs, *dus), [(d, h)] * 3, "partial")


def final(c, z, act, p, q, down, parts, dx, held):
    d, t = c.shape
    h = down.shape[1]
    args = (c, z, act, p, q, down, *parts, dx, *held)
    return pl.pallas_call(
        final_kernel,
        in_specs=[pl.BlockSpec(memory_space=pltpu.VMEM)] * len(args),
        out_specs=[pl.BlockSpec(memory_space=pltpu.HBM)] * 4,
        out_shape=[pltpu.HBM(s, BF16) for s in ((d, h), (d, h), (d, h), (d, t))],
        scratch_shapes=[pltpu.VMEM((d, h), BF16)] * 3 + [pltpu.SemaphoreType.DMA((1 + 3 * len(chunks(h)),))],
        compiler_params=PARAMS,
        cost_estimate=COST,
        name="final",
    )(*(in_vmem(a) for a in args))


def local_pair(tokens, cotangent, w_gate, w_up, w_down):
    x, g = tokens[0].T, cotangent[0].T
    x_o = shift(x, 0, True)
    g_b = shift(g, -1)
    h, z2, act2, p2, q2, x, *w = loading_first(x, (w_gate[0], w_up[0], w_down[0].T), "first_own")
    h_b = shift(h, -1)
    g_bo = shift(after(g_b, h), 0, True)
    x_o = after(x_o, g_b)
    h_o, z3, act3, p3, q3 = first(x_o, w, "first_other")
    h_bo = shift(h_o, -1)
    d_b, z0, act0, dg0, du0 = second(after(h_b, h_o), g_b, w, "second_own")
    d = shift(d_b, 1)
    d_bo, z1, act1, dg1, du1 = second(after(h_bo, d_b), g_bo, w, "second_other")
    d_o = shift(d_bo, 1)
    dx, dg2, du2 = first_back(x, after(d, d_bo), p2, q2, w, "first_back_own")
    parts = partial((z0, z1, z2), (g_b, g_bo, d), (act0, act1, act2), (dg0, dg1, dg2), (du0, du1, du2))
    gg, gu, gd, dx = final(d_o, z3, act3, p3, q3, w[2], parts, dx, (d, z2, act2, dg2, du2))
    return dx.T[None], gg[None], gu[None], gd.T[None]


def many_gates(v, gate, up):
    vf = v.astype(F32)
    inverse = lax.rsqrt(jnp.mean(vf * vf, axis=-1, keepdims=True) + EPS)
    normed = vf * inverse
    zed = normed.astype(BF16)
    active, p, q = gate_values(dot(zed, gate), dot(zed, up))
    return inverse, normed, zed, active.astype(BF16), p, q


def many_back(c, saved, gate, up, down):
    inverse, normed, _, _, p, q = saved
    da = dot(c, down, ((1,), (1,)))
    dgate, dup = (da * p).astype(BF16), (da * q).astype(BF16)
    dz = dot(dgate, gate, ((1,), (1,))) + dot(dup, up, ((1,), (1,)))
    inner = jnp.mean(dz * normed, axis=-1, keepdims=True)
    return (c.astype(F32) + inverse * (dz - normed * inner)).astype(BF16), dgate, dup


def local_many(tokens, cotangent, w_gate, w_up, w_down):
    x, g = tokens[0], cotangent[0]
    gate, up, down = w_gate[0], w_up[0], w_down[0]
    g_b = shift(g, -1)
    saved = many_gates(x, gate, up)
    h = (x.astype(F32) + dot(saved[3], down)).astype(BF16)
    saved_b = many_gates(shift(h, -1), gate, up)
    d_b, dg_b, du_b = many_back(g_b, saved_b, gate, up, down)
    d = shift(d_b, 1)
    dx, dg, du = many_back(d, saved, gate, up, down)
    tn = ((0,), (0,))
    zed = jnp.concatenate([saved_b[2], saved[2]])
    parts = (
        dot(zed, jnp.concatenate([dg_b, dg]), tn),
        dot(zed, jnp.concatenate([du_b, du]), tn),
        dot(jnp.concatenate([saved_b[3], saved[3]]), jnp.concatenate([g_b, d]), tn),
    )
    gg, gu, gd = lax.psum(tuple(a.astype(BF16) for a in parts), "dp")
    return dx[None], gg[None], gu[None], gd[None]


def solution(mesh):
    rows = P("blk", "dp", None)
    blocks = P("blk", None, None)
    body = local_pair if mesh.shape["dp"] == 2 else local_many
    return jax.shard_map(
        body,
        mesh=mesh,
        in_specs=(rows, rows, blocks, blocks, blocks),
        out_specs=(rows, blocks, blocks, blocks),
        check_vma=False,
    )
```

```python
import functools

import jax
import jax.numpy as jnp
from jax import lax
from jax.experimental import pallas as pl
from jax.experimental.pallas import tpu as pltpu
from jax.sharding import PartitionSpec as P

F32 = jnp.float32
BF16 = jnp.bfloat16
EPS = 1e-05


def shift(x, by, flip=False):
    blk, dp = lax.axis_size("blk"), lax.axis_size("dp")
    pairs = []
    for i in range(blk):
        for r in range(dp):
            to = (dp - 1 - r) if flip else r
            pairs.append((i * dp + r, ((i + by) % blk) * dp + to))
    return lax.ppermute(x, ("blk", "dp"), pairs)


def dot(a, b, dims=((1,), (0,))):
    return lax.dot_general(a, b, (dims, ((), ())), preferred_element_type=F32)


NT = ((1,), (1,))


def after(x, y):
    return lax.optimization_barrier((x, y))[0]


def normalize(v):
    inverse = lax.rsqrt(jnp.mean(v * v, axis=0, keepdims=True) + EPS)
    return inverse, v * inverse


def chunks(size, step=256):
    step = step if size % step == 0 else size
    return [slice(k, k + step) for k in range(0, size, step)]


def staggered(parts, ahead, use):
    ready = ahead(parts[0])
    for k, part in enumerate(parts):
        following = ahead(parts[k + 1]) if k + 1 < len(parts) else None
        use(part, ready)
        ready = following


def gate_values(pre_g, pre_u):
    s = 0.5 * jnp.tanh(0.5 * pre_g) + 0.5
    q = pre_g * s
    p = pre_u * (s + q * (1.0 - s))
    return q * pre_u, p, q


def input_cotangent(c, dz, inverse, normed):
    inner = jnp.mean(dz * normed, axis=0, keepdims=True)
    return (c + inverse * (dz - normed * inner)).astype(BF16)


def forward_body(x_ref, gate_ref, up_ref, down_ref, h_ref, z_ref, act_ref, p_ref, q_ref, arrived):
    x = x_ref[...].astype(F32)
    _, normed = normalize(x)
    zed = normed.astype(BF16)
    z_ref[...] = zed
    zt = zed.T

    def ahead(hc):
        arrived(hc)
        return dot(zt, gate_ref[:, hc]), dot(zt, up_ref[:, hc])

    def use(hc, ready):
        active, p, q = gate_values(*ready)
        act_ref[:, hc] = active.astype(BF16)
        p_ref[:, hc] = p.astype(BF16)
        q_ref[:, hc] = q.astype(BF16)

    staggered(chunks(gate_ref.shape[1]), ahead, use)
    h_ref[...] = (x + dot(down_ref[...], act_ref[...], NT)).astype(BF16)


def forward_kernel(*refs):
    forward_body(*refs, arrived=lambda hc: None)


def loading_forward_kernel(
    x_hbm, gate_hbm, up_hbm, down_hbm, h_ref, z_ref, act_ref, p_ref, q_ref, x_ref, gate_ref, up_ref, down_ref, sem
):
    x_copy = pltpu.make_async_copy(x_hbm, x_ref, sem.at[0])
    x_copy.start()
    copies = {}
    for k, hc in enumerate(chunks(gate_ref.shape[1])):
        copies[hc.start] = []
        for m, (src, dst) in enumerate(((gate_hbm, gate_ref), (up_hbm, up_ref), (down_hbm, down_ref))):
            copy = pltpu.make_async_copy(src.at[:, hc], dst.at[:, hc], sem.at[1 + 3 * k + m])
            copy.start()
            copies[hc.start].append(copy)
    x_copy.wait()

    def arrived(hc):
        for copy in copies[hc.start]:
            copy.wait()

    forward_body(x_ref, gate_ref, up_ref, down_ref, h_ref, z_ref, act_ref, p_ref, q_ref, arrived)


def second_kernel(h_ref, c_ref, gate_ref, up_ref, down_ref, d_ref, z_ref, act_ref, dg_ref, du_ref):
    inverse, normed = normalize(h_ref[...].astype(F32))
    zed = normed.astype(BF16)
    z_ref[...] = zed
    zt = zed.T
    ct = c_ref[...].T

    def ahead(hc):
        return dot(zt, gate_ref[:, hc]), dot(zt, up_ref[:, hc]), dot(ct, down_ref[:, hc])

    def use(hc, ready):
        active, p, q = gate_values(*ready[:2])
        act_ref[:, hc] = active.astype(BF16)
        dg_ref[:, hc] = (ready[2] * p).astype(BF16)
        du_ref[:, hc] = (ready[2] * q).astype(BF16)

    staggered(chunks(gate_ref.shape[1]), ahead, use)
    dz = dot(gate_ref[...], dg_ref[...], NT) + dot(up_ref[...], du_ref[...], NT)
    d_ref[...] = input_cotangent(c_ref[...].astype(F32), dz, inverse, normed)


def second_grads_kernel(
    h_ref, c_ref, gate_ref, up_ref, down_ref, z0_ref, c0_ref, act0_ref, dg0_ref, du0_ref, gg_ref, gu_ref, gd_ref
):
    _, normed = normalize(h_ref[...].astype(F32))
    zed = normed.astype(BF16)
    zt = zed.T
    ct = c_ref[...].T
    z = jnp.concatenate([z0_ref[...], zed], axis=1)
    c = jnp.concatenate([c0_ref[...], c_ref[...]], axis=1)

    def ahead(hc):
        return dot(zt, gate_ref[:, hc]), dot(zt, up_ref[:, hc]), dot(ct, down_ref[:, hc])

    def use(hc, ready):
        active, p, q = gate_values(*ready[:2])
        gd_ref[:, hc] = dot(c, stack(act0_ref[:, hc], active)).astype(BF16)
        gg_ref[:, hc] = dot(z, stack(dg0_ref[:, hc], ready[2] * p)).astype(BF16)
        gu_ref[:, hc] = dot(z, stack(du0_ref[:, hc], ready[2] * q)).astype(BF16)

    staggered(chunks(gate_ref.shape[1]), ahead, use)


def stack(above, below):
    return jnp.concatenate([above, below.astype(BF16)], axis=0)


def first_back_kernel(x_ref, c_ref, p_ref, q_ref, gate_ref, up_ref, down_ref, d_ref, dg_ref, du_ref):
    inverse, normed = normalize(x_ref[...].astype(F32))
    ct = c_ref[...].T

    def ahead(hc):
        return dot(ct, down_ref[:, hc])

    def use(hc, da):
        dg_ref[:, hc] = (da * p_ref[:, hc].astype(F32)).astype(BF16)
        du_ref[:, hc] = (da * q_ref[:, hc].astype(F32)).astype(BF16)

    staggered(chunks(gate_ref.shape[1]), ahead, use)
    dz = dot(gate_ref[...], dg_ref[...], NT) + dot(up_ref[...], du_ref[...], NT)
    d_ref[...] = input_cotangent(c_ref[...].astype(F32), dz, inverse, normed)


def final_kernel(
    c_ref, z_ref, act_ref, p_ref, q_ref, down_ref, pg_ref, pu_ref, pd_ref, dx_ref, c2_ref, z2_ref, act2_ref, dg2_ref, du2_ref,
    gg_hbm, gu_hbm, gd_hbm, dx_hbm, gg_ref, gu_ref, gd_ref, sem,
):
    copies = [pltpu.make_async_copy(dx_ref, dx_hbm, sem.at[0])]
    copies[0].start()
    ct = c_ref[...].T
    c = jnp.concatenate([c2_ref[...], c_ref[...]], axis=1)
    z = jnp.concatenate([z2_ref[...], z_ref[...]], axis=1)
    parts = chunks(gg_ref.shape[1])

    def add(hc, m, left, right, part_ref, ref, hbm):
        ref[:, hc] = (part_ref[:, hc].astype(F32) + dot(left, right)).astype(BF16)
        copy = pltpu.make_async_copy(ref.at[:, hc], hbm.at[:, hc], sem.at[1 + 3 * (hc.start // parts[0].stop) + m])
        copy.start()
        copies.append(copy)

    def ahead(hc):
        return dot(ct, down_ref[:, hc])

    def use(hc, da):
        add(hc, 2, c, stack(act2_ref[:, hc], act_ref[:, hc]), pd_ref, gd_ref, gd_hbm)
        add(hc, 0, z, stack(dg2_ref[:, hc], da * p_ref[:, hc].astype(F32)), pg_ref, gg_ref, gg_hbm)
        add(hc, 1, z, stack(du2_ref[:, hc], da * q_ref[:, hc].astype(F32)), pu_ref, gu_ref, gu_hbm)

    staggered(parts, ahead, use)
    for copy in copies:
        copy.wait()


PARAMS = pltpu.CompilerParams(vmem_limit_bytes=20 * 1024 * 1024)
COSTS = {}


def cost(name):
    return pl.CostEstimate(flops=COSTS.get(name, 10**10), bytes_accessed=3 * 10**7, transcendentals=0)


def in_vmem(x):
    return pltpu.with_memory_space_constraint(x, pltpu.VMEM)


def whole(kernel, args, out_shapes, name):
    spec = pl.BlockSpec(memory_space=pltpu.VMEM)
    return pl.pallas_call(
        kernel,
        in_specs=[spec] * len(args),
        out_specs=[spec] * len(out_shapes),
        out_shape=[pltpu.VMEM(s, BF16) for s in out_shapes],
        compiler_params=PARAMS,
        cost_estimate=cost(name),
        name=name,
    )(*(in_vmem(a) for a in args))


def first(x, w, name):
    d, t = x.shape
    h = w[0].shape[1]
    return whole(forward_kernel, (x, *w), [(d, t), (d, t), (t, h), (t, h), (t, h)], name)


def loading_first(x, w, name):
    d, t = x.shape
    h = w[0].shape[1]
    shapes = [(d, t), (d, t), (t, h), (t, h), (t, h), (d, t), (d, h), (d, h), (d, h)]
    return pl.pallas_call(
        loading_forward_kernel,
        in_specs=[pl.BlockSpec(memory_space=pltpu.HBM)] * 4,
        out_specs=[pl.BlockSpec(memory_space=pltpu.VMEM)] * len(shapes),
        out_shape=[pltpu.VMEM(s, BF16) for s in shapes],
        scratch_shapes=[pltpu.SemaphoreType.DMA((1 + 3 * len(chunks(h)),))],
        compiler_params=PARAMS,
        cost_estimate=cost(name),
        name=name,
    )(*(pltpu.with_memory_space_constraint(a, pltpu.HBM) for a in (x, *w)))


def second(v, c, w):
    d, t = v.shape
    h = w[0].shape[1]
    return whole(second_kernel, (v, c, *w), [(d, t), (d, t), (t, h), (t, h), (t, h)], "second_own")


def second_grads(v, c, w, own):
    d, h = w[0].shape
    return whole(second_grads_kernel, (v, c, *w, *own), [(d, h)] * 3, "second_grads")


def first_back(x, c, p, q, w, name):
    d, t = x.shape
    h = w[0].shape[1]
    return whole(first_back_kernel, (x, c, p, q, *w), [(d, t), (t, h), (t, h)], name)


def final(c, z, act, p, q, down, parts, dx, held):
    d, t = c.shape
    h = down.shape[1]
    args = (c, z, act, p, q, down, *parts, dx, *held)
    return pl.pallas_call(
        final_kernel,
        in_specs=[pl.BlockSpec(memory_space=pltpu.VMEM)] * len(args),
        out_specs=[pl.BlockSpec(memory_space=pltpu.HBM)] * 4,
        out_shape=[pltpu.HBM(s, BF16) for s in ((d, h), (d, h), (d, h), (d, t))],
        scratch_shapes=[pltpu.VMEM((d, h), BF16)] * 3 + [pltpu.SemaphoreType.DMA((1 + 3 * len(chunks(h)),))],
        compiler_params=PARAMS,
        cost_estimate=cost("final"),
        name="final",
    )(*(in_vmem(a) for a in args))


def local_pair(tokens, cotangent, w_gate, w_up, w_down):
    x, g = tokens[0].T, cotangent[0].T
    x_o = shift(x, 0, True)
    g_b = shift(g, -1)
    h, z2, act2, p2, q2, x, *w = loading_first(x, (w_gate[0], w_up[0], w_down[0].T), "first_own")
    h_b = shift(h, -1)
    g_bo = shift(after(g_b, h), 0, True)
    x_o = after(x_o, g_b)
    h_o, z3, act3, p3, q3 = first(x_o, w, "first_other")
    h_bo = shift(h_o, -1)
    d_b, z0, act0, dg0, du0 = second(after(h_b, h_o), g_b, w)
    d = shift(d_b, 1)
    d_o = shift(d_b, 1, True)
    parts = second_grads(after(h_bo, d_b), g_bo, w, (z0, g_b, act0, dg0, du0))
    dx, dg2, du2 = first_back(x, after(d, parts[0]), p2, q2, w, "first_back_own")
    gg, gu, gd, dx = final(d_o, z3, act3, p3, q3, w[2], parts, dx, (d, z2, act2, dg2, du2))
    return dx.T[None], gg[None], gu[None], gd.T[None]


def many_gates(v, gate, up):
    vf = v.astype(F32)
    inverse = lax.rsqrt(jnp.mean(vf * vf, axis=-1, keepdims=True) + EPS)
    normed = vf * inverse
    zed = normed.astype(BF16)
    active, p, q = gate_values(dot(zed, gate), dot(zed, up))
    return inverse, normed, zed, active.astype(BF16), p, q


def many_back(c, saved, gate, up, down):
    inverse, normed, _, _, p, q = saved
    da = dot(c, down, ((1,), (1,)))
    dgate, dup = (da * p).astype(BF16), (da * q).astype(BF16)
    dz = dot(dgate, gate, ((1,), (1,))) + dot(dup, up, ((1,), (1,)))
    inner = jnp.mean(dz * normed, axis=-1, keepdims=True)
    return (c.astype(F32) + inverse * (dz - normed * inner)).astype(BF16), dgate, dup


def local_many(tokens, cotangent, w_gate, w_up, w_down):
    x, g = tokens[0], cotangent[0]
    gate, up, down = w_gate[0], w_up[0], w_down[0]
    g_b = shift(g, -1)
    saved = many_gates(x, gate, up)
    h = (x.astype(F32) + dot(saved[3], down)).astype(BF16)
    saved_b = many_gates(shift(h, -1), gate, up)
    d_b, dg_b, du_b = many_back(g_b, saved_b, gate, up, down)
    d = shift(d_b, 1)
    dx, dg, du = many_back(d, saved, gate, up, down)
    tn = ((0,), (0,))
    zed = jnp.concatenate([saved_b[2], saved[2]])
    parts = (
        dot(zed, jnp.concatenate([dg_b, dg]), tn),
        dot(zed, jnp.concatenate([du_b, du]), tn),
        dot(jnp.concatenate([saved_b[3], saved[3]]), jnp.concatenate([g_b, d]), tn),
    )
    gg, gu, gd = lax.psum(tuple(a.astype(BF16) for a in parts), "dp")
    return dx[None], gg[None], gu[None], gd[None]


def solution(mesh):
    rows = P("blk", "dp", None)
    blocks = P("blk", None, None)
    body = local_pair if mesh.shape["dp"] == 2 else local_many
    return jax.shard_map(
        body,
        mesh=mesh,
        in_specs=(rows, rows, blocks, blocks, blocks),
        out_specs=(rows, blocks, blocks, blocks),
        check_vma=False,
    )
```

```python
import functools

import jax
import jax.numpy as jnp
from jax import lax
from jax.experimental import pallas as pl
from jax.experimental.pallas import tpu as pltpu
from jax.sharding import PartitionSpec as P

F32 = jnp.float32
BF16 = jnp.bfloat16
EPS = 1e-05


def shift(x, by, flip=False):
    blk, dp = lax.axis_size("blk"), lax.axis_size("dp")
    pairs = []
    for i in range(blk):
        for r in range(dp):
            to = (dp - 1 - r) if flip else r
            pairs.append((i * dp + r, ((i + by) % blk) * dp + to))
    return lax.ppermute(x, ("blk", "dp"), pairs)


def dot(a, b, dims=((1,), (0,))):
    return lax.dot_general(a, b, (dims, ((), ())), preferred_element_type=F32)


NT = ((1,), (1,))


def after(x, y):
    return lax.optimization_barrier((x, y))[0]


def normalize(v):
    inverse = lax.rsqrt(jnp.mean(v * v, axis=0, keepdims=True) + EPS)
    return inverse, v * inverse


def chunks(size, step=256):
    step = step if size % step == 0 else size
    return [slice(k, k + step) for k in range(0, size, step)]


def staggered(parts, ahead, use):
    ready = ahead(parts[0])
    for k, part in enumerate(parts):
        following = ahead(parts[k + 1]) if k + 1 < len(parts) else None
        use(part, ready)
        ready = following


def gate_values(pre_g, pre_u):
    s = 0.5 * jnp.tanh(0.5 * pre_g) + 0.5
    q = pre_g * s
    p = pre_u * (s + q * (1.0 - s))
    return q * pre_u, p, q


def input_cotangent(c, dz, inverse, normed):
    inner = jnp.mean(dz * normed, axis=0, keepdims=True)
    return (c + inverse * (dz - normed * inner)).astype(BF16)


def forward_body(x_ref, gate_ref, up_ref, down_ref, h_ref, z_ref, act_ref, p_ref, q_ref, arrived):
    x = x_ref[...].astype(F32)
    _, normed = normalize(x)
    zed = normed.astype(BF16)
    z_ref[...] = zed
    zt = zed.T

    def ahead(hc):
        arrived(hc)
        return dot(zt, gate_ref[:, hc]), dot(zt, up_ref[:, hc])

    total = [x]

    def use(hc, ready):
        active, p, q = gate_values(*ready)
        active = active.astype(BF16)
        act_ref[:, hc] = active
        p_ref[:, hc] = p.astype(BF16)
        q_ref[:, hc] = q.astype(BF16)
        total[0] += dot(down_ref[:, hc], active, NT)

    staggered(chunks(gate_ref.shape[1]), ahead, use)
    h_ref[...] = total[0].astype(BF16)


def forward_kernel(*refs):
    forward_body(*refs, arrived=lambda hc: None)


def loading_forward_kernel(
    x_hbm, gate_hbm, up_hbm, down_hbm, h_ref, z_ref, act_ref, p_ref, q_ref, x_ref, gate_ref, up_ref, down_ref, sem
):
    x_copy = pltpu.make_async_copy(x_hbm, x_ref, sem.at[0])
    x_copy.start()
    copies = {}
    for k, hc in enumerate(chunks(gate_ref.shape[1])):
        copies[hc.start] = []
        for m, (src, dst) in enumerate(((gate_hbm, gate_ref), (up_hbm, up_ref), (down_hbm, down_ref))):
            copy = pltpu.make_async_copy(src.at[:, hc], dst.at[:, hc], sem.at[1 + 3 * k + m])
            copy.start()
            copies[hc.start].append(copy)
    x_copy.wait()

    def arrived(hc):
        for copy in copies[hc.start]:
            copy.wait()

    forward_body(x_ref, gate_ref, up_ref, down_ref, h_ref, z_ref, act_ref, p_ref, q_ref, arrived)


def hidden_cotangent_kernel(c_ref, down_ref, da_ref):
    ct = c_ref[...].T
    for hc in chunks(down_ref.shape[1]):
        da_ref[:, hc] = dot(ct, down_ref[:, hc])


def second_kernel(h_ref, c_ref, gate_ref, up_ref, da_ref, d_ref, z_ref, act_ref, dg_ref, du_ref):
    inverse, normed = normalize(h_ref[...].astype(F32))
    zed = normed.astype(BF16)
    z_ref[...] = zed
    zt = zed.T

    def ahead(hc):
        return dot(zt, gate_ref[:, hc]), dot(zt, up_ref[:, hc])

    def use(hc, ready):
        active, p, q = gate_values(*ready)
        act_ref[:, hc] = active.astype(BF16)
        dg_ref[:, hc] = (da_ref[:, hc] * p).astype(BF16)
        du_ref[:, hc] = (da_ref[:, hc] * q).astype(BF16)

    staggered(chunks(gate_ref.shape[1]), ahead, use)
    dz = dot(gate_ref[...], dg_ref[...], NT) + dot(up_ref[...], du_ref[...], NT)
    d_ref[...] = input_cotangent(c_ref[...].astype(F32), dz, inverse, normed)


def second_grads_kernel(
    h_ref, c_ref, gate_ref, up_ref, down_ref, z0_ref, c0_ref, act0_ref, dg0_ref, du0_ref, gg_ref, gu_ref, gd_ref
):
    _, normed = normalize(h_ref[...].astype(F32))
    zed = normed.astype(BF16)
    zt = zed.T
    ct = c_ref[...].T
    z = jnp.concatenate([z0_ref[...], zed], axis=1)
    c = jnp.concatenate([c0_ref[...], c_ref[...]], axis=1)

    def ahead(hc):
        return dot(zt, gate_ref[:, hc]), dot(zt, up_ref[:, hc]), dot(ct, down_ref[:, hc])

    def use(hc, ready):
        active, p, q = gate_values(*ready[:2])
        gd_ref[:, hc] = dot(c, stack(act0_ref[:, hc], active)).astype(BF16)
        gg_ref[:, hc] = dot(z, stack(dg0_ref[:, hc], ready[2] * p)).astype(BF16)
        gu_ref[:, hc] = dot(z, stack(du0_ref[:, hc], ready[2] * q)).astype(BF16)

    staggered(chunks(gate_ref.shape[1]), ahead, use)


def stack(above, below):
    return jnp.concatenate([above, below.astype(BF16)], axis=0)


def first_back_kernel(x_ref, c_ref, p_ref, q_ref, gate_ref, up_ref, down_ref, d_ref, dg_ref, du_ref):
    inverse, normed = normalize(x_ref[...].astype(F32))
    ct = c_ref[...].T

    def ahead(hc):
        return dot(ct, down_ref[:, hc])

    def use(hc, da):
        dg_ref[:, hc] = (da * p_ref[:, hc].astype(F32)).astype(BF16)
        du_ref[:, hc] = (da * q_ref[:, hc].astype(F32)).astype(BF16)

    staggered(chunks(gate_ref.shape[1]), ahead, use)
    dz = dot(gate_ref[...], dg_ref[...], NT) + dot(up_ref[...], du_ref[...], NT)
    d_ref[...] = input_cotangent(c_ref[...].astype(F32), dz, inverse, normed)


def final_kernel(
    c_ref, z_ref, act_ref, p_ref, q_ref, down_ref, pg_ref, pu_ref, pd_ref, dx_ref, c2_ref, z2_ref, act2_ref, dg2_ref, du2_ref,
    gg_hbm, gu_hbm, gd_hbm, dx_hbm, gg_ref, gu_ref, gd_ref, sem,
):
    copies = [pltpu.make_async_copy(dx_ref, dx_hbm, sem.at[0])]
    copies[0].start()
    ct = c_ref[...].T
    c = jnp.concatenate([c2_ref[...], c_ref[...]], axis=1)
    z = jnp.concatenate([z2_ref[...], z_ref[...]], axis=1)
    parts = chunks(gg_ref.shape[1])

    def add(hc, m, left, right, part_ref, ref, hbm):
        ref[:, hc] = (part_ref[:, hc].astype(F32) + dot(left, right)).astype(BF16)
        copy = pltpu.make_async_copy(ref.at[:, hc], hbm.at[:, hc], sem.at[1 + 3 * (hc.start // parts[0].stop) + m])
        copy.start()
        copies.append(copy)

    def ahead(hc):
        return dot(ct, down_ref[:, hc])

    def use(hc, da):
        add(hc, 2, c, stack(act2_ref[:, hc], act_ref[:, hc]), pd_ref, gd_ref, gd_hbm)
        add(hc, 0, z, stack(dg2_ref[:, hc], da * p_ref[:, hc].astype(F32)), pg_ref, gg_ref, gg_hbm)
        add(hc, 1, z, stack(du2_ref[:, hc], da * q_ref[:, hc].astype(F32)), pu_ref, gu_ref, gu_hbm)

    staggered(parts, ahead, use)
    for copy in copies:
        copy.wait()


PARAMS = pltpu.CompilerParams(vmem_limit_bytes=20 * 1024 * 1024)
COSTS = {}


def cost(name):
    return pl.CostEstimate(flops=COSTS.get(name, 10**10), bytes_accessed=3 * 10**7, transcendentals=0)


def in_vmem(x):
    return pltpu.with_memory_space_constraint(x, pltpu.VMEM)


def whole(kernel, args, out_shapes, name, kind=BF16):
    spec = pl.BlockSpec(memory_space=pltpu.VMEM)
    return pl.pallas_call(
        kernel,
        in_specs=[spec] * len(args),
        out_specs=[spec] * len(out_shapes),
        out_shape=[pltpu.VMEM(s, kind) for s in out_shapes],
        compiler_params=PARAMS,
        cost_estimate=cost(name),
        name=name,
    )(*(in_vmem(a) for a in args))


def first(x, w, name):
    d, t = x.shape
    h = w[0].shape[1]
    return whole(forward_kernel, (x, *w), [(d, t), (d, t), (t, h), (t, h), (t, h)], name)


def loading_first(x, w, name):
    d, t = x.shape
    h = w[0].shape[1]
    shapes = [(d, t), (d, t), (t, h), (t, h), (t, h), (d, t), (d, h), (d, h), (d, h)]
    return pl.pallas_call(
        loading_forward_kernel,
        in_specs=[pl.BlockSpec(memory_space=pltpu.HBM)] * 4,
        out_specs=[pl.BlockSpec(memory_space=pltpu.VMEM)] * len(shapes),
        out_shape=[pltpu.VMEM(s, BF16) for s in shapes],
        scratch_shapes=[pltpu.SemaphoreType.DMA((1 + 3 * len(chunks(h)),))],
        compiler_params=PARAMS,
        cost_estimate=cost(name),
        name=name,
    )(*(pltpu.with_memory_space_constraint(a, pltpu.HBM) for a in (x, *w)))


def hidden_cotangent(c, down):
    return whole(hidden_cotangent_kernel, (c, down), [(c.shape[1], down.shape[1])], "hidden_cotangent", F32)[0]


def second(v, c, gate, up, da):
    d, t = v.shape
    h = gate.shape[1]
    return whole(second_kernel, (v, c, gate, up, da), [(d, t), (d, t), (t, h), (t, h), (t, h)], "second_own")


def second_grads(v, c, w, own):
    d, h = w[0].shape
    return whole(second_grads_kernel, (v, c, *w, *own), [(d, h)] * 3, "second_grads")


def first_back(x, c, p, q, w, name):
    d, t = x.shape
    h = w[0].shape[1]
    return whole(first_back_kernel, (x, c, p, q, *w), [(d, t), (t, h), (t, h)], name)


def final(c, z, act, p, q, down, parts, dx, held):
    d, t = c.shape
    h = down.shape[1]
    args = (c, z, act, p, q, down, *parts, dx, *held)
    return pl.pallas_call(
        final_kernel,
        in_specs=[pl.BlockSpec(memory_space=pltpu.VMEM)] * len(args),
        out_specs=[pl.BlockSpec(memory_space=pltpu.HBM)] * 4,
        out_shape=[pltpu.HBM(s, BF16) for s in ((d, h), (d, h), (d, h), (d, t))],
        scratch_shapes=[pltpu.VMEM((d, h), BF16)] * 3 + [pltpu.SemaphoreType.DMA((1 + 3 * len(chunks(h)),))],
        compiler_params=PARAMS,
        cost_estimate=cost("final"),
        name="final",
    )(*(in_vmem(a) for a in args))


def local_pair(tokens, cotangent, w_gate, w_up, w_down):
    x, g = tokens[0].T, cotangent[0].T
    x_o = shift(x, 0, True)
    g_b = shift(g, -1)
    h, z2, act2, p2, q2, x, *w = loading_first(x, (w_gate[0], w_up[0], w_down[0].T), "first_own")
    h_b = shift(h, -1)
    g_bo = shift(after(g_b, h), 0, True)
    da_b = hidden_cotangent(after(g_b, h), w[2])
    x_o = after(x_o, da_b)
    h_o, z3, act3, p3, q3 = first(x_o, w, "first_other")
    h_bo = shift(h_o, -1)
    d_b, z0, act0, dg0, du0 = second(after(h_b, h_o), g_b, w[0], w[1], da_b)
    d = shift(d_b, 1)
    d_o = shift(d_b, 1, True)
    parts = second_grads(after(h_bo, d_b), g_bo, w, (z0, g_b, act0, dg0, du0))
    dx, dg2, du2 = first_back(x, after(d, parts[0]), p2, q2, w, "first_back_own")
    gg, gu, gd, dx = final(d_o, z3, act3, p3, q3, w[2], parts, dx, (d, z2, act2, dg2, du2))
    return dx.T[None], gg[None], gu[None], gd.T[None]


def many_gates(v, gate, up):
    vf = v.astype(F32)
    inverse = lax.rsqrt(jnp.mean(vf * vf, axis=-1, keepdims=True) + EPS)
    normed = vf * inverse
    zed = normed.astype(BF16)
    active, p, q = gate_values(dot(zed, gate), dot(zed, up))
    return inverse, normed, zed, active.astype(BF16), p, q


def many_back(c, saved, gate, up, down):
    inverse, normed, _, _, p, q = saved
    da = dot(c, down, ((1,), (1,)))
    dgate, dup = (da * p).astype(BF16), (da * q).astype(BF16)
    dz = dot(dgate, gate, ((1,), (1,))) + dot(dup, up, ((1,), (1,)))
    inner = jnp.mean(dz * normed, axis=-1, keepdims=True)
    return (c.astype(F32) + inverse * (dz - normed * inner)).astype(BF16), dgate, dup


def local_many(tokens, cotangent, w_gate, w_up, w_down):
    x, g = tokens[0], cotangent[0]
    gate, up, down = w_gate[0], w_up[0], w_down[0]
    g_b = shift(g, -1)
    saved = many_gates(x, gate, up)
    h = (x.astype(F32) + dot(saved[3], down)).astype(BF16)
    saved_b = many_gates(shift(h, -1), gate, up)
    d_b, dg_b, du_b = many_back(g_b, saved_b, gate, up, down)
    d = shift(d_b, 1)
    dx, dg, du = many_back(d, saved, gate, up, down)
    tn = ((0,), (0,))
    zed = jnp.concatenate([saved_b[2], saved[2]])
    parts = (
        dot(zed, jnp.concatenate([dg_b, dg]), tn),
        dot(zed, jnp.concatenate([du_b, du]), tn),
        dot(jnp.concatenate([saved_b[3], saved[3]]), jnp.concatenate([g_b, d]), tn),
    )
    gg, gu, gd = lax.psum(tuple(a.astype(BF16) for a in parts), "dp")
    return dx[None], gg[None], gu[None], gd[None]


def solution(mesh):
    rows = P("blk", "dp", None)
    blocks = P("blk", None, None)
    body = local_pair if mesh.shape["dp"] == 2 else local_many
    return jax.shard_map(
        body,
        mesh=mesh,
        in_specs=(rows, rows, blocks, blocks, blocks),
        out_specs=(rows, blocks, blocks, blocks),
        check_vma=False,
    )
```

```python
import functools

import jax
import jax.numpy as jnp
from jax import lax
from jax.experimental import pallas as pl
from jax.experimental.pallas import tpu as pltpu
from jax.sharding import PartitionSpec as P

F32 = jnp.float32
BF16 = jnp.bfloat16
EPS = 1e-05


def shift(x, by, flip=False):
    blk, dp = lax.axis_size("blk"), lax.axis_size("dp")
    pairs = []
    for i in range(blk):
        for r in range(dp):
            to = (dp - 1 - r) if flip else r
            pairs.append((i * dp + r, ((i + by) % blk) * dp + to))
    return lax.ppermute(x, ("blk", "dp"), pairs)


def dot(a, b, dims=((1,), (0,))):
    return lax.dot_general(a, b, (dims, ((), ())), preferred_element_type=F32)


NT = ((1,), (1,))


def after(x, y):
    return lax.optimization_barrier((x, y))[0]


def normalize(v):
    inverse = lax.rsqrt(jnp.mean(v * v, axis=0, keepdims=True) + EPS)
    return inverse, v * inverse


def chunks(size, step=256):
    step = step if size % step == 0 else size
    return [slice(k, k + step) for k in range(0, size, step)]


def staggered(parts, ahead, use):
    ready = ahead(parts[0])
    for k, part in enumerate(parts):
        following = ahead(parts[k + 1]) if k + 1 < len(parts) else None
        use(part, ready)
        ready = following


def gate_values(pre_g, pre_u):
    s = 0.5 * jnp.tanh(0.5 * pre_g) + 0.5
    q = pre_g * s
    p = pre_u * (s + q * (1.0 - s))
    return q * pre_u, p, q


def input_cotangent(c, dz, inverse, normed):
    inner = jnp.mean(dz * normed, axis=0, keepdims=True)
    return (c + inverse * (dz - normed * inner)).astype(BF16)


def forward_body(x_ref, gate_ref, up_ref, down_ref, h_ref, z_ref, act_ref, p_ref, q_ref, arrived):
    x = x_ref[...].astype(F32)
    _, normed = normalize(x)
    zed = normed.astype(BF16)
    z_ref[...] = zed
    zt = zed.T

    def ahead(hc):
        arrived(hc)
        return dot(zt, gate_ref[:, hc]), dot(zt, up_ref[:, hc])

    total = [x]

    def use(hc, ready):
        active, p, q = gate_values(*ready)
        active = active.astype(BF16)
        act_ref[:, hc] = active
        p_ref[:, hc] = p.astype(BF16)
        q_ref[:, hc] = q.astype(BF16)
        total[0] += dot(down_ref[:, hc], active, NT)

    staggered(chunks(gate_ref.shape[1]), ahead, use)
    h_ref[...] = total[0].astype(BF16)


def forward_kernel(*refs):
    forward_body(*refs, arrived=lambda hc: None)


def loading_forward_kernel(
    x_hbm, gate_hbm, up_hbm, down_hbm, h_ref, z_ref, act_ref, p_ref, q_ref, x_ref, gate_ref, up_ref, down_ref, sem
):
    x_copy = pltpu.make_async_copy(x_hbm, x_ref, sem.at[0])
    x_copy.start()
    copies = {}
    for k, hc in enumerate(chunks(gate_ref.shape[1])):
        copies[hc.start] = []
        for m, (src, dst) in enumerate(((gate_hbm, gate_ref), (up_hbm, up_ref), (down_hbm, down_ref))):
            copy = pltpu.make_async_copy(src.at[:, hc], dst.at[:, hc], sem.at[1 + 3 * k + m])
            copy.start()
            copies[hc.start].append(copy)
    x_copy.wait()

    def arrived(hc):
        for copy in copies[hc.start]:
            copy.wait()

    forward_body(x_ref, gate_ref, up_ref, down_ref, h_ref, z_ref, act_ref, p_ref, q_ref, arrived)


def hidden_cotangent_kernel(c_ref, down_ref, da_ref):
    ct = c_ref[...].T
    for hc in chunks(down_ref.shape[1]):
        da_ref[:, hc] = dot(ct, down_ref[:, hc])


def second_kernel(h_ref, c_ref, gate_ref, up_ref, da_ref, d_ref, z_ref, act_ref, dg_ref, du_ref):
    inverse, normed = normalize(h_ref[...].astype(F32))
    zed = normed.astype(BF16)
    z_ref[...] = zed
    zt = zed.T

    def ahead(hc):
        return dot(zt, gate_ref[:, hc]), dot(zt, up_ref[:, hc])

    def use(hc, ready):
        active, p, q = gate_values(*ready)
        act_ref[:, hc] = active.astype(BF16)
        dg_ref[:, hc] = (da_ref[:, hc] * p).astype(BF16)
        du_ref[:, hc] = (da_ref[:, hc] * q).astype(BF16)

    staggered(chunks(gate_ref.shape[1]), ahead, use)
    dz = dot(gate_ref[...], dg_ref[...], NT) + dot(up_ref[...], du_ref[...], NT)
    d_ref[...] = input_cotangent(c_ref[...].astype(F32), dz, inverse, normed)


def second_grads_kernel(
    h_ref, c_ref, gate_ref, up_ref, down_ref, z0_ref, c0_ref, act0_ref, dg0_ref, du0_ref, gg_ref, gu_ref, gd_ref
):
    _, normed = normalize(h_ref[...].astype(F32))
    zed = normed.astype(BF16)
    zt = zed.T
    ct = c_ref[...].T
    z = jnp.concatenate([z0_ref[...], zed], axis=1)
    c = jnp.concatenate([c0_ref[...], c_ref[...]], axis=1)

    def ahead(hc):
        return dot(zt, gate_ref[:, hc]), dot(zt, up_ref[:, hc]), dot(ct, down_ref[:, hc])

    def use(hc, ready):
        active, p, q = gate_values(*ready[:2])
        gd_ref[:, hc] = dot(c, stack(act0_ref[:, hc], active)).astype(BF16)
        gg_ref[:, hc] = dot(z, stack(dg0_ref[:, hc], ready[2] * p)).astype(BF16)
        gu_ref[:, hc] = dot(z, stack(du0_ref[:, hc], ready[2] * q)).astype(BF16)

    staggered(chunks(gate_ref.shape[1]), ahead, use)


def stack(above, below):
    return jnp.concatenate([above, below.astype(BF16)], axis=0)


def whole_tiles(tokens):
    return tokens // 256 * 256 if tokens > 256 else tokens


def first_back_kernel(
    x_ref, c_ref, p_ref, q_ref, gate_ref, up_ref, down_ref, z_ref, act_ref, pg_ref, pu_ref, pd_ref,
    d_ref, dg_ref, du_ref, gg_ref, gu_ref, gd_ref,
):
    inverse, normed = normalize(x_ref[...].astype(F32))
    ct = c_ref[...].T
    cut = whole_tiles(act_ref.shape[0])
    c = c_ref[:, :cut]
    z = z_ref[:, :cut]

    def ahead(hc):
        return dot(ct, down_ref[:, hc])

    def use(hc, da):
        dgate = (da * p_ref[:, hc].astype(F32)).astype(BF16)
        dup = (da * q_ref[:, hc].astype(F32)).astype(BF16)
        dg_ref[:, hc] = dgate
        du_ref[:, hc] = dup
        gd_ref[:, hc] = (pd_ref[:, hc].astype(F32) + dot(c, act_ref[:cut, hc])).astype(BF16)
        gg_ref[:, hc] = (pg_ref[:, hc].astype(F32) + dot(z, dgate[:cut])).astype(BF16)
        gu_ref[:, hc] = (pu_ref[:, hc].astype(F32) + dot(z, dup[:cut])).astype(BF16)

    staggered(chunks(gate_ref.shape[1]), ahead, use)
    dz = dot(gate_ref[...], dg_ref[...], NT) + dot(up_ref[...], du_ref[...], NT)
    d_ref[...] = input_cotangent(c_ref[...].astype(F32), dz, inverse, normed)


def final_kernel(
    c_ref, z_ref, act_ref, p_ref, q_ref, down_ref, pg_ref, pu_ref, pd_ref, dx_ref, c2_ref, z2_ref, act2_ref, dg2_ref, du2_ref,
    gg_hbm, gu_hbm, gd_hbm, dx_hbm, gg_ref, gu_ref, gd_ref, sem,
):
    copies = [pltpu.make_async_copy(dx_ref, dx_hbm, sem.at[0])]
    copies[0].start()
    ct = c_ref[...].T
    cut = whole_tiles(act_ref.shape[0])
    c = jnp.concatenate([c2_ref[:, cut:], c_ref[...]], axis=1)
    z = jnp.concatenate([z2_ref[:, cut:], z_ref[...]], axis=1)
    parts = chunks(gg_ref.shape[1])

    def add(hc, m, left, right, part_ref, ref, hbm):
        ref[:, hc] = (part_ref[:, hc].astype(F32) + dot(left, right)).astype(BF16)
        copy = pltpu.make_async_copy(ref.at[:, hc], hbm.at[:, hc], sem.at[1 + 3 * (hc.start // parts[0].stop) + m])
        copy.start()
        copies.append(copy)

    def ahead(hc):
        return dot(ct, down_ref[:, hc])

    def use(hc, da):
        add(hc, 2, c, stack(act2_ref[cut:, hc], act_ref[:, hc]), pd_ref, gd_ref, gd_hbm)
        add(hc, 0, z, stack(dg2_ref[cut:, hc], da * p_ref[:, hc].astype(F32)), pg_ref, gg_ref, gg_hbm)
        add(hc, 1, z, stack(du2_ref[cut:, hc], da * q_ref[:, hc].astype(F32)), pu_ref, gu_ref, gu_hbm)

    staggered(parts, ahead, use)
    for copy in copies:
        copy.wait()


PARAMS = pltpu.CompilerParams(vmem_limit_bytes=20 * 1024 * 1024)
COSTS = {}


def cost(name):
    return pl.CostEstimate(flops=COSTS.get(name, 10**10), bytes_accessed=3 * 10**7, transcendentals=0)


def in_vmem(x):
    return pltpu.with_memory_space_constraint(x, pltpu.VMEM)


def whole(kernel, args, out_shapes, name, kind=BF16):
    spec = pl.BlockSpec(memory_space=pltpu.VMEM)
    return pl.pallas_call(
        kernel,
        in_specs=[spec] * len(args),
        out_specs=[spec] * len(out_shapes),
        out_shape=[pltpu.VMEM(s, kind) for s in out_shapes],
        compiler_params=PARAMS,
        cost_estimate=cost(name),
        name=name,
    )(*(in_vmem(a) for a in args))


def first(x, w, name):
    d, t = x.shape
    h = w[0].shape[1]
    return whole(forward_kernel, (x, *w), [(d, t), (d, t), (t, h), (t, h), (t, h)], name)


def loading_first(x, w, name):
    d, t = x.shape
    h = w[0].shape[1]
    shapes = [(d, t), (d, t), (t, h), (t, h), (t, h), (d, t), (d, h), (d, h), (d, h)]
    return pl.pallas_call(
        loading_forward_kernel,
        in_specs=[pl.BlockSpec(memory_space=pltpu.HBM)] * 4,
        out_specs=[pl.BlockSpec(memory_space=pltpu.VMEM)] * len(shapes),
        out_shape=[pltpu.VMEM(s, BF16) for s in shapes],
        scratch_shapes=[pltpu.SemaphoreType.DMA((1 + 3 * len(chunks(h)),))],
        compiler_params=PARAMS,
        cost_estimate=cost(name),
        name=name,
    )(*(pltpu.with_memory_space_constraint(a, pltpu.HBM) for a in (x, *w)))


def hidden_cotangent(c, down):
    return whole(hidden_cotangent_kernel, (c, down), [(c.shape[1], down.shape[1])], "hidden_cotangent", F32)[0]


def second(v, c, gate, up, da):
    d, t = v.shape
    h = gate.shape[1]
    return whole(second_kernel, (v, c, gate, up, da), [(d, t), (d, t), (t, h), (t, h), (t, h)], "second_own")


def second_grads(v, c, w, own):
    d, h = w[0].shape
    return whole(second_grads_kernel, (v, c, *w, *own), [(d, h)] * 3, "second_grads")


def first_back(x, c, p, q, w, z, act, parts):
    d, t = x.shape
    h = w[0].shape[1]
    shapes = [(d, t), (t, h), (t, h)] + [(d, h)] * 3
    return whole(first_back_kernel, (x, c, p, q, *w, z, act, *parts), shapes, "first_back_own")


def final(c, z, act, p, q, down, parts, dx, held):
    d, t = c.shape
    h = down.shape[1]
    args = (c, z, act, p, q, down, *parts, dx, *held)
    return pl.pallas_call(
        final_kernel,
        in_specs=[pl.BlockSpec(memory_space=pltpu.VMEM)] * len(args),
        out_specs=[pl.BlockSpec(memory_space=pltpu.HBM)] * 4,
        out_shape=[pltpu.HBM(s, BF16) for s in ((d, h), (d, h), (d, h), (d, t))],
        scratch_shapes=[pltpu.VMEM((d, h), BF16)] * 3 + [pltpu.SemaphoreType.DMA((1 + 3 * len(chunks(h)),))],
        compiler_params=PARAMS,
        cost_estimate=cost("final"),
        name="final",
    )(*(in_vmem(a) for a in args))


def local_pair(tokens, cotangent, w_gate, w_up, w_down):
    x, g = tokens[0].T, cotangent[0].T
    x_o = shift(x, 0, True)
    g_b = shift(g, -1)
    h, z2, act2, p2, q2, x, *w = loading_first(x, (w_gate[0], w_up[0], w_down[0].T), "first_own")
    h_b = shift(h, -1)
    g_bo = shift(after(g_b, h), 0, True)
    da_b = hidden_cotangent(after(g_b, h), w[2])
    x_o = after(x_o, da_b)
    h_o, z3, act3, p3, q3 = first(x_o, w, "first_other")
    h_bo = shift(h_o, -1)
    d_b, z0, act0, dg0, du0 = second(after(h_b, h_o), g_b, w[0], w[1], da_b)
    d = shift(d_b, 1)
    d_o = shift(d_b, 1, True)
    parts = second_grads(after(h_bo, d_b), g_bo, w, (z0, g_b, act0, dg0, du0))
    dx, dg2, du2, *parts = first_back(x, d, p2, q2, w, z2, act2, parts)
    gg, gu, gd, dx = final(d_o, z3, act3, p3, q3, w[2], parts, dx, (d, z2, act2, dg2, du2))
    return dx.T[None], gg[None], gu[None], gd.T[None]


def many_gates(v, gate, up):
    vf = v.astype(F32)
    inverse = lax.rsqrt(jnp.mean(vf * vf, axis=-1, keepdims=True) + EPS)
    normed = vf * inverse
    zed = normed.astype(BF16)
    active, p, q = gate_values(dot(zed, gate), dot(zed, up))
    return inverse, normed, zed, active.astype(BF16), p, q


def many_back(c, saved, gate, up, down):
    inverse, normed, _, _, p, q = saved
    da = dot(c, down, ((1,), (1,)))
    dgate, dup = (da * p).astype(BF16), (da * q).astype(BF16)
    dz = dot(dgate, gate, ((1,), (1,))) + dot(dup, up, ((1,), (1,)))
    inner = jnp.mean(dz * normed, axis=-1, keepdims=True)
    return (c.astype(F32) + inverse * (dz - normed * inner)).astype(BF16), dgate, dup


def local_many(tokens, cotangent, w_gate, w_up, w_down):
    x, g = tokens[0], cotangent[0]
    gate, up, down = w_gate[0], w_up[0], w_down[0]
    g_b = shift(g, -1)
    saved = many_gates(x, gate, up)
    h = (x.astype(F32) + dot(saved[3], down)).astype(BF16)
    saved_b = many_gates(shift(h, -1), gate, up)
    d_b, dg_b, du_b = many_back(g_b, saved_b, gate, up, down)
    d = shift(d_b, 1)
    dx, dg, du = many_back(d, saved, gate, up, down)
    tn = ((0,), (0,))
    zed = jnp.concatenate([saved_b[2], saved[2]])
    parts = (
        dot(zed, jnp.concatenate([dg_b, dg]), tn),
        dot(zed, jnp.concatenate([du_b, du]), tn),
        dot(jnp.concatenate([saved_b[3], saved[3]]), jnp.concatenate([g_b, d]), tn),
    )
    gg, gu, gd = lax.psum(tuple(a.astype(BF16) for a in parts), "dp")
    return dx[None], gg[None], gu[None], gd[None]


def solution(mesh):
    rows = P("blk", "dp", None)
    blocks = P("blk", None, None)
    body = local_pair if mesh.shape["dp"] == 2 else local_many
    return jax.shard_map(
        body,
        mesh=mesh,
        in_specs=(rows, rows, blocks, blocks, blocks),
        out_specs=(rows, blocks, blocks, blocks),
        check_vma=False,
    )
```

```python
import functools

import jax
import jax.numpy as jnp
from jax import lax
from jax.experimental import pallas as pl
from jax.experimental.pallas import tpu as pltpu
from jax.sharding import PartitionSpec as P

F32 = jnp.float32
BF16 = jnp.bfloat16
EPS = 1e-05


def shift(x, by, flip=False):
    blk, dp = lax.axis_size("blk"), lax.axis_size("dp")
    pairs = []
    for i in range(blk):
        for r in range(dp):
            to = (dp - 1 - r) if flip else r
            pairs.append((i * dp + r, ((i + by) % blk) * dp + to))
    return lax.ppermute(x, ("blk", "dp"), pairs)


def dot(a, b, dims=((1,), (0,))):
    return lax.dot_general(a, b, (dims, ((), ())), preferred_element_type=F32)


NT = ((1,), (1,))


def after(x, y):
    return lax.optimization_barrier((x, y))[0]


def normalize(v):
    inverse = lax.rsqrt(jnp.mean(v * v, axis=0, keepdims=True) + EPS)
    return inverse, v * inverse


def chunks(size, step=256):
    step = step if size % step == 0 else size
    return [slice(k, k + step) for k in range(0, size, step)]


def staggered(parts, ahead, use):
    ready = ahead(parts[0])
    for k, part in enumerate(parts):
        following = ahead(parts[k + 1]) if k + 1 < len(parts) else None
        use(part, ready)
        ready = following


def gate_values(pre_g, pre_u):
    s = 0.5 * jnp.tanh(0.5 * pre_g) + 0.5
    q = pre_g * s
    p = pre_u * (s + q * (1.0 - s))
    return q * pre_u, p, q


def input_cotangent(c, dz, inverse, normed):
    inner = jnp.mean(dz * normed, axis=0, keepdims=True)
    return (c + inverse * (dz - normed * inner)).astype(BF16)


def forward_body(x_ref, gate_ref, up_ref, down_ref, h_ref, z_ref, act_ref, p_ref, q_ref, arrived):
    x = x_ref[...].astype(F32)
    _, normed = normalize(x)
    zed = normed.astype(BF16)
    z_ref[...] = zed
    zt = zed.T

    def ahead(hc):
        arrived(hc)
        return dot(zt, gate_ref[:, hc]), dot(zt, up_ref[:, hc])

    total = [x]

    def use(hc, ready):
        active, p, q = gate_values(*ready)
        active = active.astype(BF16)
        act_ref[:, hc] = active
        p_ref[:, hc] = p.astype(BF16)
        q_ref[:, hc] = q.astype(BF16)
        total[0] += dot(down_ref[:, hc], active, NT)

    staggered(chunks(gate_ref.shape[1]), ahead, use)
    h_ref[...] = total[0].astype(BF16)


def forward_kernel(*refs):
    forward_body(*refs, arrived=lambda hc: None)


def loading_forward_kernel(
    x_hbm, gate_hbm, up_hbm, down_hbm, h_ref, z_ref, act_ref, p_ref, q_ref, x_ref, gate_ref, up_ref, down_ref, sem
):
    x_copy = pltpu.make_async_copy(x_hbm, x_ref, sem.at[0])
    x_copy.start()
    copies = {}
    for k, hc in enumerate(chunks(gate_ref.shape[1])):
        copies[hc.start] = []
        for m, (src, dst) in enumerate(((gate_hbm, gate_ref), (up_hbm, up_ref), (down_hbm, down_ref))):
            copy = pltpu.make_async_copy(src.at[:, hc], dst.at[:, hc], sem.at[1 + 3 * k + m])
            copy.start()
            copies[hc.start].append(copy)
    x_copy.wait()

    def arrived(hc):
        for copy in copies[hc.start]:
            copy.wait()

    forward_body(x_ref, gate_ref, up_ref, down_ref, h_ref, z_ref, act_ref, p_ref, q_ref, arrived)


def hidden_cotangent_kernel(c_ref, down_ref, da_ref):
    ct = c_ref[...].T
    for hc in chunks(down_ref.shape[1]):
        da_ref[:, hc] = dot(ct, down_ref[:, hc])


def second_kernel(h_ref, c_ref, gate_ref, up_ref, da_ref, d_ref, z_ref, act_ref, dg_ref, du_ref):
    inverse, normed = normalize(h_ref[...].astype(F32))
    zed = normed.astype(BF16)
    z_ref[...] = zed
    zt = zed.T

    def ahead(hc):
        return dot(zt, gate_ref[:, hc]), dot(zt, up_ref[:, hc])

    def use(hc, ready):
        active, p, q = gate_values(*ready)
        act_ref[:, hc] = active.astype(BF16)
        dg_ref[:, hc] = (da_ref[:, hc] * p).astype(BF16)
        du_ref[:, hc] = (da_ref[:, hc] * q).astype(BF16)

    staggered(chunks(gate_ref.shape[1]), ahead, use)
    dz = dot(gate_ref[...], dg_ref[...], NT) + dot(up_ref[...], du_ref[...], NT)
    d_ref[...] = input_cotangent(c_ref[...].astype(F32), dz, inverse, normed)


def second_grads_kernel(
    h_ref, c_ref, gate_ref, up_ref, down_ref, z0_ref, c0_ref, act0_ref, dg0_ref, du0_ref, gg_ref, gu_ref, gd_ref
):
    _, normed = normalize(h_ref[...].astype(F32))
    zed = normed.astype(BF16)
    zt = zed.T
    ct = c_ref[...].T
    z = jnp.concatenate([z0_ref[...], zed], axis=1)
    c = jnp.concatenate([c0_ref[...], c_ref[...]], axis=1)

    def ahead(hc):
        return dot(zt, gate_ref[:, hc]), dot(zt, up_ref[:, hc]), dot(ct, down_ref[:, hc])

    def use(hc, ready):
        active, p, q = gate_values(*ready[:2])
        gd_ref[:, hc] = dot(c, stack(act0_ref[:, hc], active)).astype(BF16)
        gg_ref[:, hc] = dot(z, stack(dg0_ref[:, hc], ready[2] * p)).astype(BF16)
        gu_ref[:, hc] = dot(z, stack(du0_ref[:, hc], ready[2] * q)).astype(BF16)

    staggered(chunks(gate_ref.shape[1]), ahead, use)


def stack(above, below):
    return jnp.concatenate([above, below.astype(BF16)], axis=0)


def whole_tiles(tokens):
    return tokens // 256 * 256 if tokens > 256 else tokens


def first_back_kernel(
    x_ref, c_ref, p_ref, q_ref, gate_ref, up_ref, down_ref, z_ref, act_ref, pg_ref, pu_ref, pd_ref,
    d_ref, dg_ref, du_ref, gg_ref, gu_ref, gd_ref,
):
    inverse, normed = normalize(x_ref[...].astype(F32))
    ct = c_ref[...].T
    cut = whole_tiles(act_ref.shape[0])
    c = c_ref[:, :cut]
    z = z_ref[:, :cut]

    def ahead(hc):
        return dot(ct, down_ref[:, hc])

    def use(hc, da):
        dgate = (da * p_ref[:, hc].astype(F32)).astype(BF16)
        dup = (da * q_ref[:, hc].astype(F32)).astype(BF16)
        dg_ref[:, hc] = dgate
        du_ref[:, hc] = dup
        gd_ref[:, hc] = (pd_ref[:, hc].astype(F32) + dot(c, act_ref[:cut, hc])).astype(BF16)
        gg_ref[:, hc] = (pg_ref[:, hc].astype(F32) + dot(z, dgate[:cut])).astype(BF16)
        gu_ref[:, hc] = (pu_ref[:, hc].astype(F32) + dot(z, dup[:cut])).astype(BF16)

    staggered(chunks(gate_ref.shape[1]), ahead, use)
    dz = dot(gate_ref[...], dg_ref[...], NT) + dot(up_ref[...], du_ref[...], NT)
    d_ref[...] = input_cotangent(c_ref[...].astype(F32), dz, inverse, normed)


def final_kernel(
    c_ref, z_ref, act_ref, p_ref, q_ref, down_ref, pg_ref, pu_ref, pd_ref, dx_ref, c2_ref, z2_ref, act2_ref, dg2_ref, du2_ref,
    gg_hbm, gu_hbm, gd_hbm, dx_hbm, gg_ref, gu_ref, gd_ref, sem,
):
    copies = [pltpu.make_async_copy(dx_ref, dx_hbm, sem.at[0])]
    copies[0].start()
    ct = c_ref[...].T
    cut = whole_tiles(act_ref.shape[0])
    c = jnp.concatenate([c2_ref[:, cut:], c_ref[...]], axis=1)
    z = jnp.concatenate([z2_ref[:, cut:], z_ref[...]], axis=1)
    parts = chunks(gg_ref.shape[1])

    def add(hc, m, left, right, part_ref, ref, hbm):
        ref[:, hc] = (part_ref[:, hc].astype(F32) + dot(left, right)).astype(BF16)
        copy = pltpu.make_async_copy(ref.at[:, hc], hbm.at[:, hc], sem.at[1 + 3 * (hc.start // parts[0].stop) + m])
        copy.start()
        copies.append(copy)

    def ahead(hc):
        return dot(ct, down_ref[:, hc])

    def use(hc, da):
        add(hc, 2, c, stack(act2_ref[cut:, hc], act_ref[:, hc]), pd_ref, gd_ref, gd_hbm)
        add(hc, 0, z, stack(dg2_ref[cut:, hc], da * p_ref[:, hc].astype(F32)), pg_ref, gg_ref, gg_hbm)
        add(hc, 1, z, stack(du2_ref[cut:, hc], da * q_ref[:, hc].astype(F32)), pu_ref, gu_ref, gu_hbm)

    staggered(parts, ahead, use)
    for copy in copies:
        copy.wait()


PARAMS = pltpu.CompilerParams(vmem_limit_bytes=20 * 1024 * 1024)
COSTS = {}


def cost(name):
    return pl.CostEstimate(flops=COSTS.get(name, 10**10), bytes_accessed=3 * 10**7, transcendentals=0)


def in_vmem(x):
    return pltpu.with_memory_space_constraint(x, pltpu.VMEM)


def whole(kernel, args, out_shapes, name, kind=BF16):
    spec = pl.BlockSpec(memory_space=pltpu.VMEM)
    return pl.pallas_call(
        kernel,
        in_specs=[spec] * len(args),
        out_specs=[spec] * len(out_shapes),
        out_shape=[pltpu.VMEM(s, kind) for s in out_shapes],
        compiler_params=PARAMS,
        cost_estimate=cost(name),
        name=name,
    )(*(in_vmem(a) for a in args))


def first(x, w, name):
    d, t = x.shape
    h = w[0].shape[1]
    return whole(forward_kernel, (x, *w), [(d, t), (d, t), (t, h), (t, h), (t, h)], name)


def loading_first(x, w, name):
    d, t = x.shape
    h = w[0].shape[1]
    shapes = [(d, t), (d, t), (t, h), (t, h), (t, h), (d, t), (d, h), (d, h), (d, h)]
    return pl.pallas_call(
        loading_forward_kernel,
        in_specs=[pl.BlockSpec(memory_space=pltpu.HBM)] * 4,
        out_specs=[pl.BlockSpec(memory_space=pltpu.VMEM)] * len(shapes),
        out_shape=[pltpu.VMEM(s, BF16) for s in shapes],
        scratch_shapes=[pltpu.SemaphoreType.DMA((1 + 3 * len(chunks(h)),))],
        compiler_params=PARAMS,
        cost_estimate=cost(name),
        name=name,
    )(*(pltpu.with_memory_space_constraint(a, pltpu.HBM) for a in (x, *w)))


def hidden_cotangent(c, down):
    return whole(hidden_cotangent_kernel, (c, down), [(c.shape[1], down.shape[1])], "hidden_cotangent", F32)[0]


def second(v, c, gate, up, da):
    d, t = v.shape
    h = gate.shape[1]
    return whole(second_kernel, (v, c, gate, up, da), [(d, t), (d, t), (t, h), (t, h), (t, h)], "second_own")


def second_grads(v, c, w, own):
    d, h = w[0].shape
    return whole(second_grads_kernel, (v, c, *w, *own), [(d, h)] * 3, "second_grads")


def first_back(x, c, p, q, w, z, act, parts):
    d, t = x.shape
    h = w[0].shape[1]
    shapes = [(d, t), (t, h), (t, h)] + [(d, h)] * 3
    return whole(first_back_kernel, (x, c, p, q, *w, z, act, *parts), shapes, "first_back_own")


def final(c, z, act, p, q, down, parts, dx, held):
    d, t = c.shape
    h = down.shape[1]
    args = (c, z, act, p, q, down, *parts, dx, *held)
    return pl.pallas_call(
        final_kernel,
        in_specs=[pl.BlockSpec(memory_space=pltpu.VMEM)] * len(args),
        out_specs=[pl.BlockSpec(memory_space=pltpu.HBM)] * 4,
        out_shape=[pltpu.HBM(s, BF16) for s in ((d, h), (d, h), (d, h), (d, t))],
        scratch_shapes=[pltpu.VMEM((d, h), BF16)] * 3 + [pltpu.SemaphoreType.DMA((1 + 3 * len(chunks(h)),))],
        compiler_params=PARAMS,
        cost_estimate=cost("final"),
        name="final",
    )(*(in_vmem(a) for a in args))


def local_pair(tokens, cotangent, w_gate, w_up, w_down):
    x, g = tokens[0].T, cotangent[0].T
    x_o = shift(x, 0, True)
    g_b = shift(g, -1)
    h, z2, act2, p2, q2, x, *w = loading_first(x, (w_gate[0], w_up[0], w_down[0].T), "first_own")
    h_b = shift(h, -1)
    g_bo = shift(after(g, h), -1, True)
    da_b = hidden_cotangent(after(g_b, h), w[2])
    x_o = after(x_o, da_b)
    h_o, z3, act3, p3, q3 = first(x_o, w, "first_other")
    h_bo = shift(h_o, -1)
    d_b, z0, act0, dg0, du0 = second(after(h_b, h_o), g_b, w[0], w[1], da_b)
    d = shift(d_b, 1)
    d_o = shift(d_b, 1, True)
    parts = second_grads(after(h_bo, d_b), g_bo, w, (z0, g_b, act0, dg0, du0))
    dx, dg2, du2, *parts = first_back(x, d, p2, q2, w, z2, act2, parts)
    gg, gu, gd, dx = final(d_o, z3, act3, p3, q3, w[2], parts, dx, (d, z2, act2, dg2, du2))
    return dx.T[None], gg[None], gu[None], gd.T[None]


def many_gates(v, gate, up):
    vf = v.astype(F32)
    inverse = lax.rsqrt(jnp.mean(vf * vf, axis=-1, keepdims=True) + EPS)
    normed = vf * inverse
    zed = normed.astype(BF16)
    active, p, q = gate_values(dot(zed, gate), dot(zed, up))
    return inverse, normed, zed, active.astype(BF16), p, q


def many_back(c, saved, gate, up, down):
    inverse, normed, _, _, p, q = saved
    da = dot(c, down, ((1,), (1,)))
    dgate, dup = (da * p).astype(BF16), (da * q).astype(BF16)
    dz = dot(dgate, gate, ((1,), (1,))) + dot(dup, up, ((1,), (1,)))
    inner = jnp.mean(dz * normed, axis=-1, keepdims=True)
    return (c.astype(F32) + inverse * (dz - normed * inner)).astype(BF16), dgate, dup


def local_many(tokens, cotangent, w_gate, w_up, w_down):
    x, g = tokens[0], cotangent[0]
    gate, up, down = w_gate[0], w_up[0], w_down[0]
    g_b = shift(g, -1)
    saved = many_gates(x, gate, up)
    h = (x.astype(F32) + dot(saved[3], down)).astype(BF16)
    saved_b = many_gates(shift(h, -1), gate, up)
    d_b, dg_b, du_b = many_back(g_b, saved_b, gate, up, down)
    d = shift(d_b, 1)
    dx, dg, du = many_back(d, saved, gate, up, down)
    tn = ((0,), (0,))
    zed = jnp.concatenate([saved_b[2], saved[2]])
    parts = (
        dot(zed, jnp.concatenate([dg_b, dg]), tn),
        dot(zed, jnp.concatenate([du_b, du]), tn),
        dot(jnp.concatenate([saved_b[3], saved[3]]), jnp.concatenate([g_b, d]), tn),
    )
    gg, gu, gd = lax.psum(tuple(a.astype(BF16) for a in parts), "dp")
    return dx[None], gg[None], gu[None], gd[None]


def solution(mesh):
    rows = P("blk", "dp", None)
    blocks = P("blk", None, None)
    body = local_pair if mesh.shape["dp"] == 2 else local_many
    return jax.shard_map(
        body,
        mesh=mesh,
        in_specs=(rows, rows, blocks, blocks, blocks),
        out_specs=(rows, blocks, blocks, blocks),
        check_vma=False,
    )
```

```python
import functools

import jax
import jax.numpy as jnp
from jax import lax
from jax.experimental import pallas as pl
from jax.experimental.pallas import tpu as pltpu
from jax.sharding import PartitionSpec as P

F32 = jnp.float32
BF16 = jnp.bfloat16
EPS = 1e-05


def shift(x, by, flip=False):
    blk, dp = lax.axis_size("blk"), lax.axis_size("dp")
    pairs = []
    for i in range(blk):
        for r in range(dp):
            to = (dp - 1 - r) if flip else r
            pairs.append((i * dp + r, ((i + by) % blk) * dp + to))
    return lax.ppermute(x, ("blk", "dp"), pairs)


def dot(a, b, dims=((1,), (0,))):
    return lax.dot_general(a, b, (dims, ((), ())), preferred_element_type=F32)


NT = ((1,), (1,))


def after(x, y):
    return lax.optimization_barrier((x, y))[0]


def normalize(v):
    inverse = lax.rsqrt(jnp.mean(v * v, axis=0, keepdims=True) + EPS)
    return inverse, v * inverse


def chunks(size, step=256):
    step = step if size % step == 0 else size
    return [slice(k, k + step) for k in range(0, size, step)]


def staggered(parts, ahead, use):
    ready = ahead(parts[0])
    for k, part in enumerate(parts):
        following = ahead(parts[k + 1]) if k + 1 < len(parts) else None
        use(part, ready)
        ready = following


def gate_values(pre_g, pre_u):
    s = 0.5 * jnp.tanh(0.5 * pre_g) + 0.5
    q = pre_g * s
    p = pre_u * (s + q * (1.0 - s))
    return q * pre_u, p, q


def input_cotangent(c, dz, inverse, normed):
    inner = jnp.mean(dz * normed, axis=0, keepdims=True)
    return (c + inverse * (dz - normed * inner)).astype(BF16)


def forward_body(x_ref, gate_ref, up_ref, down_ref, h_ref, z_ref, act_ref, p_ref, q_ref, arrived):
    x = x_ref[...].astype(F32)
    _, normed = normalize(x)
    zed = normed.astype(BF16)
    z_ref[...] = zed
    zt = zed.T

    def ahead(hc):
        arrived(hc)
        return dot(zt, gate_ref[:, hc]), dot(zt, up_ref[:, hc])

    total = [x]

    def use(hc, ready):
        active, p, q = gate_values(*ready)
        active = active.astype(BF16)
        act_ref[:, hc] = active
        p_ref[:, hc] = p.astype(BF16)
        q_ref[:, hc] = q.astype(BF16)
        total[0] += dot(down_ref[:, hc], active, NT)

    staggered(chunks(gate_ref.shape[1]), ahead, use)
    h_ref[...] = total[0].astype(BF16)


def forward_kernel(*refs):
    forward_body(*refs, arrived=lambda hc: None)


def loading_forward_kernel(
    x_hbm, gate_hbm, up_hbm, down_hbm, h_ref, z_ref, act_ref, p_ref, q_ref, x_ref, gate_ref, up_ref, down_ref, sem
):
    x_copy = pltpu.make_async_copy(x_hbm, x_ref, sem.at[0])
    x_copy.start()
    copies = {}
    for k, hc in enumerate(chunks(gate_ref.shape[1])):
        copies[hc.start] = []
        for m, (src, dst) in enumerate(((gate_hbm, gate_ref), (up_hbm, up_ref), (down_hbm, down_ref))):
            copy = pltpu.make_async_copy(src.at[:, hc], dst.at[:, hc], sem.at[1 + 3 * k + m])
            copy.start()
            copies[hc.start].append(copy)
    x_copy.wait()

    def arrived(hc):
        for copy in copies[hc.start]:
            copy.wait()

    forward_body(x_ref, gate_ref, up_ref, down_ref, h_ref, z_ref, act_ref, p_ref, q_ref, arrived)


def hidden_cotangent_kernel(c_ref, down_ref, da_ref):
    ct = c_ref[...].T
    for hc in chunks(down_ref.shape[1]):
        da_ref[:, hc] = dot(ct, down_ref[:, hc])


def second_kernel(h_ref, c_ref, gate_ref, up_ref, da_ref, d_lo_ref, d_hi_ref, z_ref, act_ref, dg_ref, du_ref):
    inverse, normed = normalize(h_ref[...].astype(F32))
    zed = normed.astype(BF16)
    z_ref[...] = zed
    zt = zed.T

    def ahead(hc):
        return dot(zt, gate_ref[:, hc]), dot(zt, up_ref[:, hc])

    def use(hc, ready):
        active, p, q = gate_values(*ready)
        act_ref[:, hc] = active.astype(BF16)
        dg_ref[:, hc] = (da_ref[:, hc] * p).astype(BF16)
        du_ref[:, hc] = (da_ref[:, hc] * q).astype(BF16)

    staggered(chunks(gate_ref.shape[1]), ahead, use)
    dz = dot(gate_ref[...], dg_ref[...], NT) + dot(up_ref[...], du_ref[...], NT)
    d = input_cotangent(c_ref[...].astype(F32), dz, inverse, normed)
    half = d_lo_ref.shape[0]
    d_lo_ref[...] = d[:half]
    d_hi_ref[...] = d[half:]


def second_grads_kernel(
    h_ref, c_ref, gate_ref, up_ref, down_ref, z0_ref, c0_ref, act0_ref, dg0_ref, du0_ref, gg_ref, gu_ref, gd_ref
):
    _, normed = normalize(h_ref[...].astype(F32))
    zed = normed.astype(BF16)
    zt = zed.T
    ct = c_ref[...].T
    z = jnp.concatenate([z0_ref[...], zed], axis=1)
    c = jnp.concatenate([c0_ref[...], c_ref[...]], axis=1)

    def ahead(hc):
        return dot(zt, gate_ref[:, hc]), dot(zt, up_ref[:, hc]), dot(ct, down_ref[:, hc])

    def use(hc, ready):
        active, p, q = gate_values(*ready[:2])
        gd_ref[:, hc] = dot(c, stack(act0_ref[:, hc], active)).astype(BF16)
        gg_ref[:, hc] = dot(z, stack(dg0_ref[:, hc], ready[2] * p)).astype(BF16)
        gu_ref[:, hc] = dot(z, stack(du0_ref[:, hc], ready[2] * q)).astype(BF16)

    staggered(chunks(gate_ref.shape[1]), ahead, use)


def stack(above, below):
    return jnp.concatenate([above, below.astype(BF16)], axis=0)


def whole_tiles(tokens):
    return tokens // 256 * 256 if tokens > 256 else tokens


def first_back_kernel(
    x_ref, c_lo_ref, c_hi_ref, p_ref, q_ref, gate_ref, up_ref, down_ref, z_ref, act_ref, pg_ref, pu_ref, pd_ref,
    d_ref, dg_ref, du_ref, gg_ref, gu_ref, gd_ref,
):
    inverse, normed = normalize(x_ref[...].astype(F32))
    whole_c = jnp.concatenate([c_lo_ref[...], c_hi_ref[...]], axis=0)
    ct = whole_c.T
    cut = whole_tiles(act_ref.shape[0])
    c = whole_c[:, :cut]
    z = z_ref[:, :cut]

    def ahead(hc):
        return dot(ct, down_ref[:, hc])

    def use(hc, da):
        dgate = (da * p_ref[:, hc].astype(F32)).astype(BF16)
        dup = (da * q_ref[:, hc].astype(F32)).astype(BF16)
        dg_ref[:, hc] = dgate
        du_ref[:, hc] = dup
        gd_ref[:, hc] = (pd_ref[:, hc].astype(F32) + dot(c, act_ref[:cut, hc])).astype(BF16)
        gg_ref[:, hc] = (pg_ref[:, hc].astype(F32) + dot(z, dgate[:cut])).astype(BF16)
        gu_ref[:, hc] = (pu_ref[:, hc].astype(F32) + dot(z, dup[:cut])).astype(BF16)

    staggered(chunks(gate_ref.shape[1]), ahead, use)
    dz = dot(gate_ref[...], dg_ref[...], NT) + dot(up_ref[...], du_ref[...], NT)
    d_ref[...] = input_cotangent(whole_c.astype(F32), dz, inverse, normed)


def final_kernel(
    c_lo_ref, c_hi_ref, z_ref, act_ref, p_ref, q_ref, down_ref, pg_ref, pu_ref, pd_ref, dx_ref, c2_lo_ref, c2_hi_ref, z2_ref, act2_ref, dg2_ref, du2_ref,
    gg_hbm, gu_hbm, gd_hbm, dx_hbm, gg_ref, gu_ref, gd_ref, sem,
):
    copies = [pltpu.make_async_copy(dx_ref, dx_hbm, sem.at[0])]
    copies[0].start()
    whole_c = jnp.concatenate([c_lo_ref[...], c_hi_ref[...]], axis=0)
    ct = whole_c.T
    cut = whole_tiles(act_ref.shape[0])
    c2 = jnp.concatenate([c2_lo_ref[:, cut:], c2_hi_ref[:, cut:]], axis=0)
    c = jnp.concatenate([c2, whole_c], axis=1)
    z = jnp.concatenate([z2_ref[:, cut:], z_ref[...]], axis=1)
    parts = chunks(gg_ref.shape[1])

    def add(hc, m, left, right, part_ref, ref, hbm):
        ref[:, hc] = (part_ref[:, hc].astype(F32) + dot(left, right)).astype(BF16)
        copy = pltpu.make_async_copy(ref.at[:, hc], hbm.at[:, hc], sem.at[1 + 3 * (hc.start // parts[0].stop) + m])
        copy.start()
        copies.append(copy)

    def ahead(hc):
        return dot(ct, down_ref[:, hc])

    def use(hc, da):
        add(hc, 2, c, stack(act2_ref[cut:, hc], act_ref[:, hc]), pd_ref, gd_ref, gd_hbm)
        add(hc, 0, z, stack(dg2_ref[cut:, hc], da * p_ref[:, hc].astype(F32)), pg_ref, gg_ref, gg_hbm)
        add(hc, 1, z, stack(du2_ref[cut:, hc], da * q_ref[:, hc].astype(F32)), pu_ref, gu_ref, gu_hbm)

    staggered(parts, ahead, use)
    for copy in copies:
        copy.wait()


PARAMS = pltpu.CompilerParams(vmem_limit_bytes=20 * 1024 * 1024)
COSTS = {}


def cost(name):
    return pl.CostEstimate(flops=COSTS.get(name, 10**10), bytes_accessed=3 * 10**7, transcendentals=0)


def in_vmem(x):
    return pltpu.with_memory_space_constraint(x, pltpu.VMEM)


def whole(kernel, args, out_shapes, name, kind=BF16):
    spec = pl.BlockSpec(memory_space=pltpu.VMEM)
    return pl.pallas_call(
        kernel,
        in_specs=[spec] * len(args),
        out_specs=[spec] * len(out_shapes),
        out_shape=[pltpu.VMEM(s, kind) for s in out_shapes],
        compiler_params=PARAMS,
        cost_estimate=cost(name),
        name=name,
    )(*(in_vmem(a) for a in args))


def first(x, w, name):
    d, t = x.shape
    h = w[0].shape[1]
    return whole(forward_kernel, (x, *w), [(d, t), (d, t), (t, h), (t, h), (t, h)], name)


def loading_first(x, w, name):
    d, t = x.shape
    h = w[0].shape[1]
    shapes = [(d, t), (d, t), (t, h), (t, h), (t, h), (d, t), (d, h), (d, h), (d, h)]
    return pl.pallas_call(
        loading_forward_kernel,
        in_specs=[pl.BlockSpec(memory_space=pltpu.HBM)] * 4,
        out_specs=[pl.BlockSpec(memory_space=pltpu.VMEM)] * len(shapes),
        out_shape=[pltpu.VMEM(s, BF16) for s in shapes],
        scratch_shapes=[pltpu.SemaphoreType.DMA((1 + 3 * len(chunks(h)),))],
        compiler_params=PARAMS,
        cost_estimate=cost(name),
        name=name,
    )(*(pltpu.with_memory_space_constraint(a, pltpu.HBM) for a in (x, *w)))


def hidden_cotangent(c, down):
    return whole(hidden_cotangent_kernel, (c, down), [(c.shape[1], down.shape[1])], "hidden_cotangent", F32)[0]


def second(v, c, gate, up, da):
    d, t = v.shape
    h = gate.shape[1]
    shapes = [(d // 2, t), (d - d // 2, t), (d, t), (t, h), (t, h), (t, h)]
    return whole(second_kernel, (v, c, gate, up, da), shapes, "second_own")


def second_grads(v, c, w, own):
    d, h = w[0].shape
    return whole(second_grads_kernel, (v, c, *w, *own), [(d, h)] * 3, "second_grads")


def first_back(x, c, p, q, w, z, act, parts):
    d, t = x.shape
    h = w[0].shape[1]
    shapes = [(d, t), (t, h), (t, h)] + [(d, h)] * 3
    return whole(first_back_kernel, (x, *c, p, q, *w, z, act, *parts), shapes, "first_back_own")


def final(c, z, act, p, q, down, parts, dx, held):
    (d, h), t = down.shape, act.shape[0]
    args = (*c, z, act, p, q, down, *parts, dx, *held)
    return pl.pallas_call(
        final_kernel,
        in_specs=[pl.BlockSpec(memory_space=pltpu.VMEM)] * len(args),
        out_specs=[pl.BlockSpec(memory_space=pltpu.HBM)] * 4,
        out_shape=[pltpu.HBM(s, BF16) for s in ((d, h), (d, h), (d, h), (d, t))],
        scratch_shapes=[pltpu.VMEM((d, h), BF16)] * 3 + [pltpu.SemaphoreType.DMA((1 + 3 * len(chunks(h)),))],
        compiler_params=PARAMS,
        cost_estimate=cost("final"),
        name="final",
    )(*(in_vmem(a) for a in args))


def local_pair(tokens, cotangent, w_gate, w_up, w_down):
    x, g = tokens[0].T, cotangent[0].T
    x_o = shift(x, 0, True)
    g_b = shift(g, -1)
    h, z2, act2, p2, q2, x, *w = loading_first(x, (w_gate[0], w_up[0], w_down[0].T), "first_own")
    h_b = shift(h, -1)
    g_bo = shift(after(g_b, h), 0, True)
    da_b = hidden_cotangent(after(g_b, h), w[2])
    x_o = after(x_o, da_b)
    h_o, z3, act3, p3, q3 = first(x_o, w, "first_other")
    h_bo = shift(h_o, -1)
    *d_b, z0, act0, dg0, du0 = second(after(h_b, h_o), g_b, w[0], w[1], da_b)
    d = [shift(part, 1) for part in d_b]
    d_o = [shift(part, 1, True) for part in d_b]
    parts = second_grads(after(h_bo, d_b[0]), g_bo, w, (z0, g_b, act0, dg0, du0))
    dx, dg2, du2, *parts = first_back(x, d, p2, q2, w, z2, act2, parts)
    gg, gu, gd, dx = final(d_o, z3, act3, p3, q3, w[2], parts, dx, (*d, z2, act2, dg2, du2))
    return dx.T[None], gg[None], gu[None], gd.T[None]


def many_gates(v, gate, up):
    vf = v.astype(F32)
    inverse = lax.rsqrt(jnp.mean(vf * vf, axis=-1, keepdims=True) + EPS)
    normed = vf * inverse
    zed = normed.astype(BF16)
    active, p, q = gate_values(dot(zed, gate), dot(zed, up))
    return inverse, normed, zed, active.astype(BF16), p, q


def many_back(c, saved, gate, up, down):
    inverse, normed, _, _, p, q = saved
    da = dot(c, down, ((1,), (1,)))
    dgate, dup = (da * p).astype(BF16), (da * q).astype(BF16)
    dz = dot(dgate, gate, ((1,), (1,))) + dot(dup, up, ((1,), (1,)))
    inner = jnp.mean(dz * normed, axis=-1, keepdims=True)
    return (c.astype(F32) + inverse * (dz - normed * inner)).astype(BF16), dgate, dup


def local_many(tokens, cotangent, w_gate, w_up, w_down):
    x, g = tokens[0], cotangent[0]
    gate, up, down = w_gate[0], w_up[0], w_down[0]
    g_b = shift(g, -1)
    saved = many_gates(x, gate, up)
    h = (x.astype(F32) + dot(saved[3], down)).astype(BF16)
    saved_b = many_gates(shift(h, -1), gate, up)
    d_b, dg_b, du_b = many_back(g_b, saved_b, gate, up, down)
    d = shift(d_b, 1)
    dx, dg, du = many_back(d, saved, gate, up, down)
    tn = ((0,), (0,))
    zed = jnp.concatenate([saved_b[2], saved[2]])
    parts = (
        dot(zed, jnp.concatenate([dg_b, dg]), tn),
        dot(zed, jnp.concatenate([du_b, du]), tn),
        dot(jnp.concatenate([saved_b[3], saved[3]]), jnp.concatenate([g_b, d]), tn),
    )
    gg, gu, gd = lax.psum(tuple(a.astype(BF16) for a in parts), "dp")
    return dx[None], gg[None], gu[None], gd[None]


def solution(mesh):
    rows = P("blk", "dp", None)
    blocks = P("blk", None, None)
    body = local_pair if mesh.shape["dp"] == 2 else local_many
    return jax.shard_map(
        body,
        mesh=mesh,
        in_specs=(rows, rows, blocks, blocks, blocks),
        out_specs=(rows, blocks, blocks, blocks),
        check_vma=False,
    )
```

```python
import functools

import jax
import jax.numpy as jnp
from jax import lax
from jax.experimental import pallas as pl
from jax.experimental.pallas import tpu as pltpu
from jax.sharding import PartitionSpec as P

F32 = jnp.float32
BF16 = jnp.bfloat16
EPS = 1e-05


def shift(x, by, flip=False):
    blk, dp = lax.axis_size("blk"), lax.axis_size("dp")
    pairs = []
    for i in range(blk):
        for r in range(dp):
            to = (dp - 1 - r) if flip else r
            pairs.append((i * dp + r, ((i + by) % blk) * dp + to))
    return lax.ppermute(x, ("blk", "dp"), pairs)


def dot(a, b, dims=((1,), (0,))):
    return lax.dot_general(a, b, (dims, ((), ())), preferred_element_type=F32)


NT = ((1,), (1,))


def after(x, y):
    return lax.optimization_barrier((x, y))[0]


def normalize(v):
    inverse = lax.rsqrt(jnp.mean(v * v, axis=0, keepdims=True) + EPS)
    return inverse, v * inverse


def chunks(size, step=256):
    step = step if size % step == 0 else size
    return [slice(k, k + step) for k in range(0, size, step)]


def staggered(parts, ahead, use):
    ready = ahead(parts[0])
    for k, part in enumerate(parts):
        following = ahead(parts[k + 1]) if k + 1 < len(parts) else None
        use(part, ready)
        ready = following


def gate_values(pre_g, pre_u):
    s = 0.5 * jnp.tanh(0.5 * pre_g) + 0.5
    q = pre_g * s
    p = pre_u * (s + q * (1.0 - s))
    return q * pre_u, p, q


def input_cotangent(c, dz, inverse, normed):
    inner = jnp.mean(dz * normed, axis=0, keepdims=True)
    return (c + inverse * (dz - normed * inner)).astype(BF16)


def forward_body(x_ref, gate_ref, up_ref, down_ref, h_ref, z_ref, act_ref, p_ref, q_ref, arrived):
    x = x_ref[...].astype(F32)
    _, normed = normalize(x)
    zed = normed.astype(BF16)
    z_ref[...] = zed
    zt = zed.T

    def ahead(hc):
        arrived(hc)
        return dot(zt, gate_ref[:, hc]), dot(zt, up_ref[:, hc])

    total = [x]

    def use(hc, ready):
        active, p, q = gate_values(*ready)
        active = active.astype(BF16)
        act_ref[:, hc] = active
        p_ref[:, hc] = p.astype(BF16)
        q_ref[:, hc] = q.astype(BF16)
        total[0] += dot(down_ref[:, hc], active, NT)

    staggered(chunks(gate_ref.shape[1]), ahead, use)
    h_ref[...] = total[0].astype(BF16)


def forward_kernel(*refs):
    forward_body(*refs, arrived=lambda hc: None)


def loading_forward_kernel(
    x_hbm, gate_hbm, up_hbm, down_hbm, h_ref, z_ref, act_ref, p_ref, q_ref, x_ref, gate_ref, up_ref, down_ref, sem
):
    x_copy = pltpu.make_async_copy(x_hbm, x_ref, sem.at[0])
    x_copy.start()
    copies = {}
    for k, hc in enumerate(chunks(gate_ref.shape[1])):
        copies[hc.start] = []
        for m, (src, dst) in enumerate(((gate_hbm, gate_ref), (up_hbm, up_ref), (down_hbm, down_ref))):
            copy = pltpu.make_async_copy(src.at[:, hc], dst.at[:, hc], sem.at[1 + 3 * k + m])
            copy.start()
            copies[hc.start].append(copy)
    x_copy.wait()

    def arrived(hc):
        for copy in copies[hc.start]:
            copy.wait()

    forward_body(x_ref, gate_ref, up_ref, down_ref, h_ref, z_ref, act_ref, p_ref, q_ref, arrived)


def hidden_cotangent_kernel(c_ref, down_ref, da_ref):
    ct = c_ref[...].T
    for hc in chunks(down_ref.shape[1]):
        da_ref[:, hc] = dot(ct, down_ref[:, hc])


def second_kernel(h_ref, c_ref, gate_ref, up_ref, da_ref, d_ref, d_lo_ref, d_hi_ref, z_ref, act_ref, dg_ref, du_ref):
    inverse, normed = normalize(h_ref[...].astype(F32))
    zed = normed.astype(BF16)
    z_ref[...] = zed
    zt = zed.T

    def ahead(hc):
        return dot(zt, gate_ref[:, hc]), dot(zt, up_ref[:, hc])

    def use(hc, ready):
        active, p, q = gate_values(*ready)
        act_ref[:, hc] = active.astype(BF16)
        dg_ref[:, hc] = (da_ref[:, hc] * p).astype(BF16)
        du_ref[:, hc] = (da_ref[:, hc] * q).astype(BF16)

    staggered(chunks(gate_ref.shape[1]), ahead, use)
    dz = dot(gate_ref[...], dg_ref[...], NT) + dot(up_ref[...], du_ref[...], NT)
    d = input_cotangent(c_ref[...].astype(F32), dz, inverse, normed)
    d_ref[...] = d
    half = d_lo_ref.shape[0]
    d_lo_ref[...] = d[:half]
    d_hi_ref[...] = d[half:]


def second_grads_kernel(
    h_ref, c_ref, gate_ref, up_ref, down_ref, z0_ref, c0_ref, act0_ref, dg0_ref, du0_ref, gg_ref, gu_ref, gd_ref
):
    _, normed = normalize(h_ref[...].astype(F32))
    zed = normed.astype(BF16)
    zt = zed.T
    ct = c_ref[...].T
    z = jnp.concatenate([z0_ref[...], zed], axis=1)
    c = jnp.concatenate([c0_ref[...], c_ref[...]], axis=1)

    def ahead(hc):
        return dot(zt, gate_ref[:, hc]), dot(zt, up_ref[:, hc]), dot(ct, down_ref[:, hc])

    def use(hc, ready):
        active, p, q = gate_values(*ready[:2])
        gd_ref[:, hc] = dot(c, stack(act0_ref[:, hc], active)).astype(BF16)
        gg_ref[:, hc] = dot(z, stack(dg0_ref[:, hc], ready[2] * p)).astype(BF16)
        gu_ref[:, hc] = dot(z, stack(du0_ref[:, hc], ready[2] * q)).astype(BF16)

    staggered(chunks(gate_ref.shape[1]), ahead, use)


def stack(above, below):
    return jnp.concatenate([above, below.astype(BF16)], axis=0)


def whole_tiles(tokens):
    return tokens // 256 * 256 if tokens > 256 else tokens


def first_back_kernel(
    x_ref, c_lo_ref, c_hi_ref, p_ref, q_ref, gate_ref, up_ref, down_ref, z_ref, act_ref, pg_ref, pu_ref, pd_ref,
    d_ref, dg_ref, du_ref, gg_ref, gu_ref, gd_ref,
):
    inverse, normed = normalize(x_ref[...].astype(F32))
    whole_c = jnp.concatenate([c_lo_ref[...], c_hi_ref[...]], axis=0)
    ct = whole_c.T
    cut = whole_tiles(act_ref.shape[0])
    c = whole_c[:, :cut]
    z = z_ref[:, :cut]

    def ahead(hc):
        return dot(ct, down_ref[:, hc])

    def use(hc, da):
        dgate = (da * p_ref[:, hc].astype(F32)).astype(BF16)
        dup = (da * q_ref[:, hc].astype(F32)).astype(BF16)
        dg_ref[:, hc] = dgate
        du_ref[:, hc] = dup
        gd_ref[:, hc] = (pd_ref[:, hc].astype(F32) + dot(c, act_ref[:cut, hc])).astype(BF16)
        gg_ref[:, hc] = (pg_ref[:, hc].astype(F32) + dot(z, dgate[:cut])).astype(BF16)
        gu_ref[:, hc] = (pu_ref[:, hc].astype(F32) + dot(z, dup[:cut])).astype(BF16)

    staggered(chunks(gate_ref.shape[1]), ahead, use)
    dz = dot(gate_ref[...], dg_ref[...], NT) + dot(up_ref[...], du_ref[...], NT)
    d_ref[...] = input_cotangent(whole_c.astype(F32), dz, inverse, normed)


def final_kernel(
    c_ref, z_ref, act_ref, p_ref, q_ref, down_ref, pg_ref, pu_ref, pd_ref, dx_ref, c2_lo_ref, c2_hi_ref, z2_ref, act2_ref, dg2_ref, du2_ref,
    gg_hbm, gu_hbm, gd_hbm, dx_hbm, gg_ref, gu_ref, gd_ref, sem,
):
    copies = [pltpu.make_async_copy(dx_ref, dx_hbm, sem.at[0])]
    copies[0].start()
    ct = c_ref[...].T
    cut = whole_tiles(act_ref.shape[0])
    c2 = jnp.concatenate([c2_lo_ref[:, cut:], c2_hi_ref[:, cut:]], axis=0)
    c = jnp.concatenate([c2, c_ref[...]], axis=1)
    z = jnp.concatenate([z2_ref[:, cut:], z_ref[...]], axis=1)
    parts = chunks(gg_ref.shape[1])

    def add(hc, m, left, right, part_ref, ref, hbm):
        ref[:, hc] = (part_ref[:, hc].astype(F32) + dot(left, right)).astype(BF16)
        copy = pltpu.make_async_copy(ref.at[:, hc], hbm.at[:, hc], sem.at[1 + 3 * (hc.start // parts[0].stop) + m])
        copy.start()
        copies.append(copy)

    def ahead(hc):
        return dot(ct, down_ref[:, hc])

    def use(hc, da):
        add(hc, 2, c, stack(act2_ref[cut:, hc], act_ref[:, hc]), pd_ref, gd_ref, gd_hbm)
        add(hc, 0, z, stack(dg2_ref[cut:, hc], da * p_ref[:, hc].astype(F32)), pg_ref, gg_ref, gg_hbm)
        add(hc, 1, z, stack(du2_ref[cut:, hc], da * q_ref[:, hc].astype(F32)), pu_ref, gu_ref, gu_hbm)

    staggered(parts, ahead, use)
    for copy in copies:
        copy.wait()


PARAMS = pltpu.CompilerParams(vmem_limit_bytes=20 * 1024 * 1024)
COSTS = {}


def cost(name):
    return pl.CostEstimate(flops=COSTS.get(name, 10**10), bytes_accessed=3 * 10**7, transcendentals=0)


def in_vmem(x):
    return pltpu.with_memory_space_constraint(x, pltpu.VMEM)


def whole(kernel, args, out_shapes, name, kind=BF16):
    spec = pl.BlockSpec(memory_space=pltpu.VMEM)
    return pl.pallas_call(
        kernel,
        in_specs=[spec] * len(args),
        out_specs=[spec] * len(out_shapes),
        out_shape=[pltpu.VMEM(s, kind) for s in out_shapes],
        compiler_params=PARAMS,
        cost_estimate=cost(name),
        name=name,
    )(*(in_vmem(a) for a in args))


def first(x, w, name):
    d, t = x.shape
    h = w[0].shape[1]
    return whole(forward_kernel, (x, *w), [(d, t), (d, t), (t, h), (t, h), (t, h)], name)


def loading_first(x, w, name):
    d, t = x.shape
    h = w[0].shape[1]
    shapes = [(d, t), (d, t), (t, h), (t, h), (t, h), (d, t), (d, h), (d, h), (d, h)]
    return pl.pallas_call(
        loading_forward_kernel,
        in_specs=[pl.BlockSpec(memory_space=pltpu.HBM)] * 4,
        out_specs=[pl.BlockSpec(memory_space=pltpu.VMEM)] * len(shapes),
        out_shape=[pltpu.VMEM(s, BF16) for s in shapes],
        scratch_shapes=[pltpu.SemaphoreType.DMA((1 + 3 * len(chunks(h)),))],
        compiler_params=PARAMS,
        cost_estimate=cost(name),
        name=name,
    )(*(pltpu.with_memory_space_constraint(a, pltpu.HBM) for a in (x, *w)))


def hidden_cotangent(c, down):
    return whole(hidden_cotangent_kernel, (c, down), [(c.shape[1], down.shape[1])], "hidden_cotangent", F32)[0]


def second(v, c, gate, up, da):
    d, t = v.shape
    h = gate.shape[1]
    shapes = [(d, t), (d // 2, t), (d - d // 2, t), (d, t), (t, h), (t, h), (t, h)]
    return whole(second_kernel, (v, c, gate, up, da), shapes, "second_own")


def second_grads(v, c, w, own):
    d, h = w[0].shape
    return whole(second_grads_kernel, (v, c, *w, *own), [(d, h)] * 3, "second_grads")


def first_back(x, c, p, q, w, z, act, parts):
    d, t = x.shape
    h = w[0].shape[1]
    shapes = [(d, t), (t, h), (t, h)] + [(d, h)] * 3
    return whole(first_back_kernel, (x, *c, p, q, *w, z, act, *parts), shapes, "first_back_own")


def final(c, z, act, p, q, down, parts, dx, held):
    (d, h), t = down.shape, act.shape[0]
    args = (c, z, act, p, q, down, *parts, dx, *held)
    return pl.pallas_call(
        final_kernel,
        in_specs=[pl.BlockSpec(memory_space=pltpu.VMEM)] * len(args),
        out_specs=[pl.BlockSpec(memory_space=pltpu.HBM)] * 4,
        out_shape=[pltpu.HBM(s, BF16) for s in ((d, h), (d, h), (d, h), (d, t))],
        scratch_shapes=[pltpu.VMEM((d, h), BF16)] * 3 + [pltpu.SemaphoreType.DMA((1 + 3 * len(chunks(h)),))],
        compiler_params=PARAMS,
        cost_estimate=cost("final"),
        name="final",
    )(*(in_vmem(a) for a in args))


def local_pair(tokens, cotangent, w_gate, w_up, w_down):
    x, g = tokens[0].T, cotangent[0].T
    x_o = shift(x, 0, True)
    g_b = shift(g, -1)
    h, z2, act2, p2, q2, x, *w = loading_first(x, (w_gate[0], w_up[0], w_down[0].T), "first_own")
    h_b = shift(h, -1)
    g_bo = shift(after(g_b, h), 0, True)
    da_b = hidden_cotangent(after(g_b, h), w[2])
    x_o = after(x_o, da_b)
    h_o, z3, act3, p3, q3 = first(x_o, w, "first_other")
    h_bo = shift(h_o, -1)
    d_b, *d_halves, z0, act0, dg0, du0 = second(after(h_b, h_o), g_b, w[0], w[1], da_b)
    d = [shift(part, 1) for part in d_halves]
    d_o = shift(d_b, 1, True)
    parts = second_grads(after(h_bo, d_b), g_bo, w, (z0, g_b, act0, dg0, du0))
    dx, dg2, du2, *parts = first_back(x, d, p2, q2, w, z2, act2, parts)
    gg, gu, gd, dx = final(d_o, z3, act3, p3, q3, w[2], parts, dx, (*d, z2, act2, dg2, du2))
    return dx.T[None], gg[None], gu[None], gd.T[None]


def many_gates(v, gate, up):
    vf = v.astype(F32)
    inverse = lax.rsqrt(jnp.mean(vf * vf, axis=-1, keepdims=True) + EPS)
    normed = vf * inverse
    zed = normed.astype(BF16)
    active, p, q = gate_values(dot(zed, gate), dot(zed, up))
    return inverse, normed, zed, active.astype(BF16), p, q


def many_back(c, saved, gate, up, down):
    inverse, normed, _, _, p, q = saved
    da = dot(c, down, ((1,), (1,)))
    dgate, dup = (da * p).astype(BF16), (da * q).astype(BF16)
    dz = dot(dgate, gate, ((1,), (1,))) + dot(dup, up, ((1,), (1,)))
    inner = jnp.mean(dz * normed, axis=-1, keepdims=True)
    return (c.astype(F32) + inverse * (dz - normed * inner)).astype(BF16), dgate, dup


def local_many(tokens, cotangent, w_gate, w_up, w_down):
    x, g = tokens[0], cotangent[0]
    gate, up, down = w_gate[0], w_up[0], w_down[0]
    g_b = shift(g, -1)
    saved = many_gates(x, gate, up)
    h = (x.astype(F32) + dot(saved[3], down)).astype(BF16)
    saved_b = many_gates(shift(h, -1), gate, up)
    d_b, dg_b, du_b = many_back(g_b, saved_b, gate, up, down)
    d = shift(d_b, 1)
    dx, dg, du = many_back(d, saved, gate, up, down)
    tn = ((0,), (0,))
    zed = jnp.concatenate([saved_b[2], saved[2]])
    parts = (
        dot(zed, jnp.concatenate([dg_b, dg]), tn),
        dot(zed, jnp.concatenate([du_b, du]), tn),
        dot(jnp.concatenate([saved_b[3], saved[3]]), jnp.concatenate([g_b, d]), tn),
    )
    gg, gu, gd = lax.psum(tuple(a.astype(BF16) for a in parts), "dp")
    return dx[None], gg[None], gu[None], gd[None]


def solution(mesh):
    rows = P("blk", "dp", None)
    blocks = P("blk", None, None)
    body = local_pair if mesh.shape["dp"] == 2 else local_many
    return jax.shard_map(
        body,
        mesh=mesh,
        in_specs=(rows, rows, blocks, blocks, blocks),
        out_specs=(rows, blocks, blocks, blocks),
        check_vma=False,
    )
```

```python
import functools

import jax
import jax.numpy as jnp
from jax import lax
from jax.experimental import pallas as pl
from jax.experimental.pallas import tpu as pltpu
from jax.sharding import PartitionSpec as P

F32 = jnp.float32
BF16 = jnp.bfloat16
EPS = 1e-05


def shift(x, by, flip=False):
    blk, dp = lax.axis_size("blk"), lax.axis_size("dp")
    pairs = []
    for i in range(blk):
        for r in range(dp):
            to = (dp - 1 - r) if flip else r
            pairs.append((i * dp + r, ((i + by) % blk) * dp + to))
    return lax.ppermute(x, ("blk", "dp"), pairs)


def dot(a, b, dims=((1,), (0,))):
    return lax.dot_general(a, b, (dims, ((), ())), preferred_element_type=F32)


NT = ((1,), (1,))


def after(x, y):
    return lax.optimization_barrier((x, y))[0]


def normalize(v):
    inverse = lax.rsqrt(jnp.mean(v * v, axis=0, keepdims=True) + EPS)
    return inverse, v * inverse


def chunks(size, step=256):
    step = step if size % step == 0 else size
    return [slice(k, k + step) for k in range(0, size, step)]


def staggered(parts, ahead, use):
    ready = ahead(parts[0])
    for k, part in enumerate(parts):
        following = ahead(parts[k + 1]) if k + 1 < len(parts) else None
        use(part, ready)
        ready = following


def gate_values(pre_g, pre_u):
    s = 0.5 * jnp.tanh(0.5 * pre_g) + 0.5
    q = pre_g * s
    p = pre_u * (s + q * (1.0 - s))
    return q * pre_u, p, q


def input_cotangent(c, dz, inverse, normed):
    inner = jnp.mean(dz * normed, axis=0, keepdims=True)
    return (c + inverse * (dz - normed * inner)).astype(BF16)


def forward_body(x_ref, gate_ref, up_ref, down_ref, h_ref, z_ref, act_ref, p_ref, q_ref, arrived):
    x = x_ref[...].astype(F32)
    _, normed = normalize(x)
    zed = normed.astype(BF16)
    z_ref[...] = zed
    zt = zed.T

    def ahead(hc):
        arrived(hc)
        return dot(zt, gate_ref[:, hc]), dot(zt, up_ref[:, hc])

    total = [x]

    def use(hc, ready):
        active, p, q = gate_values(*ready)
        active = active.astype(BF16)
        act_ref[:, hc] = active
        p_ref[:, hc] = p.astype(BF16)
        q_ref[:, hc] = q.astype(BF16)
        total[0] += dot(down_ref[:, hc], active, NT)

    staggered(chunks(gate_ref.shape[1]), ahead, use)
    h_ref[...] = total[0].astype(BF16)


def forward_kernel(*refs):
    forward_body(*refs, arrived=lambda hc: None)


def loading_forward_kernel(
    x_hbm, gate_hbm, up_hbm, down_hbm, h_ref, z_ref, act_ref, p_ref, q_ref, x_ref, gate_ref, up_ref, down_ref, sem
):
    x_copy = pltpu.make_async_copy(x_hbm, x_ref, sem.at[0])
    x_copy.start()
    copies = {}
    for k, hc in enumerate(chunks(gate_ref.shape[1])):
        copies[hc.start] = []
        for m, (src, dst) in enumerate(((gate_hbm, gate_ref), (up_hbm, up_ref), (down_hbm, down_ref))):
            copy = pltpu.make_async_copy(src.at[:, hc], dst.at[:, hc], sem.at[1 + 3 * k + m])
            copy.start()
            copies[hc.start].append(copy)
    x_copy.wait()

    def arrived(hc):
        for copy in copies[hc.start]:
            copy.wait()

    forward_body(x_ref, gate_ref, up_ref, down_ref, h_ref, z_ref, act_ref, p_ref, q_ref, arrived)


def hidden_cotangent_kernel(c_ref, down_ref, da_ref):
    ct = c_ref[...].T
    for hc in chunks(down_ref.shape[1]):
        da_ref[:, hc] = dot(ct, down_ref[:, hc])


def second_kernel(h_ref, c_ref, gate_ref, up_ref, da_ref, d_first_ref, d_last_ref, d_lo_ref, d_hi_ref, z_ref, act_ref, dg_ref, du_ref):
    inverse, normed = normalize(h_ref[...].astype(F32))
    zed = normed.astype(BF16)
    z_ref[...] = zed
    zt = zed.T

    def ahead(hc):
        return dot(zt, gate_ref[:, hc]), dot(zt, up_ref[:, hc])

    def use(hc, ready):
        active, p, q = gate_values(*ready)
        act_ref[:, hc] = active.astype(BF16)
        dg_ref[:, hc] = (da_ref[:, hc] * p).astype(BF16)
        du_ref[:, hc] = (da_ref[:, hc] * q).astype(BF16)

    staggered(chunks(gate_ref.shape[1]), ahead, use)
    dz = dot(gate_ref[...], dg_ref[...], NT) + dot(up_ref[...], du_ref[...], NT)
    d = input_cotangent(c_ref[...].astype(F32), dz, inverse, normed)
    cut = d_first_ref.shape[1]
    d_first_ref[...] = d[:, :cut]
    d_last_ref[...] = d[:, cut:]
    half = d_lo_ref.shape[0]
    d_lo_ref[...] = d[:half]
    d_hi_ref[...] = d[half:]


def second_grads_kernel(
    h_ref, c_ref, gate_ref, up_ref, down_ref, z0_ref, c0_ref, act0_ref, dg0_ref, du0_ref, gg_ref, gu_ref, gd_ref
):
    _, normed = normalize(h_ref[...].astype(F32))
    zed = normed.astype(BF16)
    zt = zed.T
    ct = c_ref[...].T
    z = jnp.concatenate([z0_ref[...], zed], axis=1)
    c = jnp.concatenate([c0_ref[...], c_ref[...]], axis=1)

    def ahead(hc):
        return dot(zt, gate_ref[:, hc]), dot(zt, up_ref[:, hc]), dot(ct, down_ref[:, hc])

    def use(hc, ready):
        active, p, q = gate_values(*ready[:2])
        gd_ref[:, hc] = dot(c, stack(act0_ref[:, hc], active)).astype(BF16)
        gg_ref[:, hc] = dot(z, stack(dg0_ref[:, hc], ready[2] * p)).astype(BF16)
        gu_ref[:, hc] = dot(z, stack(du0_ref[:, hc], ready[2] * q)).astype(BF16)

    staggered(chunks(gate_ref.shape[1]), ahead, use)


def stack(above, below):
    return jnp.concatenate([above, below.astype(BF16)], axis=0)


def whole_tiles(tokens):
    return tokens // 256 * 256 if tokens > 256 else tokens


def first_back_kernel(
    x_ref, c_lo_ref, c_hi_ref, p_ref, q_ref, gate_ref, up_ref, down_ref, z_ref, act_ref, pg_ref, pu_ref, pd_ref,
    d_ref, dg_ref, du_ref, gg_ref, gu_ref, gd_ref,
):
    inverse, normed = normalize(x_ref[...].astype(F32))
    whole_c = jnp.concatenate([c_lo_ref[...], c_hi_ref[...]], axis=0)
    ct = whole_c.T
    cut = whole_tiles(act_ref.shape[0])
    c = whole_c[:, :cut]
    z = z_ref[:, :cut]

    def ahead(hc):
        return dot(ct, down_ref[:, hc])

    def use(hc, da):
        dgate = (da * p_ref[:, hc].astype(F32)).astype(BF16)
        dup = (da * q_ref[:, hc].astype(F32)).astype(BF16)
        dg_ref[:, hc] = dgate
        du_ref[:, hc] = dup
        gd_ref[:, hc] = (pd_ref[:, hc].astype(F32) + dot(c, act_ref[:cut, hc])).astype(BF16)
        gg_ref[:, hc] = (pg_ref[:, hc].astype(F32) + dot(z, dgate[:cut])).astype(BF16)
        gu_ref[:, hc] = (pu_ref[:, hc].astype(F32) + dot(z, dup[:cut])).astype(BF16)

    staggered(chunks(gate_ref.shape[1]), ahead, use)
    dz = dot(gate_ref[...], dg_ref[...], NT) + dot(up_ref[...], du_ref[...], NT)
    d_ref[...] = input_cotangent(whole_c.astype(F32), dz, inverse, normed)


def add_kernel(c_ref, z_ref, act_ref, p_ref, q_ref, down_ref, pg_ref, pu_ref, pd_ref, gg_ref, gu_ref, gd_ref):
    c = c_ref[...]
    cut = c.shape[1]
    z = z_ref[:, :cut]
    ct = c.T

    def ahead(hc):
        return dot(ct, down_ref[:, hc])

    def use(hc, da):
        dgate = (da * p_ref[:cut, hc].astype(F32)).astype(BF16)
        dup = (da * q_ref[:cut, hc].astype(F32)).astype(BF16)
        gd_ref[:, hc] = (pd_ref[:, hc].astype(F32) + dot(c, act_ref[:cut, hc])).astype(BF16)
        gg_ref[:, hc] = (pg_ref[:, hc].astype(F32) + dot(z, dgate)).astype(BF16)
        gu_ref[:, hc] = (pu_ref[:, hc].astype(F32) + dot(z, dup)).astype(BF16)

    staggered(chunks(gg_ref.shape[1]), ahead, use)


def final_kernel(
    c_ref, z_ref, act_ref, p_ref, q_ref, down_ref, pg_ref, pu_ref, pd_ref, dx_ref, c2_lo_ref, c2_hi_ref, z2_ref, act2_ref, dg2_ref, du2_ref,
    gg_hbm, gu_hbm, gd_hbm, dx_hbm, gg_ref, gu_ref, gd_ref, sem,
):
    copies = [pltpu.make_async_copy(dx_ref, dx_hbm, sem.at[0])]
    copies[0].start()
    ct = c_ref[...].T
    cut = whole_tiles(act_ref.shape[0])
    c2 = jnp.concatenate([c2_lo_ref[:, cut:], c2_hi_ref[:, cut:]], axis=0)
    c = jnp.concatenate([c2, c_ref[...]], axis=1)
    z = jnp.concatenate([z2_ref[:, cut:], z_ref[:, cut:]], axis=1)
    parts = chunks(gg_ref.shape[1])

    def add(hc, m, left, right, part_ref, ref, hbm):
        ref[:, hc] = (part_ref[:, hc].astype(F32) + dot(left, right)).astype(BF16)
        copy = pltpu.make_async_copy(ref.at[:, hc], hbm.at[:, hc], sem.at[1 + 3 * (hc.start // parts[0].stop) + m])
        copy.start()
        copies.append(copy)

    def ahead(hc):
        return dot(ct, down_ref[:, hc])

    def use(hc, da):
        add(hc, 2, c, stack(act2_ref[cut:, hc], act_ref[cut:, hc]), pd_ref, gd_ref, gd_hbm)
        add(hc, 0, z, stack(dg2_ref[cut:, hc], da * p_ref[cut:, hc].astype(F32)), pg_ref, gg_ref, gg_hbm)
        add(hc, 1, z, stack(du2_ref[cut:, hc], da * q_ref[cut:, hc].astype(F32)), pu_ref, gu_ref, gu_hbm)

    staggered(parts, ahead, use)
    for copy in copies:
        copy.wait()


PARAMS = pltpu.CompilerParams(vmem_limit_bytes=20 * 1024 * 1024)
COSTS = {}


def cost(name):
    return pl.CostEstimate(flops=COSTS.get(name, 10**10), bytes_accessed=3 * 10**7, transcendentals=0)


def in_vmem(x):
    return pltpu.with_memory_space_constraint(x, pltpu.VMEM)


def whole(kernel, args, out_shapes, name, kind=BF16):
    spec = pl.BlockSpec(memory_space=pltpu.VMEM)
    return pl.pallas_call(
        kernel,
        in_specs=[spec] * len(args),
        out_specs=[spec] * len(out_shapes),
        out_shape=[pltpu.VMEM(s, kind) for s in out_shapes],
        compiler_params=PARAMS,
        cost_estimate=cost(name),
        name=name,
    )(*(in_vmem(a) for a in args))


def first(x, w, name):
    d, t = x.shape
    h = w[0].shape[1]
    return whole(forward_kernel, (x, *w), [(d, t), (d, t), (t, h), (t, h), (t, h)], name)


def loading_first(x, w, name):
    d, t = x.shape
    h = w[0].shape[1]
    shapes = [(d, t), (d, t), (t, h), (t, h), (t, h), (d, t), (d, h), (d, h), (d, h)]
    return pl.pallas_call(
        loading_forward_kernel,
        in_specs=[pl.BlockSpec(memory_space=pltpu.HBM)] * 4,
        out_specs=[pl.BlockSpec(memory_space=pltpu.VMEM)] * len(shapes),
        out_shape=[pltpu.VMEM(s, BF16) for s in shapes],
        scratch_shapes=[pltpu.SemaphoreType.DMA((1 + 3 * len(chunks(h)),))],
        compiler_params=PARAMS,
        cost_estimate=cost(name),
        name=name,
    )(*(pltpu.with_memory_space_constraint(a, pltpu.HBM) for a in (x, *w)))


def hidden_cotangent(c, down):
    return whole(hidden_cotangent_kernel, (c, down), [(c.shape[1], down.shape[1])], "hidden_cotangent", F32)[0]


def second(v, c, gate, up, da):
    d, t = v.shape
    h = gate.shape[1]
    cut = whole_tiles(t)
    shapes = [(d, cut), (d, t - cut), (d // 2, t), (d - d // 2, t), (d, t), (t, h), (t, h), (t, h)]
    return whole(second_kernel, (v, c, gate, up, da), shapes, "second_own")


def second_grads(v, c, w, own):
    d, h = w[0].shape
    return whole(second_grads_kernel, (v, c, *w, *own), [(d, h)] * 3, "second_grads")


def first_back(x, c, p, q, w, z, act, parts):
    d, t = x.shape
    h = w[0].shape[1]
    shapes = [(d, t), (t, h), (t, h)] + [(d, h)] * 3
    return whole(first_back_kernel, (x, *c, p, q, *w, z, act, *parts), shapes, "first_back_own")


def add(c, z, act, p, q, down, parts):
    return whole(add_kernel, (c, z, act, p, q, down, *parts), [down.shape] * 3, "add_other")


def final(c, z, act, p, q, down, parts, dx, held):
    (d, h), t = down.shape, act.shape[0]
    args = (c, z, act, p, q, down, *parts, dx, *held)
    return pl.pallas_call(
        final_kernel,
        in_specs=[pl.BlockSpec(memory_space=pltpu.VMEM)] * len(args),
        out_specs=[pl.BlockSpec(memory_space=pltpu.HBM)] * 4,
        out_shape=[pltpu.HBM(s, BF16) for s in ((d, h), (d, h), (d, h), (d, t))],
        scratch_shapes=[pltpu.VMEM((d, h), BF16)] * 3 + [pltpu.SemaphoreType.DMA((1 + 3 * len(chunks(h)),))],
        compiler_params=PARAMS,
        cost_estimate=cost("final"),
        name="final",
    )(*(in_vmem(a) for a in args))


def local_pair(tokens, cotangent, w_gate, w_up, w_down):
    x, g = tokens[0].T, cotangent[0].T
    x_o = shift(x, 0, True)
    g_b = shift(g, -1)
    h, z2, act2, p2, q2, x, *w = loading_first(x, (w_gate[0], w_up[0], w_down[0].T), "first_own")
    h_b = shift(h, -1)
    g_bo = shift(after(g_b, h), 0, True)
    da_b = hidden_cotangent(after(g_b, h), w[2])
    x_o = after(x_o, da_b)
    h_o, z3, act3, p3, q3 = first(x_o, w, "first_other")
    h_bo = shift(h_o, -1)
    d_first, d_last, *d_halves, z0, act0, dg0, du0 = second(after(h_b, h_o), g_b, w[0], w[1], da_b)
    d = [shift(part, 1) for part in d_halves]
    o_first = shift(d_first, 1, True)
    o_last = shift(after(d_last, h_bo), 1, True)
    parts = second_grads(after(h_bo, d_first), g_bo, w, (z0, g_b, act0, dg0, du0))
    dx, dg2, du2, *parts = first_back(x, d, p2, q2, w, z2, act2, parts)
    parts = add(o_first, z3, act3, p3, q3, w[2], parts)
    gg, gu, gd, dx = final(o_last, z3, act3, p3, q3, w[2], parts, dx, (*d, z2, act2, dg2, du2))
    return dx.T[None], gg[None], gu[None], gd.T[None]


def many_gates(v, gate, up):
    vf = v.astype(F32)
    inverse = lax.rsqrt(jnp.mean(vf * vf, axis=-1, keepdims=True) + EPS)
    normed = vf * inverse
    zed = normed.astype(BF16)
    active, p, q = gate_values(dot(zed, gate), dot(zed, up))
    return inverse, normed, zed, active.astype(BF16), p, q


def many_back(c, saved, gate, up, down):
    inverse, normed, _, _, p, q = saved
    da = dot(c, down, ((1,), (1,)))
    dgate, dup = (da * p).astype(BF16), (da * q).astype(BF16)
    dz = dot(dgate, gate, ((1,), (1,))) + dot(dup, up, ((1,), (1,)))
    inner = jnp.mean(dz * normed, axis=-1, keepdims=True)
    return (c.astype(F32) + inverse * (dz - normed * inner)).astype(BF16), dgate, dup


def local_many(tokens, cotangent, w_gate, w_up, w_down):
    x, g = tokens[0], cotangent[0]
    gate, up, down = w_gate[0], w_up[0], w_down[0]
    g_b = shift(g, -1)
    saved = many_gates(x, gate, up)
    h = (x.astype(F32) + dot(saved[3], down)).astype(BF16)
    saved_b = many_gates(shift(h, -1), gate, up)
    d_b, dg_b, du_b = many_back(g_b, saved_b, gate, up, down)
    d = shift(d_b, 1)
    dx, dg, du = many_back(d, saved, gate, up, down)
    tn = ((0,), (0,))
    zed = jnp.concatenate([saved_b[2], saved[2]])
    parts = (
        dot(zed, jnp.concatenate([dg_b, dg]), tn),
        dot(zed, jnp.concatenate([du_b, du]), tn),
        dot(jnp.concatenate([saved_b[3], saved[3]]), jnp.concatenate([g_b, d]), tn),
    )
    gg, gu, gd = lax.psum(tuple(a.astype(BF16) for a in parts), "dp")
    return dx[None], gg[None], gu[None], gd[None]


def solution(mesh):
    rows = P("blk", "dp", None)
    blocks = P("blk", None, None)
    body = local_pair if mesh.shape["dp"] == 2 else local_many
    return jax.shard_map(
        body,
        mesh=mesh,
        in_specs=(rows, rows, blocks, blocks, blocks),
        out_specs=(rows, blocks, blocks, blocks),
        check_vma=False,
    )
```

```python
import functools

import jax
import jax.numpy as jnp
from jax import lax
from jax.experimental import pallas as pl
from jax.experimental.pallas import tpu as pltpu
from jax.sharding import PartitionSpec as P

F32 = jnp.float32
BF16 = jnp.bfloat16
EPS = 1e-05


def shift(x, by, flip=False):
    blk, dp = lax.axis_size("blk"), lax.axis_size("dp")
    pairs = []
    for i in range(blk):
        for r in range(dp):
            to = (dp - 1 - r) if flip else r
            pairs.append((i * dp + r, ((i + by) % blk) * dp + to))
    return lax.ppermute(x, ("blk", "dp"), pairs)


def dot(a, b, dims=((1,), (0,))):
    return lax.dot_general(a, b, (dims, ((), ())), preferred_element_type=F32)


NT = ((1,), (1,))


def after(x, y):
    return lax.optimization_barrier((x, y))[0]


def normalize(v):
    inverse = lax.rsqrt(jnp.mean(v * v, axis=0, keepdims=True) + EPS)
    return inverse, v * inverse


def chunks(size, step=256):
    step = step if size % step == 0 else size
    return [slice(k, k + step) for k in range(0, size, step)]


def staggered(parts, ahead, use):
    ready = ahead(parts[0])
    for k, part in enumerate(parts):
        following = ahead(parts[k + 1]) if k + 1 < len(parts) else None
        use(part, ready)
        ready = following


def gate_values(pre_g, pre_u):
    s = 0.5 * jnp.tanh(0.5 * pre_g) + 0.5
    q = pre_g * s
    p = pre_u * (s + q * (1.0 - s))
    return q * pre_u, p, q


def input_cotangent(c, dz, inverse, normed):
    inner = jnp.mean(dz * normed, axis=0, keepdims=True)
    return (c + inverse * (dz - normed * inner)).astype(BF16)


def forward_body(x_ref, gate_ref, up_ref, down_ref, h_ref, z_ref, act_ref, p_ref, q_ref, arrived):
    x = x_ref[...].astype(F32)
    _, normed = normalize(x)
    zed = normed.astype(BF16)
    z_ref[...] = zed
    zt = zed.T

    def ahead(hc):
        arrived(hc)
        return dot(zt, gate_ref[:, hc]), dot(zt, up_ref[:, hc])

    total = [x]

    def use(hc, ready):
        active, p, q = gate_values(*ready)
        active = active.astype(BF16)
        act_ref[:, hc] = active
        p_ref[:, hc] = p.astype(BF16)
        q_ref[:, hc] = q.astype(BF16)
        total[0] += dot(down_ref[:, hc], active, NT)

    staggered(chunks(gate_ref.shape[1]), ahead, use)
    h_ref[...] = total[0].astype(BF16)


def forward_kernel(*refs):
    forward_body(*refs, arrived=lambda hc: None)


def loading_forward_kernel(
    x_hbm, gate_hbm, up_hbm, down_hbm, h_ref, z_ref, act_ref, p_ref, q_ref, x_ref, gate_ref, up_ref, down_ref, sem
):
    x_copy = pltpu.make_async_copy(x_hbm, x_ref, sem.at[0])
    x_copy.start()
    copies = {}
    for k, hc in enumerate(chunks(gate_ref.shape[1])):
        copies[hc.start] = []
        for m, (src, dst) in enumerate(((gate_hbm, gate_ref), (up_hbm, up_ref), (down_hbm, down_ref))):
            copy = pltpu.make_async_copy(src.at[:, hc], dst.at[:, hc], sem.at[1 + 3 * k + m])
            copy.start()
            copies[hc.start].append(copy)
    x_copy.wait()

    def arrived(hc):
        for copy in copies[hc.start]:
            copy.wait()

    forward_body(x_ref, gate_ref, up_ref, down_ref, h_ref, z_ref, act_ref, p_ref, q_ref, arrived)


def hidden_cotangent_kernel(c_ref, down_ref, da_ref):
    ct = c_ref[...].T
    for hc in chunks(down_ref.shape[1]):
        da_ref[:, hc] = dot(ct, down_ref[:, hc])


def second_kernel(h_ref, c_ref, gate_ref, up_ref, da_ref, d_first_ref, d_last_ref, d_lo_ref, d_hi_ref, z_ref, act_ref, dg_ref, du_ref):
    inverse, normed = normalize(h_ref[...].astype(F32))
    zed = normed.astype(BF16)
    z_ref[...] = zed
    zt = zed.T

    def ahead(hc):
        return dot(zt, gate_ref[:, hc]), dot(zt, up_ref[:, hc])

    def use(hc, ready):
        active, p, q = gate_values(*ready)
        act_ref[:, hc] = active.astype(BF16)
        dg_ref[:, hc] = (da_ref[:, hc] * p).astype(BF16)
        du_ref[:, hc] = (da_ref[:, hc] * q).astype(BF16)

    staggered(chunks(gate_ref.shape[1]), ahead, use)
    dz = dot(gate_ref[...], dg_ref[...], NT) + dot(up_ref[...], du_ref[...], NT)
    d = input_cotangent(c_ref[...].astype(F32), dz, inverse, normed)
    cut = d_first_ref.shape[1]
    d_first_ref[...] = d[:, :cut]
    d_last_ref[...] = d[:, cut:]
    half = d_lo_ref.shape[0]
    d_lo_ref[...] = d[:half]
    d_hi_ref[...] = d[half:]


def second_grads_kernel(
    h_ref, c_ref, gate_ref, up_ref, down_ref, z0_ref, c0_ref, act0_ref, dg0_ref, du0_ref, gg_ref, gu_ref, gd_ref
):
    _, normed = normalize(h_ref[...].astype(F32))
    zed = normed.astype(BF16)
    zt = zed.T
    ct = c_ref[...].T
    z = jnp.concatenate([z0_ref[...], zed], axis=1)
    c = jnp.concatenate([c0_ref[...], c_ref[...]], axis=1)

    def ahead(hc):
        return dot(zt, gate_ref[:, hc]), dot(zt, up_ref[:, hc]), dot(ct, down_ref[:, hc])

    def use(hc, ready):
        active, p, q = gate_values(*ready[:2])
        gd_ref[:, hc] = dot(c, stack(act0_ref[:, hc], active)).astype(BF16)
        gg_ref[:, hc] = dot(z, stack(dg0_ref[:, hc], ready[2] * p)).astype(BF16)
        gu_ref[:, hc] = dot(z, stack(du0_ref[:, hc], ready[2] * q)).astype(BF16)

    staggered(chunks(gate_ref.shape[1]), ahead, use)


def stack(above, below):
    return jnp.concatenate([above, below.astype(BF16)], axis=0)


def whole_tiles(tokens):
    return tokens // 256 * 256 if tokens > 256 else tokens


def first_back_kernel(
    x_ref, c_lo_ref, c_hi_ref, p_ref, q_ref, gate_ref, up_ref, down_ref, z_ref, act_ref, pg_ref, pu_ref, pd_ref,
    d_ref, dg_ref, du_ref, gg_ref, gu_ref, gd_ref,
):
    inverse, normed = normalize(x_ref[...].astype(F32))
    whole_c = jnp.concatenate([c_lo_ref[...], c_hi_ref[...]], axis=0)
    ct = whole_c.T
    cut = whole_tiles(act_ref.shape[0])
    c = whole_c[:, :cut]
    z = z_ref[:, :cut]

    def ahead(hc):
        return dot(ct, down_ref[:, hc])

    def use(hc, da):
        dgate = (da * p_ref[:, hc].astype(F32)).astype(BF16)
        dup = (da * q_ref[:, hc].astype(F32)).astype(BF16)
        dg_ref[:, hc] = dgate
        du_ref[:, hc] = dup
        gd_ref[:, hc] = (pd_ref[:, hc].astype(F32) + dot(c, act_ref[:cut, hc])).astype(BF16)
        gg_ref[:, hc] = (pg_ref[:, hc].astype(F32) + dot(z, dgate[:cut])).astype(BF16)
        gu_ref[:, hc] = (pu_ref[:, hc].astype(F32) + dot(z, dup[:cut])).astype(BF16)

    staggered(chunks(gate_ref.shape[1]), ahead, use)
    dz = dot(gate_ref[...], dg_ref[...], NT) + dot(up_ref[...], du_ref[...], NT)
    d_ref[...] = input_cotangent(whole_c.astype(F32), dz, inverse, normed)


def add_kernel(c_ref, z_ref, act_ref, p_ref, q_ref, down_ref, pg_ref, pu_ref, pd_ref, gg_ref, gu_ref, gd_ref):
    c = c_ref[...]
    cut = c.shape[1]
    z = z_ref[:, :cut]
    ct = c.T

    def ahead(hc):
        return dot(ct, down_ref[:, hc])

    def use(hc, da):
        dgate = (da * p_ref[:cut, hc].astype(F32)).astype(BF16)
        dup = (da * q_ref[:cut, hc].astype(F32)).astype(BF16)
        gd_ref[:, hc] = (pd_ref[:, hc].astype(F32) + dot(c, act_ref[:cut, hc])).astype(BF16)
        gg_ref[:, hc] = (pg_ref[:, hc].astype(F32) + dot(z, dgate)).astype(BF16)
        gu_ref[:, hc] = (pu_ref[:, hc].astype(F32) + dot(z, dup)).astype(BF16)

    staggered(chunks(gg_ref.shape[1]), ahead, use)


def final_kernel(
    c_ref, z_ref, act_ref, p_ref, q_ref, down_ref, pg_ref, pu_ref, pd_ref, dx_ref, c2_lo_ref, c2_hi_ref, z2_ref, act2_ref, dg2_ref, du2_ref,
    gg_hbm, gu_hbm, gd_hbm, dx_hbm, gg_ref, gu_ref, gd_ref, sem,
):
    copies = [pltpu.make_async_copy(dx_ref, dx_hbm, sem.at[0])]
    copies[0].start()
    ct = c_ref[...].T
    cut = whole_tiles(act_ref.shape[0])
    c2 = jnp.concatenate([c2_lo_ref[:, cut:], c2_hi_ref[:, cut:]], axis=0)
    c = jnp.concatenate([c2, c_ref[...]], axis=1)
    z = jnp.concatenate([z2_ref[:, cut:], z_ref[:, cut:]], axis=1)
    parts = chunks(gg_ref.shape[1])

    def add(hc, m, left, right, part_ref, ref, hbm):
        ref[:, hc] = (part_ref[:, hc].astype(F32) + dot(left, right)).astype(BF16)
        copy = pltpu.make_async_copy(ref.at[:, hc], hbm.at[:, hc], sem.at[1 + 3 * (hc.start // parts[0].stop) + m])
        copy.start()
        copies.append(copy)

    def ahead(hc):
        return dot(ct, down_ref[:, hc])

    def use(hc, da):
        add(hc, 2, c, stack(act2_ref[cut:, hc], act_ref[cut:, hc]), pd_ref, gd_ref, gd_hbm)
        add(hc, 0, z, stack(dg2_ref[cut:, hc], da * p_ref[cut:, hc].astype(F32)), pg_ref, gg_ref, gg_hbm)
        add(hc, 1, z, stack(du2_ref[cut:, hc], da * q_ref[cut:, hc].astype(F32)), pu_ref, gu_ref, gu_hbm)

    staggered(parts, ahead, use)
    for copy in copies:
        copy.wait()


PARAMS = pltpu.CompilerParams(vmem_limit_bytes=20 * 1024 * 1024)
COSTS = {}


def cost(name):
    return pl.CostEstimate(flops=COSTS.get(name, 10**10), bytes_accessed=3 * 10**7, transcendentals=0)


def in_vmem(x):
    return pltpu.with_memory_space_constraint(x, pltpu.VMEM)


def whole(kernel, args, out_shapes, name, kind=BF16):
    spec = pl.BlockSpec(memory_space=pltpu.VMEM)
    return pl.pallas_call(
        kernel,
        in_specs=[spec] * len(args),
        out_specs=[spec] * len(out_shapes),
        out_shape=[pltpu.VMEM(s, kind) for s in out_shapes],
        compiler_params=PARAMS,
        cost_estimate=cost(name),
        name=name,
    )(*(in_vmem(a) for a in args))


def first(x, w, name):
    d, t = x.shape
    h = w[0].shape[1]
    return whole(forward_kernel, (x, *w), [(d, t), (d, t), (t, h), (t, h), (t, h)], name)


def loading_first(x, w, name):
    d, t = x.shape
    h = w[0].shape[1]
    shapes = [(d, t), (d, t), (t, h), (t, h), (t, h), (d, t), (d, h), (d, h), (d, h)]
    return pl.pallas_call(
        loading_forward_kernel,
        in_specs=[pl.BlockSpec(memory_space=pltpu.HBM)] * 4,
        out_specs=[pl.BlockSpec(memory_space=pltpu.VMEM)] * len(shapes),
        out_shape=[pltpu.VMEM(s, BF16) for s in shapes],
        scratch_shapes=[pltpu.SemaphoreType.DMA((1 + 3 * len(chunks(h)),))],
        compiler_params=PARAMS,
        cost_estimate=cost(name),
        name=name,
    )(*(pltpu.with_memory_space_constraint(a, pltpu.HBM) for a in (x, *w)))


def hidden_cotangent(c, down):
    return whole(hidden_cotangent_kernel, (c, down), [(c.shape[1], down.shape[1])], "hidden_cotangent", F32)[0]


def second(v, c, gate, up, da):
    d, t = v.shape
    h = gate.shape[1]
    cut, most = whole_tiles(t), d * 7 // 9
    shapes = [(d, cut), (d, t - cut), (most, t), (d - most, t), (d, t), (t, h), (t, h), (t, h)]
    return whole(second_kernel, (v, c, gate, up, da), shapes, "second_own")


def second_grads(v, c, w, own):
    d, h = w[0].shape
    return whole(second_grads_kernel, (v, c, *w, *own), [(d, h)] * 3, "second_grads")


def first_back(x, c, p, q, w, z, act, parts):
    d, t = x.shape
    h = w[0].shape[1]
    shapes = [(d, t), (t, h), (t, h)] + [(d, h)] * 3
    return whole(first_back_kernel, (x, *c, p, q, *w, z, act, *parts), shapes, "first_back_own")


def add(c, z, act, p, q, down, parts):
    return whole(add_kernel, (c, z, act, p, q, down, *parts), [down.shape] * 3, "add_other")


def final(c, z, act, p, q, down, parts, dx, held):
    (d, h), t = down.shape, act.shape[0]
    args = (c, z, act, p, q, down, *parts, dx, *held)
    return pl.pallas_call(
        final_kernel,
        in_specs=[pl.BlockSpec(memory_space=pltpu.VMEM)] * len(args),
        out_specs=[pl.BlockSpec(memory_space=pltpu.HBM)] * 4,
        out_shape=[pltpu.HBM(s, BF16) for s in ((d, h), (d, h), (d, h), (d, t))],
        scratch_shapes=[pltpu.VMEM((d, h), BF16)] * 3 + [pltpu.SemaphoreType.DMA((1 + 3 * len(chunks(h)),))],
        compiler_params=PARAMS,
        cost_estimate=cost("final"),
        name="final",
    )(*(in_vmem(a) for a in args))


def local_pair(tokens, cotangent, w_gate, w_up, w_down):
    x, g = tokens[0].T, cotangent[0].T
    x_o = shift(x, 0, True)
    g_b = shift(g, -1)
    h, z2, act2, p2, q2, x, *w = loading_first(x, (w_gate[0], w_up[0], w_down[0].T), "first_own")
    h_b = shift(h, -1)
    g_bo = shift(after(g_b, h), 0, True)
    da_b = hidden_cotangent(after(g_b, h), w[2])
    x_o = after(x_o, da_b)
    h_o, z3, act3, p3, q3 = first(x_o, w, "first_other")
    h_bo = shift(h_o, -1)
    d_first, d_last, *d_halves, z0, act0, dg0, du0 = second(after(h_b, h_o), g_b, w[0], w[1], da_b)
    d = [shift(part, 1) for part in d_halves]
    o_first = shift(d_first, 1, True)
    o_last = shift(after(d_last, h_bo), 1, True)
    parts = second_grads(after(h_bo, d_first), g_bo, w, (z0, g_b, act0, dg0, du0))
    dx, dg2, du2, *parts = first_back(x, d, p2, q2, w, z2, act2, parts)
    parts = add(o_first, z3, act3, p3, q3, w[2], parts)
    gg, gu, gd, dx = final(o_last, z3, act3, p3, q3, w[2], parts, dx, (*d, z2, act2, dg2, du2))
    return dx.T[None], gg[None], gu[None], gd.T[None]


def many_gates(v, gate, up):
    vf = v.astype(F32)
    inverse = lax.rsqrt(jnp.mean(vf * vf, axis=-1, keepdims=True) + EPS)
    normed = vf * inverse
    zed = normed.astype(BF16)
    active, p, q = gate_values(dot(zed, gate), dot(zed, up))
    return inverse, normed, zed, active.astype(BF16), p, q


def many_back(c, saved, gate, up, down):
    inverse, normed, _, _, p, q = saved
    da = dot(c, down, ((1,), (1,)))
    dgate, dup = (da * p).astype(BF16), (da * q).astype(BF16)
    dz = dot(dgate, gate, ((1,), (1,))) + dot(dup, up, ((1,), (1,)))
    inner = jnp.mean(dz * normed, axis=-1, keepdims=True)
    return (c.astype(F32) + inverse * (dz - normed * inner)).astype(BF16), dgate, dup


def local_many(tokens, cotangent, w_gate, w_up, w_down):
    x, g = tokens[0], cotangent[0]
    gate, up, down = w_gate[0], w_up[0], w_down[0]
    g_b = shift(g, -1)
    saved = many_gates(x, gate, up)
    h = (x.astype(F32) + dot(saved[3], down)).astype(BF16)
    saved_b = many_gates(shift(h, -1), gate, up)
    d_b, dg_b, du_b = many_back(g_b, saved_b, gate, up, down)
    d = shift(d_b, 1)
    dx, dg, du = many_back(d, saved, gate, up, down)
    tn = ((0,), (0,))
    zed = jnp.concatenate([saved_b[2], saved[2]])
    parts = (
        dot(zed, jnp.concatenate([dg_b, dg]), tn),
        dot(zed, jnp.concatenate([du_b, du]), tn),
        dot(jnp.concatenate([saved_b[3], saved[3]]), jnp.concatenate([g_b, d]), tn),
    )
    gg, gu, gd = lax.psum(tuple(a.astype(BF16) for a in parts), "dp")
    return dx[None], gg[None], gu[None], gd[None]


def solution(mesh):
    rows = P("blk", "dp", None)
    blocks = P("blk", None, None)
    body = local_pair if mesh.shape["dp"] == 2 else local_many
    return jax.shard_map(
        body,
        mesh=mesh,
        in_specs=(rows, rows, blocks, blocks, blocks),
        out_specs=(rows, blocks, blocks, blocks),
        check_vma=False,
    )
```
